32 devices in a mesh: dp: 16 (over z, y, x), head: 2 (over core).
Axes of the slice: x: 2, y: 2, z: 4, core: 2. Of those that a mesh axis runs over, the one named last changes fastest.
Arguments:
- tokens: bfloat16 [16, 2048, 768], P('dp'), may hold values from -6 to 6
- segment_ids: int32 [16, 2048], P('dp'), may hold values from 0 to 3, never falling along the last dimension, each value on 1 to 1024 neighbouring positions
- counts: int32 [16], P('dp'), may hold values from 512 to 2048, as said below
- w_qkv: bfloat16 [3, 768, 768], P(None, 'dp', 'head'), may hold values from -0.21875 to 0.21875
- w_out: bfloat16 [768, 768], P('head', 'dp'), may hold values from -1.25 to 1.25
- w_in: bfloat16 [2, 768, 1152], P(None, ('dp', 'head')), may hold values from -0.21875 to 0.21875
- w_down: bfloat16 [1152, 768], P(None, ('dp', 'head')), may hold values from -0.1875 to 0.1875
- ln1_gain: bfloat16 [768], P(('dp', 'head')), may hold values from 0.5 to 1.5
- ln2_gain: bfloat16 [768], P(('dp', 'head')), may hold values from 0.5 to 1.5
- cotangent: bfloat16 [16, 2048, 768], P('dp', 'head'), may hold values from -6 to 6
Outputs:
- result: bfloat16 [16, 2048, 768], P('dp', 'head')
- grad_tokens: float32 [16, 2048, 768], P('dp', 'head')
- grad_w_qkv: float32 [3, 768, 768], P(None, 'dp', 'head')
- grad_w_out: float32 [768, 768], P('head', 'dp')
- grad_w_in: float32 [2, 768, 1152], P(None, ('dp', 'head'))
- grad_w_down: float32 [1152, 768], P(None, ('dp', 'head'))
- grad_ln1: float32 [768], P(('dp', 'head'))
- grad_ln2: float32 [768], P(('dp', 'head'))
The draws below stay inside these ranges and needn't reach their ends.
Inputs may be any that keep to these rules, and one draw needn't show every extreme that they name: `segment_ids`: ids never fall along a row; each document spans 1 to 1024 positions and some document exactly 1024. `counts`: some row is full in every draw.
All inputs are finite; a program needn't handle non-finite values.
Results may differ from the reference program's by a relative error of at most 0.018.
Values may be sent and summed in bfloat16 or wider, within the bound.
No kernel may reach another device: no remote copies, remote signals or barrier semaphores. Data moves between devices by JAX's collectives and lax.ppermute only.
A program may use at most 256 MiB of HBM per device.

```python
import functools
import math
import jax
import jax.numpy as jnp
import numpy as np
from jax import lax

D = 768
HEAD_DIM = 64
FF = 1152
ROW_LEN = 2048
NSEG = 4
ROWS = 16


def draw_counts(key, part):
    first_key = jax.random.fold_in(key, 11)
    second_key = jax.random.fold_in(key, 23)
    drawn = jax.random.randint(first_key, (ROWS,), ROW_LEN // 4, ROW_LEN + 1)
    picked = jax.random.randint(second_key, (), 0, ROWS)
    return jnp.where(jnp.arange(ROWS) == picked, ROW_LEN, drawn).astype(jnp.int32)


def block_levels(rng, extent, shards, least, high):
    def one(position, blocks):
        steps = jax.random.uniform(jax.random.fold_in(jax.random.fold_in(rng, 6), position), (blocks,), jnp.float32, least / len(shards), high / len(shards))
        return jnp.repeat(jnp.exp(steps), extent[position] // blocks).reshape((-1,) + (1,) * (len(extent) - position - 1))

    level = one(*shards[0])
    for cut in shards[1:]:
        level = level * one(*cut)
    return level


def length_profile(number_of, total, reach, lean):
    weights = [(1 << 20) // math.isqrt(rank ** lean) + 1 for rank in range(2, number_of + 1)]
    surplus, holding = total - reach - (number_of - 1), [1] * (number_of - 1)
    while surplus > 0:
        movable = [i for i in range(number_of - 1) if holding[i] < reach]
        mass, remaining = sum([weights[i] for i in movable]), surplus
        for i in movable:
            extra = min(reach - holding[i], max(1, remaining * weights[i] // mass), surplus)
            holding[i] = holding[i] + extra
            surplus = surplus - extra
    return np.array([reach] + holding)


def uneven_parts(own_key, amount, total, most, lean):
    if amount == 2:
        one = jax.random.randint(own_key, (), max(1, total - most), min(most, total - 1) + 1)
        return jnp.stack([one, total - one])
    lengths = jnp.asarray(length_profile(amount, total, most, lean), jnp.int32)
    pairs = (amount - 1) // 2
    source_of, receiver = lengths[1:1 + 2 * pairs:2], lengths[2:2 + 2 * pairs:2]
    room = jnp.minimum(source_of - 1, most - receiver)
    passed = jax.random.randint(jax.random.fold_in(own_key, 1), (pairs,), 0, 1 << 20) % (room + 1)
    lengths = lengths.at[1:1 + 2 * pairs:2].set(source_of - passed).at[2:2 + 2 * pairs:2].set(receiver + passed)
    return lengths[jax.random.permutation(jax.random.fold_in(own_key, 2), amount)]


def noise(rng, extent, scale, bound, cuts=(), held_as=jnp.bfloat16):
    loudness = block_levels(rng, extent, cuts, -0.22, 0.18) if cuts else 1.0
    values = jax.random.normal(rng, extent, jnp.float32) * scale * loudness
    return jnp.minimum(jnp.maximum(values, -bound), bound).astype(held_as)


def setup_inputs(seed: int = 0) -> dict:
    key_of = jax.random.split(jax.random.key(seed), 11)
    tokens = noise(key_of[0], (ROWS, ROW_LEN, D), 1.0, 6.0, ((0, 16),))
    segment_ids = jax.vmap(lambda own: jnp.searchsorted(jnp.cumsum(uneven_parts(own, NSEG, ROW_LEN, ROW_LEN // 2, 0)), jnp.arange(ROW_LEN), side="right"))(jax.random.split(key_of[1], ROWS)).reshape((ROWS, ROW_LEN)).astype(jnp.int32)
    counts = draw_counts(jax.random.fold_in(key_of[10], 71), 0)
    w_qkv = noise(key_of[3], (3, D, D), D ** -0.5, 0.21875, ((1, 16), (2, 2)))
    w_out = noise(key_of[4], (D, D), (D // 32) ** -0.5, 1.25, ((0, 2), (1, 16)))
    w_in = noise(key_of[5], (2, D, FF), D ** -0.5, 0.21875, ((1, 32),))
    w_down = noise(key_of[6], (FF, D), FF ** -0.5, 0.1875, ((1, 32),))
    ln1_gain = jnp.clip(1.0 + 0.1 * jax.random.normal(key_of[7], (D,), jnp.float32), 0.5, 1.5).astype(jnp.bfloat16)
    ln2_gain = jnp.clip(1.0 + 0.1 * jax.random.normal(key_of[8], (D,), jnp.float32), 0.5, 1.5).astype(jnp.bfloat16)
    cotangent = noise(key_of[9], (ROWS, ROW_LEN, D), 1.0, 6.0, ((0, 16), (1, 2)))
    return dict(tokens=tokens, segment_ids=segment_ids, counts=counts, w_qkv=w_qkv, w_out=w_out, w_in=w_in, w_down=w_down, ln1_gain=ln1_gain, ln2_gain=ln2_gain, cotangent=cotangent)


layer_eps = 1e-05
rope_theta = 160000.0
neg_large = -1e+30

@jax.custom_vjp
def low(v):
    return lax.optimization_barrier(v.astype(jnp.bfloat16)).astype(jnp.float32)

@jax.custom_vjp
def low_back(v):
    return v

def low_keep(v):
    return (low(v), None)

def low_pass(kept, grad):
    return (grad,)

def back_keep(v):
    return (v, None)

def back_low(kept, grad):
    return (low(grad),)
low.defvjp(low_keep, low_pass)
low_back.defvjp(back_keep, back_low)

def layer_norm(values, gain):
    center = values - lax.optimization_barrier(jnp.mean(values, axis=-1, keepdims=True))
    spread = lax.optimization_barrier(jnp.mean(center * center, axis=-1, keepdims=True))
    return center * lax.rsqrt(spread + layer_eps) * gain

def rotary_tables(length, head_size):
    freqs = rope_theta ** (-jnp.arange(0, head_size, 2).astype(jnp.float32) / head_size)
    angles = jnp.arange(length).astype(jnp.float32)[:, None] * freqs[None, :]
    angles = jnp.concatenate([angles, angles], axis=1)
    return (jnp.cos(angles), jnp.sin(angles))

def rotate_half(values):
    middle = values.shape[-1] // 2
    return jnp.concatenate([-values[..., middle:], values[..., :middle]], axis=-1)

def block_mask(seg_query, seg_keys, count_valid, start_row):
    row_ids = start_row + jnp.arange(seg_query.shape[0], dtype=jnp.int32)
    col_ids = jnp.arange(seg_keys.shape[0], dtype=jnp.int32)
    allowed = (seg_query[:, None] == seg_keys[None, :]) & (col_ids[None, :] < count_valid)
    return allowed | (row_ids[:, None] == col_ids[None, :])

def attend_row(items):
    q_row, k_row, v_row, seg_row, count_valid = items
    row_length, heads_all, head_size = q_row.shape
    block = min(512, row_length)
    blocks = row_length // block
    score_scale = 1.0 / math.sqrt(head_size)

    def one_block(parts):
        q_blk, seg_blk, start_row = parts
        scores = low_back(score_scale * jnp.einsum('qhe,khe->hqk', q_blk, k_row, precision=lax.Precision.HIGHEST))
        scores = jnp.where(block_mask(seg_blk, seg_row, count_valid, start_row)[None], scores, neg_large)
        probs = low(jax.nn.softmax(scores, axis=-1))
        return jnp.einsum('hqk,khe->qhe', probs, v_row, precision=lax.Precision.HIGHEST)
    starts = jnp.arange(blocks, dtype=jnp.int32) * block
    outs = lax.map(jax.checkpoint(one_block), (q_row.reshape(blocks, block, heads_all, head_size), seg_row.reshape(blocks, block), starts))
    return outs.reshape(row_length, heads_all, head_size)

def forward(segment_ids, counts, tokens, w_qkv, w_out, w_in, w_down, gain_one, gain_two):
    row_count, row_length, width = tokens.shape
    head_size = HEAD_DIM
    heads_all = width // head_size
    valid = (jnp.arange(row_length, dtype=jnp.int32)[None, :] < counts[:, None]).astype(tokens.dtype)[..., None]
    normed1 = low(layer_norm(tokens, gain_one))
    qkv = low_back(jnp.einsum('rld,kde->krle', normed1, w_qkv, precision=lax.Precision.HIGHEST))
    qkv = qkv.reshape(3, row_count, row_length, heads_all, head_size)
    cosines, sines = rotary_tables(row_length, head_size)
    cos_b = cosines[None, :, None, :]
    sin_b = sines[None, :, None, :]
    query = low(qkv[0] * cos_b + rotate_half(qkv[0]) * sin_b)
    keyset = low(qkv[1] * cos_b + rotate_half(qkv[1]) * sin_b)
    valueset = low(qkv[2])
    attended = lax.map(attend_row, (query, keyset, valueset, segment_ids, counts))
    attended = low_back(low(attended.reshape(row_count, row_length, width)))
    attn = low_back(jnp.einsum('rlc,cd->rld', attended, w_out, precision=lax.Precision.HIGHEST))
    hidden = tokens + valid * attn
    normed2 = low(layer_norm(hidden, gain_two))
    up_gate = low_back(jnp.einsum('rld,kdf->krlf', normed2, w_in, precision=lax.Precision.HIGHEST))
    mixed = low(jax.nn.gelu(up_gate[0], approximate=False) * up_gate[1])
    ffn = low_back(jnp.einsum('rlf,fd->rld', mixed, w_down, precision=lax.Precision.HIGHEST))
    return hidden + valid * ffn

def reference(tokens, segment_ids, counts, w_qkv, w_out, w_in, w_down, ln1_gain, ln2_gain, cotangent):
    floats = [arr.astype(jnp.float32) for arr in (tokens, w_qkv, w_out, w_in, w_down, ln1_gain, ln2_gain)]
    result, pull = jax.vjp(functools.partial(forward, segment_ids, counts), *floats)
    grads = pull(cotangent.astype(jnp.float32))
    return (result.astype(jnp.bfloat16), grads[0], grads[1], grads[2], grads[3], grads[4], grads[5], grads[6])
```

```python
import functools
import math

import jax
import jax.numpy as jnp
from jax import lax
from jax.experimental import pallas as pl
from jax.experimental.pallas import tpu as pltpu
from jax.sharding import PartitionSpec as P

HEAD_DIM = 64
PAIR = 2 * HEAD_DIM
LAYER_EPS = 1e-05
ROPE_THETA = 160000.0
BIG = 1e30
LOG2_SCALE = math.log2(math.e) / math.sqrt(HEAD_DIM)
SCORE_SCALE = 1.0 / math.sqrt(HEAD_DIM)
ROW_BLOCK = 256
FWD_BQ, FWD_STEP = 512, 256
BWD_BQ, BWD_STEP = 256, 512
NT = (((1,), (1,)), ((), ()))
TN = (((0,), (0,)), ((), ()))
bf16 = jnp.bfloat16
f32 = jnp.float32
VMEM_LIMIT = 60 << 20


def vmem():
    return pl.BlockSpec(memory_space=pltpu.VMEM)


def smem():
    return pl.BlockSpec(memory_space=pltpu.SMEM)


def hbm():
    return pl.BlockSpec(memory_space=pl.ANY)


def params():
    return pltpu.CompilerParams(vmem_limit_bytes=VMEM_LIMIT)


def bit_groups(count):
    bits = count.bit_length() - 1
    shifts = []
    low = 0
    while low < bits:
        wide = min(2, bits - low)
        shifts.append((low, wide))
        low += wide
    return shifts[::-1]


def xor_permute(value, count, mask):
    return lax.ppermute(value, "dp", [(i, i ^ mask) for i in range(count)])


def core_swap(value):
    return lax.ppermute(value, "head", [(0, 1), (1, 0)])


def gather_parts(value, count):
    current = value[None]
    groups = bit_groups(count)
    for shift, wide in groups:
        parts = [current] + [xor_permute(current, count, j << shift) for j in range(1, 1 << wide)]
        if shift == 0:
            return parts
        current = jnp.stack(parts, axis=1).reshape((-1,) + value.shape)
    return [current]


def sum_kernel(count, *refs):
    ins, outs = refs[:count], refs[count:]
    for i, out in enumerate(outs):
        total = ins[0][i].astype(f32)
        for one in ins[1:]:
            total = total + one[i].astype(f32)
        out[...] = total.astype(out.dtype)


def sum_parts(arrays):
    m, rows, cols = arrays[0].shape
    return pl.pallas_call(
        functools.partial(sum_kernel, len(arrays)),
        out_shape=tuple(
            jax.ShapeDtypeStruct((rows, cols), f32 if i == 0 else bf16) for i in range(m)
        ),
        in_specs=[vmem()] * len(arrays),
        out_specs=(vmem(),) * m,
        compiler_params=params(),
        name="sum_parts",
    )(*arrays)


def reduce_parts(parts, count):
    high = len(parts[0])
    near = [parts[0]] + [xor_permute(parts[j], count, j) for j in range(1, len(parts))]
    pieces = sum_parts(near)
    shift = len(parts).bit_length() - 1
    total = pieces[0]
    for h in range(1, high):
        total = total + xor_permute(pieces[h], count, h << shift).astype(f32)
    return total


def placed_copies(parts, target, sems, me, rows):
    if len(parts) == 1:
        return [pltpu.make_async_copy(parts[0], target, sems.at[0])]
    copies = []
    wide = len(parts)
    for h in range(parts[0].shape[0]):
        for j in range(wide):
            own = jnp.bitwise_xor(me, h * wide + j)
            copies.append(
                pltpu.make_async_copy(
                    parts[j].at[h],
                    target.at[pl.ds(pl.multiple_of(own * rows, 16), rows)],
                    sems.at[h * wide + j],
                )
            )
    return copies


def document_starts(seg, length):
    starts = [jnp.int32(0)]
    for d in (1, 2, 3):
        starts.append(jnp.sum((seg < d).astype(jnp.int32)))
    return starts + [jnp.int32(length)]


def key_range(starts, live, first, size, length):
    last = jnp.minimum(first + size, live) - 1
    low = jnp.int32(0)
    high = jnp.int32(length)
    for d in (1, 2, 3):
        low = jnp.where(starts[d] <= first, starts[d], low)
    for d in (3, 2, 1):
        high = jnp.where(starts[d] > last, starts[d], high)
    high = jnp.minimum(high, live)
    return low, jnp.where(first < live, high, low)


def each_query_block(seg, live, length, size, step, work, empty):
    starts = document_starts(seg, length)

    @pl.loop(0, length // size)
    def _(i):
        first = pl.multiple_of(i * size, size)
        low, high = key_range(starts, live, first, size, length)
        base = low // 16 * 16
        steps = (high - base + step - 1) // step
        base = pl.multiple_of(jnp.maximum(jnp.minimum(base, length - steps * step), 0), 16)
        rows = pl.ds(first, size)
        for w in range(1, length // step + 1):

            @pl.when(steps == w)
            def _():
                work(rows, pl.ds(base, w * step))

        @pl.when(steps <= 0)
        def _():
            empty(rows)


def norm_stats(values):
    center = values - jnp.mean(values, axis=-1, keepdims=True)
    spread = jnp.mean(center * center, axis=-1, keepdims=True)
    inv = lax.rsqrt(spread + LAYER_EPS)
    return center * inv, inv


def norm_back(grad, normed, inv):
    return inv * (
        grad
        - jnp.mean(grad, axis=-1, keepdims=True)
        - normed * jnp.mean(grad * normed, axis=-1, keepdims=True)
    )


def half_swap(values, in_first):
    return jnp.where(in_first, pltpu.roll(values, PAIR - HEAD_DIM // 2, 1), pltpu.roll(values, HEAD_DIM // 2, 1))


def split3(values):
    a = values.astype(bf16)
    left = values - a.astype(f32)
    b = left.astype(bf16)
    return a, b, (left - b.astype(f32)).astype(bf16)


def forward_kernel(first, part_count, *refs):
    scal, seg, src = refs[:3]
    parts = refs[3 : 3 + part_count]
    cs, sn, fq, fk = refs[3 + part_count : 7 + part_count]
    outs = refs[7 + part_count :]
    if first:
        a1, gains = outs[:2]
        outs = outs[2:]
    w, q_out, k_out, v_out, o_out, lse_out, qx, kx, vx, sems = outs
    length, width = src.shape
    live, me = scal[0], scal[1]
    rows_each = width // max(16, 1) if part_count > 1 else width
    if part_count > 1:
        rows_each = parts[0].shape[1]
    copies = placed_copies(parts, w, sems, me, rows_each)
    for copy in copies:
        copy.start()
    for copy in copies:
        copy.wait()
    if first:
        turned = jnp.transpose(w[:, 4 * PAIR :].astype(f32))
        gains[0:8, :] = turned[0:8]
        gains[8:16, :] = turned[HEAD_DIM : HEAD_DIM + 8]
    lane = lax.broadcasted_iota(jnp.int32, (ROW_BLOCK, PAIR), 1)
    low_head = lane < HEAD_DIM
    in_first = (lane & (HEAD_DIM - 1)) < HEAD_DIM // 2
    zero = jnp.zeros((ROW_BLOCK, PAIR), bf16)

    @pl.loop(0, length // ROW_BLOCK)
    def _(b):
        rows = pl.ds(pl.multiple_of(b * ROW_BLOCK, ROW_BLOCK), ROW_BLOCK)
        if first:
            normed, _ = norm_stats(src[rows, :].astype(f32))
            a = (normed * gains[0:1, :]).astype(bf16)
            a1[rows, :] = a
        else:
            a = src[rows, :]
        qkv = jnp.dot(a, w[:, : 3 * PAIR], preferred_element_type=f32)
        cos, sin = cs[rows, :], sn[rows, :]
        u = qkv[:, :PAIR]
        q = (u * cos + half_swap(u, in_first) * sin).astype(bf16)
        u = qkv[:, PAIR : 2 * PAIR]
        k = (u * cos + half_swap(u, in_first) * sin).astype(bf16)
        v = qkv[:, 2 * PAIR :].astype(bf16)
        q_out[rows, :] = q
        k_out[rows, :] = k
        v_out[rows, :] = v
        scaled = q.astype(f32) * LOG2_SCALE
        high = scaled.astype(bf16)
        rest = (scaled - high.astype(f32)).astype(bf16)
        for h in (0, 1):
            mine = low_head if h == 0 else ~low_head
            qx[h, rows, :PAIR] = jnp.where(mine, high, zero)
            qx[h, rows, PAIR:] = jnp.where(mine, rest, fq[rows, :])
            kx[h, rows, :PAIR] = k
            kx[h, rows, PAIR:] = jnp.where(mine, k, fk[rows, :])
        vx[rows, :PAIR] = v
        vx[rows, PAIR:] = jnp.ones((ROW_BLOCK, PAIR), bf16)

    lane_q = lax.broadcasted_iota(jnp.int32, (FWD_BQ, PAIR), 1) < HEAD_DIM

    def work(rows, keys):
        values = vx[keys, :]
        scores = [
            lax.dot_general(qx[h, rows, :], kx[h, keys, :], NT, preferred_element_type=f32) for h in (0, 1)
        ]
        tops, sums = [], []
        for h in (0, 1):
            top = jnp.max(scores[h], axis=1, keepdims=True)
            probs = jnp.exp2(scores[h] - top).astype(bf16)
            tops.append(top)
            sums.append(jnp.dot(probs, values, preferred_element_type=f32))
        total = jnp.where(lane_q, sums[0][:, PAIR:], sums[1][:, PAIR:])
        out = jnp.where(lane_q, sums[0][:, :PAIR], sums[1][:, :PAIR])
        o_out[rows, :] = (out / total).astype(bf16)
        lse_out[rows, :] = jnp.maximum(jnp.where(lane_q, tops[0], tops[1]) + jnp.log2(total), -1e20)

    def empty(rows):
        o_out[rows, :] = jnp.zeros((FWD_BQ, PAIR), bf16)
        lse_out[rows, :] = jnp.zeros((FWD_BQ, PAIR), f32)

    each_query_block(seg[...], live, length, FWD_BQ, FWD_STEP, work, empty)


def forward_pair(first, scal, seg, src, parts, tables):
    length, width = src.shape
    cols = parts[0].shape[-1]
    shape = jax.ShapeDtypeStruct
    outs = [shape((width, cols), bf16)] + [shape((length, PAIR), bf16)] * 4 + [shape((length, PAIR), f32)]
    if first:
        outs = [shape((length, width), bf16), shape((16, width), f32)] + outs
    return pl.pallas_call(
        functools.partial(forward_kernel, first, len(parts)),
        out_shape=tuple(outs),
        in_specs=[smem(), vmem(), vmem()] + [hbm()] * len(parts) + [vmem()] * 4,
        out_specs=(vmem(),) * len(outs),
        scratch_shapes=[
            pltpu.VMEM((2, length, 2 * PAIR), bf16),
            pltpu.VMEM((2, length, 2 * PAIR), bf16),
            pltpu.VMEM((length, 2 * PAIR), bf16),
            pltpu.SemaphoreType.DMA((16,)),
        ],
        compiler_params=params(),
        name="attention_forward_first" if first else "attention_forward",
    )(scal, seg, src, *parts, *tables)


def backward_kernel(part_count, *refs):
    scal, seg, a1, near, far, w, q_in, k_in, v_in, o_in, lse, cs, sn, fq, fk, dqkv = refs[:16]
    parts = refs[16 : 16 + part_count]
    (grad_rows, qx, kx, dx, vx, qm, km, dq, dk, dv, grads, sems) = refs[16 + part_count :]
    length, width = a1.shape
    half = length // 2
    live, me, core = scal[0], scal[1], scal[2]
    loads = [
        pltpu.make_async_copy(near, grad_rows.at[pl.ds(pl.multiple_of(core * half, half), half)], sems.at[0]),
        pltpu.make_async_copy(far, grad_rows.at[pl.ds(pl.multiple_of((1 - core) * half, half), half)], sems.at[1]),
    ]
    for copy in loads:
        copy.start()
    for copy in loads:
        copy.wait()
    lane = lax.broadcasted_iota(jnp.int32, (ROW_BLOCK, PAIR), 1)
    in_head = lane & (HEAD_DIM - 1)
    low_head = lane < HEAD_DIM
    in_first = in_head < HEAD_DIM // 2
    zero = jnp.zeros((ROW_BLOCK, PAIR), bf16)
    minus = jnp.full((ROW_BLOCK, PAIR), -1, bf16)

    @pl.loop(0, length // ROW_BLOCK)
    def _(b):
        rows = pl.ds(pl.multiple_of(b * ROW_BLOCK, ROW_BLOCK), ROW_BLOCK)
        grad = jnp.dot(grad_rows[rows, :], w[:, 3 * PAIR : 4 * PAIR], preferred_element_type=f32).astype(bf16)
        q, k = q_in[rows, :], k_in[rows, :]
        scaled = q.astype(f32) * LOG2_SCALE
        high = scaled.astype(bf16)
        rest = (scaled - high.astype(f32)).astype(bf16)
        la, lb, lc = split3(lse[rows, :])
        fq_b = jnp.where(
            in_head == 5, la, jnp.where(in_head == 6, lb, jnp.where(in_head == 7, lc, fq[rows, :]))
        )
        fq_b = pltpu.roll(fq_b.astype(f32), HEAD_DIM, 1).astype(bf16)
        fk_b = jnp.where((in_head >= 5) & (in_head < 8), minus, fk[rows, :])
        inner = grad.astype(f32) * o_in[rows, :].astype(f32)
        for h in (0, 1):
            mine = low_head if h == 0 else ~low_head
            qx[h, rows, :PAIR] = jnp.where(mine, high, zero)
            qx[h, rows, PAIR:] = jnp.where(mine, rest, fq_b)
            kx[h, rows, :PAIR] = k
            kx[h, rows, PAIR:] = jnp.where(mine, k, fk_b)
            qm[h, rows, :] = jnp.where(mine, q, zero)
            km[h, rows, :] = jnp.where(mine, k, zero)
            dx[h, rows, :PAIR] = jnp.where(mine, grad, zero)
            delta = jnp.sum(jnp.where(mine, inner, 0.0), axis=1, keepdims=True)
            da, db, dc = split3(jnp.broadcast_to(delta, (ROW_BLOCK, PAIR)))
            dx[h, rows, PAIR:] = jnp.where(
                lane == 0, da, jnp.where(lane == 1, db, jnp.where(lane == 2, dc, zero))
            )
        vx[rows, :PAIR] = v_in[rows, :]
        vx[rows, PAIR:] = jnp.where(lane < 3, minus, zero)
        dk[rows, :] = jnp.zeros((ROW_BLOCK, PAIR), f32)
        dv[rows, :] = jnp.zeros((ROW_BLOCK, PAIR), f32)

    def work(rows, keys):
        grad_q = grad_k = grad_v = None
        for h in (0, 1):
            scores = lax.dot_general(qx[h, rows, :], kx[h, keys, :], NT, preferred_element_type=f32)
            pulled = lax.dot_general(dx[h, rows, :], vx[keys, :], NT, preferred_element_type=f32)
            probs = jnp.exp2(scores)
            grad_s = (probs * pulled).astype(bf16)
            one_q = jnp.dot(grad_s, km[h, keys, :], preferred_element_type=f32)
            one_v = lax.dot_general(probs.astype(bf16), dx[h, rows, :PAIR], TN, preferred_element_type=f32)
            one_k = lax.dot_general(grad_s, qm[h, rows, :], TN, preferred_element_type=f32)
            grad_q = one_q if h == 0 else grad_q + one_q
            grad_v = one_v if h == 0 else grad_v + one_v
            grad_k = one_k if h == 0 else grad_k + one_k
        dq[rows, :] = grad_q
        dv[keys, :] = dv[keys, :] + grad_v
        dk[keys, :] = dk[keys, :] + grad_k

    def empty(rows):
        dq[rows, :] = jnp.zeros((BWD_BQ, PAIR), f32)

    each_query_block(seg[...], live, length, BWD_BQ, BWD_STEP, work, empty)

    @pl.loop(0, length // ROW_BLOCK)
    def _(b):
        rows = pl.ds(pl.multiple_of(b * ROW_BLOCK, ROW_BLOCK), ROW_BLOCK)
        cos, sin = cs[rows, :], sn[rows, :]
        u = dq[rows, :] * SCORE_SCALE
        dqkv[rows, :PAIR] = (u * cos - half_swap(u, in_first) * sin).astype(bf16)
        u = dk[rows, :] * SCORE_SCALE
        dqkv[rows, PAIR : 2 * PAIR] = (u * cos - half_swap(u, in_first) * sin).astype(bf16)
        dqkv[rows, 2 * PAIR :] = dv[rows, :].astype(bf16)

    for m in range(width // ROW_BLOCK):
        part = slice(m * ROW_BLOCK, (m + 1) * ROW_BLOCK)
        grads[part, : 3 * PAIR] = lax.dot_general(
            a1[:, part], dqkv[...], TN, preferred_element_type=f32
        ).astype(bf16)
        grads[part, 3 * PAIR :] = lax.dot_general(
            grad_rows[:, part], o_in[...], TN, preferred_element_type=f32
        ).astype(bf16)
    if part_count == 1:
        stores = [pltpu.make_async_copy(grads, parts[0], sems.at[0])]
    else:
        rows_each = parts[0].shape[1]
        stores = []
        for h in range(parts[0].shape[0]):
            for j in range(part_count):
                own = jnp.bitwise_xor(me, h * part_count + j)
                stores.append(
                    pltpu.make_async_copy(
                        grads.at[pl.ds(pl.multiple_of(own * rows_each, 16), rows_each)],
                        parts[j].at[h],
                        sems.at[h * part_count + j],
                    )
                )
    for copy in stores:
        copy.start()
    for copy in stores:
        copy.wait()


def backward_pair(scal, seg, a1, near, far, w, saved, tables, part_shapes):
    length, width = a1.shape
    shape = jax.ShapeDtypeStruct
    outs = [shape((length, 3 * PAIR), bf16)] + [shape(s, bf16) for s in part_shapes]
    return pl.pallas_call(
        functools.partial(backward_kernel, len(part_shapes)),
        out_shape=tuple(outs),
        in_specs=[smem(), vmem(), vmem(), hbm(), hbm()] + [vmem()] * 10,
        out_specs=(vmem(),) + (hbm(),) * len(part_shapes),
        scratch_shapes=[
            pltpu.VMEM((length, width), bf16),
            pltpu.VMEM((2, length, 2 * PAIR), bf16),
            pltpu.VMEM((2, length, 2 * PAIR), bf16),
            pltpu.VMEM((2, length, 2 * PAIR), bf16),
            pltpu.VMEM((length, 2 * PAIR), bf16),
            pltpu.VMEM((2, length, PAIR), bf16),
            pltpu.VMEM((2, length, PAIR), bf16),
            pltpu.VMEM((length, PAIR), f32),
            pltpu.VMEM((length, PAIR), f32),
            pltpu.VMEM((length, PAIR), f32),
            pltpu.VMEM((width, 4 * PAIR), bf16),
            pltpu.SemaphoreType.DMA((16,)),
        ],
        compiler_params=params(),
        name="attention_backward",
    )(scal, seg, a1, near, far, w, *saved, *tables)


def project_kernel(count, low, high, scal, *refs):
    rows, weights, out = refs[:count], refs[count : 2 * count], refs[2 * count]
    total = None
    for one, w in zip(rows, weights):
        term = lax.dot_general(one[...], w[:, low:high], NT, preferred_element_type=f32)
        total = term if total is None else total + term
    out[...] = total.astype(out.dtype)


def project_far_half(scal, rows, weights, low, high):
    length, cols = rows[0].shape
    width = weights[0].shape[0]
    blocks = length // 2 // ROW_BLOCK
    return pl.pallas_call(
        functools.partial(project_kernel, len(rows), low, high),
        out_shape=jax.ShapeDtypeStruct((length // 2, width), bf16),
        grid_spec=pltpu.PrefetchScalarGridSpec(
            num_scalar_prefetch=1,
            grid=(blocks,),
            in_specs=[pl.BlockSpec((ROW_BLOCK, cols), lambda b, s: (b + (1 - s[2]) * blocks, 0))] * len(rows)
            + [pl.BlockSpec(w.shape, lambda b, s: (0, 0)) for w in weights],
            out_specs=pl.BlockSpec((ROW_BLOCK, width), lambda b, s: (b, 0)),
        ),
        compiler_params=params(),
        name="project_far_half",
    )(scal, *rows, *weights)


def final_kernel(count, scal, *refs):
    rows, weights = refs[:count], refs[count : 2 * count]
    tokens, far, grad_hidden, gains, out = refs[2 * count :]
    total = far[...].astype(f32)
    for one, w in zip(rows, weights):
        total = total + lax.dot_general(one[...], w[:, : 3 * PAIR], NT, preferred_element_type=f32)
    normed, inv = norm_stats(tokens[...].astype(f32))
    out[...] = grad_hidden[...] + norm_back(total * gains[0:1, :], normed, inv)


def final_rows(scal, rows, weights, tokens, far, grad_hidden, gains):
    length, cols = rows[0].shape
    width = tokens.shape[1]
    blocks = length // 2 // ROW_BLOCK
    whole = lambda a: pl.BlockSpec(a.shape, lambda b, s: (0, 0))
    near = lambda a: pl.BlockSpec((ROW_BLOCK, a.shape[1]), lambda b, s: (b + s[2] * blocks, 0))
    plain = pl.BlockSpec((ROW_BLOCK, width), lambda b, s: (b, 0))
    return pl.pallas_call(
        functools.partial(final_kernel, len(rows)),
        out_shape=jax.ShapeDtypeStruct((length // 2, width), f32),
        grid_spec=pltpu.PrefetchScalarGridSpec(
            num_scalar_prefetch=1,
            grid=(blocks,),
            in_specs=[near(r) for r in rows]
            + [whole(w) for w in weights]
            + [near(tokens), plain, plain, whole(gains)],
            out_specs=plain,
        ),
        compiler_params=params(),
        name="final_rows",
    )(scal, *rows, *weights, tokens, far, grad_hidden, gains)


def ffn_kernel(count, part_count, down_cols, scal, *refs):
    outs_of, weights = refs[:count], refs[count : 2 * count]
    tokens, far, cot, gains = refs[2 * count : 2 * count + 4]
    rest = refs[2 * count + 4 :]
    if part_count > 1:
        sources, rest = rest[: 2 * part_count], rest[2 * part_count :]
    else:
        sources, rest = rest[:2], rest[2:]
    result, dattn, grad_hidden, keep, send, w_in, w_down, z_all, pair_all, a2_all, dff_all, sems = rest
    width, ff = w_down.shape
    live, me, core = scal[0], scal[1], scal[2]
    step = pl.program_id(0)
    block = result.shape[0]

    @pl.when(step == 0)
    def _():
        copies = []
        if part_count == 1:
            copies.append(pltpu.make_async_copy(sources[0], w_in, sems.at[0]))
            copies.append(pltpu.make_async_copy(sources[1], w_down, sems.at[1]))
        else:
            offset = ff - down_cols
            rows_each = sources[0].shape[1]
            near_at = pl.multiple_of(core * offset, PAIR)
            far_from = pl.multiple_of(ff + (1 - core) * (down_cols - offset), PAIR)
            far_at = pl.multiple_of((1 - core) * down_cols, PAIR)
            for h in range(sources[0].shape[0]):
                for j in range(part_count):
                    own = jnp.bitwise_xor(me, h * part_count + j)
                    at = pl.ds(pl.multiple_of(own * rows_each, 16), rows_each)
                    number = 4 * (h * part_count + j)
                    mine, other = sources[j].at[h], sources[part_count + j].at[h]
                    copies += [
                        pltpu.make_async_copy(mine.at[:, :ff], w_in.at[core, at], sems.at[number]),
                        pltpu.make_async_copy(other.at[:, :ff], w_in.at[1 - core, at], sems.at[number + 1]),
                        pltpu.make_async_copy(
                            mine.at[:, ff:], w_down.at[at, pl.ds(near_at, down_cols)], sems.at[number + 2]
                        ),
                        pltpu.make_async_copy(
                            other.at[:, pl.ds(far_from, offset)],
                            w_down.at[at, pl.ds(far_at, offset)],
                            sems.at[number + 3],
                        ),
                    ]
        for copy in copies:
            copy.start()
        for copy in copies:
            copy.wait()

    here = core * (block * pl.num_programs(0)) + step * block
    position = here + lax.broadcasted_iota(jnp.int32, (block, 1), 0)
    valid = (position < live).astype(f32)
    attn = far[...].astype(f32)
    for one, w in zip(outs_of, weights):
        attn = attn + lax.dot_general(one[...], w[:, 3 * PAIR : 4 * PAIR], NT, preferred_element_type=f32)
    hidden = tokens[...].astype(f32) + valid * attn
    normed, inv = norm_stats(hidden)
    gain = gains[8:9, :]
    a2 = (normed * gain).astype(bf16)
    up = jnp.dot(a2, w_in[0], preferred_element_type=f32)
    gate = jnp.dot(a2, w_in[1], preferred_element_type=f32)
    below = 0.5 * (1.0 + lax.erf(up * math.sqrt(0.5)))
    act = up * below
    slope = below + up * jnp.exp(up * up * -0.5) * (1.0 / math.sqrt(2.0 * math.pi))
    z = (act * gate).astype(bf16)
    result[...] = (
        hidden + valid * lax.dot_general(z, w_down[...], NT, preferred_element_type=f32)
    ).astype(bf16)
    dy = cot[...].astype(f32)
    dff = (valid * dy).astype(bf16)
    dz = jnp.dot(dff, w_down[...], preferred_element_type=f32)
    du = (dz * gate * slope).astype(bf16)
    dg = (dz * act).astype(bf16)
    da2 = lax.dot_general(du, w_in[0], NT, preferred_element_type=f32) + lax.dot_general(
        dg, w_in[1], NT, preferred_element_type=f32
    )
    grad = dy + norm_back(da2 * gain, normed, inv)
    grad_hidden[...] = grad
    dattn[...] = (valid * grad).astype(bf16)
    rows = pl.ds(pl.multiple_of(step * block, block), block)
    z_all[rows, :] = z
    pair_all[0, rows, :] = du
    pair_all[1, rows, :] = dg
    a2_all[rows, :] = a2
    dff_all[rows, :] = dff

    @pl.when(step == pl.num_programs(0) - 1)
    def _():
        for m in range(width // ROW_BLOCK):
            part = slice(m * ROW_BLOCK, (m + 1) * ROW_BLOCK)
            left = a2_all[:, part]
            down = dff_all[:, part]
            if part_count == 1:
                for i in (0, 1):
                    keep[i, part, :] = lax.dot_general(
                        left, pair_all[i], TN, preferred_element_type=f32
                    ).astype(bf16)
                send[part, :] = lax.dot_general(down, z_all[...], TN, preferred_element_type=f32).astype(bf16)
            else:
                offset = ff - down_cols
                for out, who in ((send, 1 - core), (keep, core)):
                    out[part, :ff] = lax.dot_general(
                        left, pair_all[who], TN, preferred_element_type=f32
                    ).astype(bf16)
                    out[part, ff:] = lax.dot_general(
                        down,
                        z_all[:, pl.ds(pl.multiple_of(who * offset, PAIR), down_cols)],
                        TN,
                        preferred_element_type=f32,
                    ).astype(bf16)


def feed_forward(scal, outs_of, weights, tokens, far, cot, gains, sources, width, ff, down_cols):
    length = tokens.shape[0]
    half = length // 2
    blocks = half // ROW_BLOCK
    part_count = len(sources) // 2
    shape = jax.ShapeDtypeStruct
    whole = lambda a: pl.BlockSpec(a.shape, lambda b, s: (0,) * len(a.shape))
    near = lambda a: pl.BlockSpec((ROW_BLOCK, a.shape[1]), lambda b, s: (b + s[2] * blocks, 0))
    plain = pl.BlockSpec((ROW_BLOCK, width), lambda b, s: (b, 0))
    if part_count == 1:
        grads = (shape((2, width, ff), bf16), shape((width, ff), bf16))
    else:
        grads = (shape((width, ff + down_cols), bf16),) * 2
    return pl.pallas_call(
        functools.partial(ffn_kernel, len(outs_of), part_count, down_cols),
        out_shape=(shape((half, width), bf16), shape((half, width), bf16), shape((half, width), f32)) + grads,
        grid_spec=pltpu.PrefetchScalarGridSpec(
            num_scalar_prefetch=1,
            grid=(blocks,),
            in_specs=[near(o) for o in outs_of]
            + [whole(w) for w in weights]
            + [near(tokens), plain, plain, whole(gains)]
            + [hbm()] * len(sources),
            out_specs=(plain, plain, plain) + tuple(whole(g) for g in grads),
            scratch_shapes=[
                pltpu.VMEM((2, width, ff), bf16),
                pltpu.VMEM((width, ff), bf16),
                pltpu.VMEM((half, ff), bf16),
                pltpu.VMEM((2, half, ff), bf16),
                pltpu.VMEM((half, width), bf16),
                pltpu.VMEM((half, width), bf16),
                pltpu.SemaphoreType.DMA((64,)),
            ],
        ),
        compiler_params=params(),
        name="feed_forward",
    )(scal, *outs_of, *weights, tokens, far, cot, gains, *sources)


def pack_kernel(wide, scal, keep, got, *outs):
    me = scal[1]
    for j in range(wide):
        for h in range(outs[0].shape[0]):
            own = jnp.bitwise_xor(me, h * wide + j)
            outs[j][h] = (keep[own].astype(f32) + got[own].astype(f32)).astype(bf16)


def pack_parts(scal, keep, got, count):
    width, cols = keep.shape
    rows = width // count
    wide = 1 << bit_groups(count)[-1][1]
    shape = jax.ShapeDtypeStruct((count // wide, rows, cols), bf16)
    return pl.pallas_call(
        functools.partial(pack_kernel, wide),
        out_shape=(shape,) * wide,
        in_specs=[smem(), vmem(), vmem()],
        out_specs=(vmem(),) * wide,
        compiler_params=params(),
        name="pack_parts",
    )(scal, keep.reshape(count, rows, cols), got.reshape(count, rows, cols))


def rotary_tables(length):
    freqs = ROPE_THETA ** (-jnp.arange(0, HEAD_DIM, 2).astype(f32) / HEAD_DIM)
    angles = jnp.arange(length).astype(f32)[:, None] * freqs[None, :]
    cos, sin = jnp.cos(angles), jnp.sin(angles)
    return jnp.tile(cos, (1, 4)), jnp.tile(jnp.concatenate([-sin, sin], axis=1), (1, 2))


def mask_features(seg, live):
    column = jnp.arange(HEAD_DIM)[None, :]
    same = seg[:, None] == column
    position = jnp.arange(seg.shape[0])[:, None]
    query = jnp.where(column < 4, same.astype(f32), (column == 4).astype(f32))
    key = jnp.where(
        column < 4, jnp.where(same, 0.0, -BIG), jnp.where((column == 4) & (position >= live), -BIG, 0.0)
    )
    return jnp.tile(query, (1, 2)).astype(bf16), jnp.tile(key, (1, 2)).astype(bf16)


def local(tokens, segment_ids, counts, w_qkv, w_out, w_in, w_down, ln1_gain, ln2_gain, cotangent):
    count = lax.axis_size("dp")
    dp, core = lax.axis_index("dp"), lax.axis_index("head")
    length, width = tokens.shape[1:]
    ff = w_in.shape[2]
    rows_each = width // count
    fast = rows_each % 16 == 0 and count & (count - 1) == 0 and count >= 16
    pairs = w_qkv.shape[2] // PAIR
    first_core = core == 0
    pick = lambda a, b: jnp.where(first_core, a, b)
    join = lambda mine, other: jnp.concatenate([pick(mine, other), pick(other, mine)], axis=0)
    row, cot = tokens[0], cotangent[0]
    seg = segment_ids[0]
    live = counts[0]
    scal = jnp.stack([live, dp, core]).astype(jnp.int32)
    seg_tile = seg.reshape(-1, 128)

    out_turned = w_out.T
    both = jnp.stack([ln1_gain, ln2_gain], axis=1)
    both = join(both, core_swap(both))
    gain_cols = jnp.repeat(both, HEAD_DIM, axis=1)
    payloads = []
    for i in range(pairs):
        cols = slice(i * PAIR, (i + 1) * PAIR)
        payload = [w_qkv[0][:, cols], w_qkv[1][:, cols], w_qkv[2][:, cols], out_turned[:, cols]]
        payloads.append(jnp.concatenate(payload + ([gain_cols] if i == 0 else []), axis=1))
    if fast:
        pair_parts = [gather_parts(p, count) for p in payloads]
    else:
        pair_parts = [[lax.all_gather(p, "dp", axis=0, tiled=True)] for p in payloads]

    down_turned = w_down.T
    down_cols = -(-(ff // 2) // 128) * 128
    offset = ff - down_cols
    if fast:
        zero_one = jnp.concatenate([w_in[0], down_turned[:, :down_cols]], axis=1)
        one_two = jnp.concatenate([w_in[1], down_turned[:, offset:]], axis=1)
        got = core_swap(pick(one_two, zero_one))
        ffn_parts = gather_parts(join(pick(zero_one, one_two), got), count)
        sources = ffn_parts + [core_swap(p) for p in ffn_parts]
    else:
        sources = [
            lax.all_gather(w_in, ("dp", "head"), axis=1, tiled=True),
            lax.all_gather(down_turned, ("dp", "head"), axis=0, tiled=True),
        ]

    tables = rotary_tables(length) + mask_features(seg, live)
    a1, gains, *kept = forward_pair(True, scal, seg_tile, row, pair_parts[0], tables)
    saved = [kept]
    for i in range(1, pairs):
        saved.append(forward_pair(False, scal, seg_tile, a1, pair_parts[i], tables))
    weights = [s[0] for s in saved]
    outs_of = [s[4] for s in saved]

    far = core_swap(project_far_half(scal, outs_of, weights, 3 * PAIR, 4 * PAIR))
    result, near_grad, grad_hidden, keep, send = feed_forward(
        scal, outs_of, weights, row, far, cot, gains, sources, width, ff, down_cols
    )
    far_grad = core_swap(near_grad)

    if fast:
        parts = pack_parts(scal, keep, core_swap(send), count)
        done = reduce_parts(parts, count)
        rows_here = w_in.shape[1]
        low, high = done[:rows_here], done[rows_here:]
        mine = pick(low, high)
        other = core_swap(pick(high, low))
        grad_w_in = jnp.stack(
            [pick(mine[:, :ff], other[:, :ff]), pick(other[:, :ff], mine[:, :ff])]
        )
        grad_down = jnp.concatenate(
            [pick(mine[:, ff:], other[:, ff:]), pick(other[:, ff:], mine[:, ff:])[:, down_cols - offset :]],
            axis=1,
        ).T
    else:
        grad_w_in = lax.psum_scatter(keep.astype(f32), ("dp", "head"), scatter_dimension=1, tiled=True)
        grad_down = lax.psum_scatter(
            send.astype(f32), ("dp", "head"), scatter_dimension=0, tiled=True
        ).T
    grad_two = jnp.sum(grad_w_in * w_in.astype(f32), axis=(0, 2)) / ln2_gain.astype(f32)

    if fast:
        wide = len(pair_parts[0])
        part_shapes = [(count // wide, rows_each, 4 * PAIR)] * wide
    else:
        part_shapes = [(width, 4 * PAIR)]
    dqkv, shards = [], []
    for i in range(pairs):
        _, q, k, v, o, lse = saved[i]
        one, *parts = backward_pair(
            scal, seg_tile, a1, near_grad, far_grad, weights[i], (q, k, v, o, lse), tables, part_shapes
        )
        dqkv.append(one)
        if fast:
            shards.append(reduce_parts(parts, count))
        else:
            shards.append(lax.psum_scatter(parts[0].astype(f32), "dp", scatter_dimension=0, tiled=True))

    far_da = core_swap(project_far_half(scal, dqkv, weights, 0, 3 * PAIR))
    grad_tokens = final_rows(scal, dqkv, weights, row, far_da, grad_hidden, gains)

    grad_qkv = jnp.stack(
        [jnp.concatenate([s[:, c * PAIR : (c + 1) * PAIR] for s in shards], axis=1) for c in range(3)]
    )
    grad_out = jnp.concatenate([s[:, 3 * PAIR :] for s in shards], axis=1).T
    partial = jnp.sum(grad_qkv * w_qkv.astype(f32), axis=(0, 2))
    rows_here = ln1_gain.shape[0]
    low, high = partial[:rows_here], partial[rows_here:]
    grad_one = (pick(low, high) + core_swap(pick(high, low))) / ln1_gain.astype(f32)
    return (
        result[None],
        grad_tokens[None],
        grad_qkv,
        grad_out,
        grad_w_in,
        grad_down,
        grad_one,
        grad_two,
    )


def solution(mesh):
    placed = (
        P("dp", None, None),
        P("dp", None),
        P("dp"),
        P(None, "dp", "head"),
        P("head", "dp"),
        P(None, ("dp", "head"), None),
        P(None, ("dp", "head")),
        P(("dp", "head")),
        P(("dp", "head")),
        P("dp", "head", None),
    )
    return jax.shard_map(
        local,
        mesh=mesh,
        in_specs=placed,
        out_specs=(
            P("dp", "head", None),
            P("dp", "head", None),
            P(None, "dp", "head"),
            P("head", "dp"),
            P(None, ("dp", "head"), None),
            P(None, ("dp", "head")),
            P(("dp", "head")),
            P(("dp", "head")),
        ),
        check_vma=False,
    )
```

```python
import functools
import math

import jax
import jax.numpy as jnp
import numpy as np
from jax import lax
from jax.experimental import pallas as pl
from jax.experimental.pallas import tpu as pltpu
from jax.sharding import PartitionSpec as P

HEAD_DIM = 64
PAIR = 2 * HEAD_DIM
LAYER_EPS = 1e-05
ROPE_THETA = 160000.0
BIG = 1e30
LOG2_SCALE = math.log2(math.e) / math.sqrt(HEAD_DIM)
SCORE_SCALE = 1.0 / math.sqrt(HEAD_DIM)
ROW_BLOCK = 256
FWD_MIB, BWD_MIB, FFN_MIB = 32, 40, 44
FWD_BQ, FWD_STEP = 512, 256
BWD_BQ, BWD_STEP = 256, 512
NT = (((1,), (1,)), ((), ()))
TN = (((0,), (0,)), ((), ()))
bf16 = jnp.bfloat16
f32 = jnp.float32


def vmem():
    return pl.BlockSpec(memory_space=pltpu.VMEM)


def smem():
    return pl.BlockSpec(memory_space=pltpu.SMEM)


def hbm():
    return pl.BlockSpec(memory_space=pltpu.HBM)


def anywhere():
    return pl.BlockSpec(memory_space=pl.ANY)


def params(mib=16):
    return pltpu.CompilerParams(vmem_limit_bytes=mib << 20)


def lasts(micros):
    return pl.CostEstimate(flops=int(micros * 1e8), bytes_accessed=0, transcendentals=0)


def passing(kernel, inputs, deps):
    def run(*refs):
        kernel(*refs[:inputs], *refs[inputs + deps :])

    return run


def bit_groups(count):
    bits = count.bit_length() - 1
    shifts = []
    low = 0
    while low < bits:
        wide = min(2, bits - low)
        shifts.append((low, wide))
        low += wide
    return shifts[::-1]


def xor_permute(value, count, mask):
    return lax.ppermute(value, "dp", [(i, i ^ mask) for i in range(count)])


def core_swap(value):
    return lax.ppermute(value, "head", [(0, 1), (1, 0)])


def stack_kernel(*refs):
    ins, out = refs[:-1], refs[-1]
    wide = len(ins)
    for j, one in enumerate(ins):
        for h in range(one.shape[0]):
            out[h * wide + j] = one[h]


def stack_parts(parts, deps=()):
    m, rows, cols = parts[0].shape
    return pl.pallas_call(
        passing(stack_kernel, len(parts), len(deps)),
        out_shape=jax.ShapeDtypeStruct((m * len(parts), rows, cols), parts[0].dtype),
        in_specs=[vmem()] * len(parts) + [anywhere()] * len(deps),
        out_specs=vmem(),
        compiler_params=params(),
        cost_estimate=lasts(1),
        name="stack_parts",
    )(*parts, *deps)


def gather_step(current, count, group):
    shift, wide = group
    return [current] + [xor_permute(current, count, j << shift) for j in range(1, 1 << wide)]


def sum_kernel(count, *refs):
    ins, outs = refs[:count], refs[count:]
    for i, out in enumerate(outs):
        total = ins[0][i].astype(f32)
        for one in ins[1:]:
            total = total + one[i].astype(f32)
        out[...] = total.astype(out.dtype)


def sum_parts(arrays, deps=()):
    m, rows, cols = arrays[0].shape
    return pl.pallas_call(
        passing(functools.partial(sum_kernel, len(arrays)), len(arrays), len(deps)),
        out_shape=tuple(
            jax.ShapeDtypeStruct((rows, cols), f32 if i == 0 else bf16) for i in range(m)
        ),
        in_specs=[vmem()] * len(arrays) + [anywhere()] * len(deps),
        out_specs=(vmem(),) * m,
        compiler_params=params(),
        cost_estimate=lasts(2),
        name="sum_parts",
    )(*arrays, *deps)


def reduce_near(parts, count):
    return [parts[0]] + [xor_permute(parts[j], count, j) for j in range(1, len(parts))]


def reduce_far(pieces, count, wide):
    shift = wide.bit_length() - 1
    total = pieces[0]
    for h in range(1, len(pieces)):
        total = total + xor_permute(pieces[h], count, h << shift).astype(f32)
    return total


def load_kernel(pairs, scal, w_qkv, out_turned, mine, other, head, rest):
    for c in range(3):
        head[:, c * PAIR : (c + 1) * PAIR] = w_qkv[c, :, :PAIR]
        for i in range(1, pairs):
            at = (3 * (i - 1) + c) * PAIR
            rest[:, at : at + PAIR] = w_qkv[c, :, i * PAIR : (i + 1) * PAIR]
    rest[:, 3 * PAIR * (pairs - 1) :] = out_turned[...]
    mine, other = mine[...].astype(f32), other[...].astype(f32)
    first = scal[2] == 0
    gains = jnp.concatenate([jnp.where(first, mine, other), jnp.where(first, other, mine)], axis=0)
    low = lax.broadcasted_iota(jnp.int32, (gains.shape[0], PAIR), 1) < HEAD_DIM
    head[:, 3 * PAIR :] = jnp.where(low, gains[:, 0:1], gains[:, 1:2]).astype(bf16)


def attention_loads(scal, w_qkv, out_turned, mine, other):
    rows, cols = w_qkv.shape[1:]
    pairs = cols // PAIR
    shape = jax.ShapeDtypeStruct
    return pl.pallas_call(
        functools.partial(load_kernel, pairs),
        out_shape=(shape((rows, 4 * PAIR), bf16), shape((rows, 3 * PAIR * (pairs - 1) + cols), bf16)),
        in_specs=[smem()] + [vmem()] * 4,
        out_specs=(vmem(),) * 2,
        compiler_params=params(),
        cost_estimate=lasts(1),
        name="attention_loads",
    )(scal, w_qkv, out_turned, mine, other)


def placed_copies(parts, target, sems, me, rows):
    if len(parts) == 1:
        return [pltpu.make_async_copy(parts[0], target, sems.at[0])]
    copies = []
    wide = len(parts)
    for h in range(parts[0].shape[0]):
        for j in range(wide):
            own = jnp.bitwise_xor(me, h * wide + j)
            copies.append(
                pltpu.make_async_copy(
                    parts[j].at[h],
                    target.at[pl.ds(pl.multiple_of(own * rows, 16), rows)],
                    sems.at[h * wide + j],
                )
            )
    return copies


def document_starts(seg, length):
    starts = [jnp.int32(0)]
    for d in (1, 2, 3):
        starts.append(jnp.sum((seg < d).astype(jnp.int32)))
    return starts + [jnp.int32(length)]


def key_range(starts, live, first, size, length):
    last = jnp.minimum(first + size, live) - 1
    low = jnp.int32(0)
    high = jnp.int32(length)
    for d in (1, 2, 3):
        low = jnp.where(starts[d] <= first, starts[d], low)
    for d in (3, 2, 1):
        high = jnp.where(starts[d] > last, starts[d], high)
    high = jnp.minimum(high, live)
    return low, jnp.where(first < live, high, low)


def each_query_block(starts, live, length, size, step, work, empty):
    @pl.loop(0, length // size)
    def _(i):
        first = pl.multiple_of(i * size, size)
        low, high = key_range(starts, live, first, size, length)
        base = low // 16 * 16
        steps = (high - base + step - 1) // step
        base = pl.multiple_of(jnp.maximum(jnp.minimum(base, length - steps * step), 0), 16)
        rows = pl.ds(first, size)
        for w in range(1, length // step + 1):

            @pl.when(steps == w)
            def _():
                work(rows, pl.ds(base, w * step))

        @pl.when(steps <= 0)
        def _():
            empty(rows)


def lane_bounds(starts, live, length):
    column = lax.broadcasted_iota(jnp.int32, (1, PAIR), 1) & (HEAD_DIM - 1)
    low = jnp.zeros((1, PAIR), jnp.int32)
    high = jnp.where(column == 4, live, length)
    for d in range(4):
        low = jnp.where(column == d, starts[d], low)
        high = jnp.where(column == d, starts[d + 1], high)
    return column, low, high


def mask_features(bounds, first, size):
    column, low, high = bounds
    position = first + lax.broadcasted_iota(jnp.int32, (size, PAIR), 0)
    inside = (position >= low) & (position < high)
    column = jnp.broadcast_to(column, (size, PAIR))
    query = jnp.where((inside & (column < 4)) | (column == 4), 1.0, 0.0)
    return query, jnp.where(inside, 0.0, -BIG)


def rotary_block(table, turns, block):
    cos, sin = table[0], table[1]
    cos_at, sin_at = turns[0, pl.ds(block, 1), :], turns[1, pl.ds(block, 1), :]
    return cos * cos_at - sin * sin_at, sin * cos_at + cos * sin_at


def norm_stats(values):
    center = values - jnp.mean(values, axis=-1, keepdims=True)
    spread = jnp.mean(center * center, axis=-1, keepdims=True)
    inv = lax.rsqrt(spread + LAYER_EPS)
    return center * inv, inv


def norm_back(grad, normed, inv):
    return inv * (
        grad
        - jnp.mean(grad, axis=-1, keepdims=True)
        - normed * jnp.mean(grad * normed, axis=-1, keepdims=True)
    )


def half_swap(values, in_first):
    return jnp.where(in_first, pltpu.roll(values, PAIR - HEAD_DIM // 2, 1), pltpu.roll(values, HEAD_DIM // 2, 1))


def split3(values):
    a = values.astype(bf16)
    left = values - a.astype(f32)
    b = left.astype(bf16)
    return a, b, (left - b.astype(f32)).astype(bf16)


def forward_kernel(first, part_count, at, *refs):
    scal, seg, src, table, turns = refs[:5]
    parts = refs[5 : 5 + max(part_count, 1)]
    outs = refs[5 + max(part_count, 1) :]
    if first:
        a1, gains = outs[:2]
        outs = outs[2:]
    if part_count:
        w, outs = outs[0], outs[1:]
    else:
        w = parts[0]
    q_out, k_out, v_out, o_out, lse_out, qx, kx, vx, sems = outs
    length, width = src.shape
    live, me = scal[0], scal[1]

    copies = placed_copies(parts, w, sems, me, parts[0].shape[-2]) if part_count else []
    for copy in copies:
        copy.start()
    starts = document_starts(seg[...], length)
    bounds = lane_bounds(starts, live, length)
    for copy in copies:
        copy.wait()
    if first:
        turned = jnp.transpose(w[:, 3 * PAIR : 4 * PAIR].astype(f32))
        gains[0:8, :] = turned[0:8]
        gains[8:16, :] = turned[HEAD_DIM : HEAD_DIM + 8]
    lane = lax.broadcasted_iota(jnp.int32, (ROW_BLOCK, PAIR), 1)
    low_head = lane < HEAD_DIM
    in_first = (lane & (HEAD_DIM - 1)) < HEAD_DIM // 2
    zero = jnp.zeros((ROW_BLOCK, PAIR), bf16)

    @pl.loop(0, length // ROW_BLOCK)
    def _(b):
        rows = pl.ds(pl.multiple_of(b * ROW_BLOCK, ROW_BLOCK), ROW_BLOCK)
        if first:
            normed, _ = norm_stats(src[rows, :].astype(f32))
            a = (normed * gains[0:1, :]).astype(bf16)
            a1[rows, :] = a
        else:
            a = src[rows, :]
        qkv = jnp.dot(a, w[:, at : at + 3 * PAIR], preferred_element_type=f32)
        cos, sin = rotary_block(table, turns, b)
        query_mask, key_mask = mask_features(bounds, b * ROW_BLOCK, ROW_BLOCK)
        query_mask, key_mask = query_mask.astype(bf16), key_mask.astype(bf16)
        u = qkv[:, :PAIR]
        q = (u * cos + half_swap(u, in_first) * sin).astype(bf16)
        u = qkv[:, PAIR : 2 * PAIR]
        k = (u * cos + half_swap(u, in_first) * sin).astype(bf16)
        v = qkv[:, 2 * PAIR :].astype(bf16)
        q_out[rows, :] = q
        k_out[rows, :] = k
        v_out[rows, :] = v
        scaled = q.astype(f32) * LOG2_SCALE
        high = scaled.astype(bf16)
        rest = (scaled - high.astype(f32)).astype(bf16)
        for h in (0, 1):
            mine = low_head if h == 0 else ~low_head
            qx[h, rows, :PAIR] = jnp.where(mine, high, zero)
            qx[h, rows, PAIR:] = jnp.where(mine, rest, query_mask)
            kx[h, rows, :PAIR] = k
            kx[h, rows, PAIR:] = jnp.where(mine, k, key_mask)
        vx[rows, :PAIR] = v
        vx[rows, PAIR:] = jnp.ones((ROW_BLOCK, PAIR), bf16)

    lane_q = lax.broadcasted_iota(jnp.int32, (FWD_BQ, PAIR), 1) < HEAD_DIM

    def work(rows, keys):
        values = vx[keys, :]
        scores = [
            lax.dot_general(qx[h, rows, :], kx[h, keys, :], NT, preferred_element_type=f32) for h in (0, 1)
        ]
        tops, sums = [], []
        for h in (0, 1):
            top = jnp.max(scores[h], axis=1, keepdims=True)
            probs = jnp.exp2(scores[h] - top).astype(bf16)
            tops.append(top)
            sums.append(jnp.dot(probs, values, preferred_element_type=f32))
        total = jnp.where(lane_q, sums[0][:, PAIR:], sums[1][:, PAIR:])
        out = jnp.where(lane_q, sums[0][:, :PAIR], sums[1][:, :PAIR])
        o_out[rows, :] = (out / total).astype(bf16)
        lse_out[rows, :] = jnp.maximum(jnp.where(lane_q, tops[0], tops[1]) + jnp.log2(total), -1e20)

    def empty(rows):
        o_out[rows, :] = jnp.zeros((FWD_BQ, PAIR), bf16)
        lse_out[rows, :] = jnp.zeros((FWD_BQ, PAIR), f32)

    each_query_block(starts, live, length, FWD_BQ, FWD_STEP, work, empty)


def forward_pair(first, scal, seg, src, tables, parts, at, deps=()):
    length, width = src.shape
    shape = jax.ShapeDtypeStruct
    outs = [shape((length, PAIR), bf16)] * 4 + [shape((length, PAIR), f32)]
    pieces = isinstance(parts, list)
    operands = parts if pieces else [parts]
    if pieces:
        outs = [shape((width, parts[0].shape[-1]), bf16)] + outs
    if first:
        outs = [shape((length, width), bf16), shape((16, width), f32)] + outs
    kernel = functools.partial(forward_kernel, first, len(parts) if pieces else 0, at)
    return pl.pallas_call(
        passing(kernel, 5 + len(operands), len(deps)),
        out_shape=tuple(outs),
        in_specs=[smem(), vmem(), vmem(), vmem(), vmem()]
        + [hbm() if pieces else vmem()] * len(operands)
        + [anywhere()] * len(deps),
        out_specs=(vmem(),) * len(outs),
        scratch_shapes=[
            pltpu.VMEM((2, length, 2 * PAIR), bf16),
            pltpu.VMEM((2, length, 2 * PAIR), bf16),
            pltpu.VMEM((length, 2 * PAIR), bf16),
            pltpu.SemaphoreType.DMA((16,)),
        ],
        compiler_params=params(FWD_MIB),
        cost_estimate=lasts(18),
        name="attention_forward_first" if first else "attention_forward",
    )(scal, seg, src, *tables, *operands, *deps)


def backward_kernel(part_count, *refs):
    scal, seg, a1, near, far, w, q_in, k_in, v_in, o_in, lse, table, turns, dqkv = refs[:14]
    parts = refs[14 : 14 + part_count]
    (qx, kx, dx, vx, qm, km, dq, dk, dv, grads, sems) = refs[14 + part_count :]
    length, width = a1.shape
    half = length // 2
    live, me, core = scal[0], scal[1], scal[2]
    starts = document_starts(seg[...], length)
    bounds = lane_bounds(starts, live, length)
    halves = ((near, core), (far, 1 - core))
    lane = lax.broadcasted_iota(jnp.int32, (ROW_BLOCK, PAIR), 1)
    in_head = lane & (HEAD_DIM - 1)
    low_head = lane < HEAD_DIM
    in_first = in_head < HEAD_DIM // 2
    zero = jnp.zeros((ROW_BLOCK, PAIR), bf16)
    minus = jnp.full((ROW_BLOCK, PAIR), -1, bf16)

    def prepare(source, at, b):
        first = pl.multiple_of(at * half + b * ROW_BLOCK, ROW_BLOCK)
        rows = pl.ds(first, ROW_BLOCK)
        grad = jnp.dot(source[pl.ds(pl.multiple_of(b * ROW_BLOCK, ROW_BLOCK), ROW_BLOCK), :], w[...], preferred_element_type=f32).astype(bf16)
        query_mask, key_mask = mask_features(bounds, first, ROW_BLOCK)
        q, k = q_in[rows, :], k_in[rows, :]
        scaled = q.astype(f32) * LOG2_SCALE
        high = scaled.astype(bf16)
        rest = (scaled - high.astype(f32)).astype(bf16)
        la, lb, lc = split3(pltpu.roll(lse[rows, :], HEAD_DIM, 1))
        fq_b = jnp.where(
            in_head == 5, la, jnp.where(in_head == 6, lb, jnp.where(in_head == 7, lc, query_mask.astype(bf16)))
        )
        fk_b = jnp.where((in_head >= 5) & (in_head < 8), minus, key_mask.astype(bf16))
        inner = grad.astype(f32) * o_in[rows, :].astype(f32)
        for h in (0, 1):
            mine = low_head if h == 0 else ~low_head
            qx[h, rows, :PAIR] = jnp.where(mine, high, zero)
            qx[h, rows, PAIR:] = jnp.where(mine, rest, fq_b)
            kx[h, rows, :PAIR] = k
            kx[h, rows, PAIR:] = jnp.where(mine, k, fk_b)
            qm[h, rows, :] = jnp.where(mine, q, zero)
            km[h, rows, :] = jnp.where(mine, k, zero)
            dx[h, rows, :PAIR] = jnp.where(mine, grad, zero)
            delta = jnp.sum(jnp.where(mine, inner, 0.0), axis=1, keepdims=True)
            da, db, dc = split3(jnp.broadcast_to(delta, (ROW_BLOCK, PAIR)))
            dx[h, rows, PAIR:] = jnp.where(
                lane == 0, da, jnp.where(lane == 1, db, jnp.where(lane == 2, dc, zero))
            )
        vx[rows, :PAIR] = v_in[rows, :]
        vx[rows, PAIR:] = jnp.where(lane < 3, minus, zero)
        dk[rows, :] = jnp.zeros((ROW_BLOCK, PAIR), f32)
        dv[rows, :] = jnp.zeros((ROW_BLOCK, PAIR), f32)

    for source, at in halves:

        @pl.loop(0, half // ROW_BLOCK)
        def _(b):
            prepare(source, at, b)

    def work(rows, keys):
        grad_q = grad_k = grad_v = None
        for h in (0, 1):
            scores = lax.dot_general(qx[h, rows, :], kx[h, keys, :], NT, preferred_element_type=f32)
            pulled = lax.dot_general(dx[h, rows, :], vx[keys, :], NT, preferred_element_type=f32)
            probs = jnp.exp2(scores)
            grad_s = (probs * pulled).astype(bf16)
            one_q = jnp.dot(grad_s, km[h, keys, :], preferred_element_type=f32)
            one_v = lax.dot_general(probs.astype(bf16), dx[h, rows, :PAIR], TN, preferred_element_type=f32)
            one_k = lax.dot_general(grad_s, qm[h, rows, :], TN, preferred_element_type=f32)
            grad_q = one_q if h == 0 else grad_q + one_q
            grad_v = one_v if h == 0 else grad_v + one_v
            grad_k = one_k if h == 0 else grad_k + one_k
        dq[rows, :] = grad_q
        dv[keys, :] = dv[keys, :] + grad_v
        dk[keys, :] = dk[keys, :] + grad_k

    def empty(rows):
        dq[rows, :] = jnp.zeros((BWD_BQ, PAIR), f32)

    each_query_block(starts, live, length, BWD_BQ, BWD_STEP, work, empty)

    @pl.loop(0, length // ROW_BLOCK)
    def _(b):
        rows = pl.ds(pl.multiple_of(b * ROW_BLOCK, ROW_BLOCK), ROW_BLOCK)
        cos, sin = rotary_block(table, turns, b)
        u = dq[rows, :] * SCORE_SCALE
        dqkv[rows, :PAIR] = (u * cos - half_swap(u, in_first) * sin).astype(bf16)
        u = dk[rows, :] * SCORE_SCALE
        dqkv[rows, PAIR : 2 * PAIR] = (u * cos - half_swap(u, in_first) * sin).astype(bf16)
        dqkv[rows, 2 * PAIR :] = dv[rows, :].astype(bf16)

    for m in range(width // ROW_BLOCK):
        part = slice(m * ROW_BLOCK, (m + 1) * ROW_BLOCK)
        grads[part, : 3 * PAIR] = lax.dot_general(
            a1[:, part], dqkv[...], TN, preferred_element_type=f32
        ).astype(bf16)
        total = None
        for source, at in halves:
            rows = pl.ds(pl.multiple_of(at * half, half), half)
            term = lax.dot_general(source[:, part], o_in[rows, :], TN, preferred_element_type=f32)
            total = term if total is None else total + term
        grads[part, 3 * PAIR :] = total.astype(bf16)
    if part_count == 1:
        stores = [pltpu.make_async_copy(grads, parts[0], sems.at[0])]
    else:
        rows_each = parts[0].shape[1]
        stores = []
        for h in range(parts[0].shape[0]):
            for j in range(part_count):
                own = jnp.bitwise_xor(me, h * part_count + j)
                stores.append(
                    pltpu.make_async_copy(
                        grads.at[pl.ds(pl.multiple_of(own * rows_each, 16), rows_each)],
                        parts[j].at[h],
                        sems.at[h * part_count + j],
                    )
                )
    for copy in stores:
        copy.start()
    for copy in stores:
        copy.wait()


def backward_pair(scal, seg, a1, near, far, w, saved, tables, part_shapes, deps=()):
    length, width = a1.shape
    shape = jax.ShapeDtypeStruct
    outs = [shape((length, 3 * PAIR), bf16)] + [shape(s, bf16) for s in part_shapes]
    return pl.pallas_call(
        passing(functools.partial(backward_kernel, len(part_shapes)), 13, len(deps)),
        out_shape=tuple(outs),
        in_specs=[smem()] + [vmem()] * 12 + [anywhere()] * len(deps),
        out_specs=(vmem(),) + (anywhere(),) * len(part_shapes),
        scratch_shapes=[
            pltpu.VMEM((2, length, 2 * PAIR), bf16),
            pltpu.VMEM((2, length, 2 * PAIR), bf16),
            pltpu.VMEM((2, length, 2 * PAIR), bf16),
            pltpu.VMEM((length, 2 * PAIR), bf16),
            pltpu.VMEM((2, length, PAIR), bf16),
            pltpu.VMEM((2, length, PAIR), bf16),
            pltpu.VMEM((length, PAIR), f32),
            pltpu.VMEM((length, PAIR), f32),
            pltpu.VMEM((length, PAIR), f32),
            pltpu.VMEM((width, 4 * PAIR), bf16),
            pltpu.SemaphoreType.DMA((16,)),
        ],
        compiler_params=params(BWD_MIB),
        cost_estimate=lasts(30),
        name="attention_backward",
    )(scal, seg, a1, near, far, w, *saved, *tables, *deps)


def project_kernel(count, scal, *refs):
    rows, weights, out = refs[:count], refs[count : 2 * count], refs[2 * count]
    total = None
    for one, w in zip(rows, weights):
        term = lax.dot_general(one[...], w[...], NT, preferred_element_type=f32)
        total = term if total is None else total + term
    out[...] = total.astype(out.dtype)


def columns_of(weight, at, cols):
    return pl.BlockSpec((weight.shape[0], cols), lambda b, s: (0, at // cols))


def project_far_half(scal, rows, weights, deps=()):
    length, cols = rows[0].shape
    width = weights[0][0].shape[0]
    blocks = length // 2 // ROW_BLOCK
    count = len(rows)
    return pl.pallas_call(
        passing(functools.partial(project_kernel, count), 1 + 2 * count, len(deps)),
        out_shape=jax.ShapeDtypeStruct((length // 2, width), bf16),
        grid_spec=pltpu.PrefetchScalarGridSpec(
            num_scalar_prefetch=1,
            grid=(blocks,),
            in_specs=[pl.BlockSpec((ROW_BLOCK, cols), lambda b, s: (b + (1 - s[2]) * blocks, 0))] * count
            + [columns_of(w, at, cols) for w, at in weights]
            + [anywhere()] * len(deps),
            out_specs=pl.BlockSpec((ROW_BLOCK, width), lambda b, s: (b, 0)),
        ),
        compiler_params=params(),
        cost_estimate=lasts(4),
        name="project_far_half",
    )(scal, *rows, *[w for w, _ in weights], *deps)


def final_kernel(count, scal, *refs):
    rows, weights = refs[:count], refs[count : 2 * count]
    tokens, far, grad_hidden, gains, out = refs[2 * count :]
    total = far[...].astype(f32)
    for one, w in zip(rows, weights):
        total = total + lax.dot_general(one[...], w[...], NT, preferred_element_type=f32)
    normed, inv = norm_stats(tokens[...].astype(f32))
    out[...] = grad_hidden[...] + norm_back(total * gains[0:1, :], normed, inv)


def final_rows(scal, rows, weights, tokens, far, grad_hidden, gains):
    length, cols = rows[0].shape
    width = tokens.shape[1]
    blocks = length // 2 // ROW_BLOCK
    whole = lambda a: pl.BlockSpec(a.shape, lambda b, s: (0, 0))
    near = lambda a: pl.BlockSpec((ROW_BLOCK, a.shape[1]), lambda b, s: (b + s[2] * blocks, 0))
    plain = pl.BlockSpec((ROW_BLOCK, width), lambda b, s: (b, 0))
    return pl.pallas_call(
        functools.partial(final_kernel, len(rows)),
        out_shape=jax.ShapeDtypeStruct((length // 2, width), f32),
        grid_spec=pltpu.PrefetchScalarGridSpec(
            num_scalar_prefetch=1,
            grid=(blocks,),
            in_specs=[near(r) for r in rows]
            + [columns_of(w, at, cols) for w, at in weights]
            + [near(tokens), plain, plain, whole(gains)],
            out_specs=plain,
        ),
        compiler_params=params(),
        cost_estimate=lasts(7),
        name="final_rows",
    )(scal, *rows, *[w for w, _ in weights], tokens, far, grad_hidden, gains)


def ffn_kernel(count, split, down_cols, scal, *refs):
    outs_of, weights = refs[:count], refs[count : 2 * count]
    tokens, far, cot, gains, ffn_w = refs[2 * count : 2 * count + 5]
    result, dattn, grad_hidden, keep, send, z_all, pair_all, a2_all, dff_all = refs[2 * count + 5 :]
    width, ff = ffn_w.shape[1:]
    live, me, core = scal[0], scal[1], scal[2]
    step = pl.program_id(0)
    block = result.shape[0]

    here = core * (block * pl.num_programs(0)) + step * block
    position = here + lax.broadcasted_iota(jnp.int32, (block, 1), 0)
    valid = (position < live).astype(f32)
    attn = far[...].astype(f32)
    for one, w in zip(outs_of, weights):
        attn = attn + lax.dot_general(one[...], w[...], NT, preferred_element_type=f32)
    hidden = tokens[...].astype(f32) + valid * attn
    normed, inv = norm_stats(hidden)
    gain = gains[8:9, :]
    a2 = (normed * gain).astype(bf16)
    up = jnp.dot(a2, ffn_w[0], preferred_element_type=f32)
    gate = jnp.dot(a2, ffn_w[1], preferred_element_type=f32)
    below = 0.5 * (1.0 + lax.erf(up * math.sqrt(0.5)))
    act = up * below
    slope = below + up * jnp.exp(up * up * -0.5) * (1.0 / math.sqrt(2.0 * math.pi))
    z = (act * gate).astype(bf16)
    result[...] = (
        hidden + valid * lax.dot_general(z, ffn_w[2], NT, preferred_element_type=f32)
    ).astype(bf16)
    dy = cot[...].astype(f32)
    dff = (valid * dy).astype(bf16)
    dz = jnp.dot(dff, ffn_w[2], preferred_element_type=f32)
    du = (dz * gate * slope).astype(bf16)
    dg = (dz * act).astype(bf16)
    da2 = lax.dot_general(du, ffn_w[0], NT, preferred_element_type=f32) + lax.dot_general(
        dg, ffn_w[1], NT, preferred_element_type=f32
    )
    grad = dy + norm_back(da2 * gain, normed, inv)
    grad_hidden[...] = grad
    dattn[...] = (valid * grad).astype(bf16)
    rows = pl.ds(pl.multiple_of(step * block, block), block)
    z_all[rows, :] = z
    pair_all[0, rows, :] = du
    pair_all[1, rows, :] = dg
    a2_all[rows, :] = a2
    dff_all[rows, :] = dff

    @pl.when(step == pl.num_programs(0) - 1)
    def _():
        for m in range(width // ROW_BLOCK):
            part = slice(m * ROW_BLOCK, (m + 1) * ROW_BLOCK)
            left = a2_all[:, part]
            down = dff_all[:, part]
            if not split:
                for i in (0, 1):
                    keep[i, part, :] = lax.dot_general(
                        left, pair_all[i], TN, preferred_element_type=f32
                    ).astype(bf16)
                send[part, :] = lax.dot_general(down, z_all[...], TN, preferred_element_type=f32).astype(bf16)
            else:
                offset = ff - down_cols
                for out, who in ((send, 1 - core), (keep, core)):
                    out[part, :ff] = lax.dot_general(
                        left, pair_all[who], TN, preferred_element_type=f32
                    ).astype(bf16)
                    out[part, ff:] = lax.dot_general(
                        down,
                        z_all[:, pl.ds(pl.multiple_of(who * offset, PAIR), down_cols)],
                        TN,
                        preferred_element_type=f32,
                    ).astype(bf16)


def feed_forward(scal, outs_of, weights, tokens, far, cot, gains, ffn_w, down_cols, split):
    length = tokens.shape[0]
    half = length // 2
    blocks = half // ROW_BLOCK
    width, ff = ffn_w.shape[1:]
    shape = jax.ShapeDtypeStruct
    whole = lambda a: pl.BlockSpec(a.shape, lambda b, s: (0,) * len(a.shape))
    near = lambda a: pl.BlockSpec((ROW_BLOCK, a.shape[1]), lambda b, s: (b + s[2] * blocks, 0))
    plain = pl.BlockSpec((ROW_BLOCK, width), lambda b, s: (b, 0))
    if not split:
        grads = (shape((2, width, ff), bf16), shape((width, ff), bf16))
    else:
        grads = (shape((width, ff + down_cols), bf16),) * 2
    return pl.pallas_call(
        functools.partial(ffn_kernel, len(outs_of), split, down_cols),
        out_shape=(shape((half, width), bf16), shape((half, width), bf16), shape((half, width), f32)) + grads,
        grid_spec=pltpu.PrefetchScalarGridSpec(
            num_scalar_prefetch=1,
            grid=(blocks,),
            in_specs=[near(o) for o in outs_of]
            + [columns_of(w, at, PAIR) for w, at in weights]
            + [near(tokens), plain, plain, whole(gains)]
            + [vmem()],
            out_specs=(plain, plain, plain) + tuple(whole(g) for g in grads),
            scratch_shapes=[
                pltpu.VMEM((half, ff), bf16),
                pltpu.VMEM((2, half, ff), bf16),
                pltpu.VMEM((half, width), bf16),
                pltpu.VMEM((half, width), bf16),
            ],
        ),
        compiler_params=params(FFN_MIB),
        cost_estimate=lasts(35),
        name="feed_forward",
    )(scal, *outs_of, *[w for w, _ in weights], tokens, far, cot, gains, ffn_w)


def pack_kernel(wide, scal, keep, got, *outs):
    me = scal[1]
    for j in range(wide):
        for h in range(outs[0].shape[0]):
            own = jnp.bitwise_xor(me, h * wide + j)
            outs[j][h] = (keep[own].astype(f32) + got[own].astype(f32)).astype(bf16)


def pack_parts(scal, keep, got, count, deps=()):
    width, cols = keep.shape
    rows = width // count
    wide = 1 << bit_groups(count)[-1][1]
    shape = jax.ShapeDtypeStruct((count // wide, rows, cols), bf16)
    return pl.pallas_call(
        passing(functools.partial(pack_kernel, wide), 3, len(deps)),
        out_shape=(shape,) * wide,
        in_specs=[smem(), vmem(), vmem()] + [anywhere()] * len(deps),
        out_specs=(vmem(),) * wide,
        compiler_params=params(),
        cost_estimate=lasts(4),
        name="pack_parts",
    )(scal, keep.reshape(count, rows, cols), got.reshape(count, rows, cols), *deps)


def rotary_tables(length):
    freqs = ROPE_THETA ** (-np.arange(0, HEAD_DIM, 2) / HEAD_DIM)
    freqs = np.tile(np.float32(freqs).astype(np.float64), 4)
    sign = np.where(np.arange(PAIR) % HEAD_DIM < HEAD_DIM // 2, -1.0, 1.0)

    def both(positions):
        angles = positions[:, None] * freqs[None, :]
        return jnp.asarray(np.stack([np.cos(angles), np.sin(angles) * sign]), f32)

    return both(np.arange(ROW_BLOCK)), both(np.arange(0, length, ROW_BLOCK))


def local(tokens, segment_ids, counts, w_qkv, w_out, w_in, w_down, ln1_gain, ln2_gain, cotangent):
    count = lax.axis_size("dp")
    dp, core = lax.axis_index("dp"), lax.axis_index("head")
    length, width = tokens.shape[1:]
    ff = w_in.shape[2]
    rows_each = width // count
    fast = rows_each % 16 == 0 and count & (count - 1) == 0 and len(bit_groups(count)) == 2
    pairs = w_qkv.shape[2] // PAIR
    first_core = core == 0
    pick = lambda a, b: jnp.where(first_core, a, b)
    join = lambda mine, other: jnp.concatenate([pick(mine, other), pick(other, mine)], axis=0)
    row, cot = tokens[0], cotangent[0]
    seg = segment_ids[0]
    live = counts[0]
    scal = jnp.stack([live, dp, core]).astype(jnp.int32)
    seg_tile = seg.reshape(-1, 128)

    both = jnp.stack([ln1_gain, ln2_gain], axis=1)
    head_load, rest_load = attention_loads(scal, w_qkv, w_out.T, both, core_swap(both))
    down_turned = w_down.T
    down_cols = -(-(ff // 2) // 128) * 128
    offset = ff - down_cols
    tables = rotary_tables(length)
    out_at = 3 * PAIR * (pairs - 1)
    everyone = ("dp", "head")
    ffn_w = lax.all_gather(jnp.concatenate([w_in, down_turned[None]]), everyone, axis=1, tiled=True)

    if fast:
        high_bits, low_bits = bit_groups(count)
        head_high = gather_step(head_load[None], count, high_bits)
        rest_load = stack_parts([rest_load[None]], head_high[1:])
        head_parts = gather_step(stack_parts(head_high), count, low_bits)
        rest_high = gather_step(rest_load, count, high_bits)
        rest_all = stack_parts(rest_high, head_parts[1:])
        a1, gains, *kept = forward_pair(
            True, scal, seg_tile, row, tables, head_parts, 0, [rest_all]
        )
        rest_parts = gather_step(rest_all, count, low_bits)
    else:
        head_parts = [lax.all_gather(head_load, "dp", axis=0, tiled=True)]
        rest_parts = [lax.all_gather(rest_load, "dp", axis=0, tiled=True)]
        a1, gains, *kept = forward_pair(True, scal, seg_tile, row, tables, head_parts, 0)

    head_w, saved = kept[0], [kept[1:]]
    rest_w, *kept = forward_pair(False, scal, seg_tile, a1, tables, rest_parts, 0)
    saved.append(kept)
    for i in range(2, pairs):
        saved.append(forward_pair(False, scal, seg_tile, a1, tables, rest_w, 3 * PAIR * (i - 1)))
    qkv_w = [(head_w, 0)] + [(rest_w, 3 * PAIR * (i - 1)) for i in range(1, pairs)]
    out_w = [(rest_w, out_at + i * PAIR) for i in range(pairs)]
    outs_of = [s[3] for s in saved]

    far = core_swap(project_far_half(scal, outs_of, out_w))
    result, near_grad, grad_hidden, keep, send = feed_forward(
        scal, outs_of, out_w, row, far, cot, gains, ffn_w, down_cols, fast
    )
    far_grad = core_swap(near_grad)

    def backward(i, deps):
        w, at = out_w[i]
        return backward_pair(
            scal, seg_tile, a1, near_grad, far_grad, w[:, at : at + PAIR], saved[i], tables, part_shapes, deps
        )

    if fast:
        wide = 1 << low_bits[1]
        part_shapes = [(count // wide, rows_each, 4 * PAIR)] * wide
        got = core_swap(send)
        dqkv, near_parts, shards = [], [], []
        deps = []
        ffn_pieces = None
        for i in range(pairs):
            one, *parts = backward(i, deps)
            dqkv.append(one)
            near_parts.append(reduce_near(parts, count))
            if i == 0:
                ffn_near = pack_parts(scal, keep, got, count, [one])
                deps = list(ffn_near)
                ffn_near = reduce_near(ffn_near, count)
            elif i < pairs - 1:
                ffn_pieces = sum_parts(ffn_near, [one])
                pieces = sum_parts(near_parts[i - 1], [one])
                deps = list(ffn_pieces) + list(pieces)
                shards.append(reduce_far(pieces, count, wide))
        done = reduce_far(ffn_pieces, count, wide)
        pieces = sum_parts(near_parts[-2], dqkv[-1:])
        shards.append(reduce_far(pieces, count, wide))
        far_da = core_swap(project_far_half(scal, dqkv, qkv_w, pieces))
        pieces = sum_parts(near_parts[-1])
        shards.append(reduce_far(pieces, count, wide))
        rows_here = w_in.shape[1]
        low, high = done[:rows_here], done[rows_here:]
        mine = pick(low, high)
        other = core_swap(pick(high, low))
        grad_w_in = jnp.stack(
            [pick(mine[:, :ff], other[:, :ff]), pick(other[:, :ff], mine[:, :ff])]
        )
        grad_down = jnp.concatenate(
            [pick(mine[:, ff:], other[:, ff:]), pick(other[:, ff:], mine[:, ff:])[:, down_cols - offset :]],
            axis=1,
        ).T
    else:
        part_shapes = [(width, 4 * PAIR)]
        grad_w_in = lax.psum_scatter(keep.astype(f32), everyone, scatter_dimension=1, tiled=True)
        grad_down = lax.psum_scatter(send.astype(f32), everyone, scatter_dimension=0, tiled=True).T
        dqkv, shards = [], []
        for i in range(pairs):
            one, parts = backward(i, ())
            dqkv.append(one)
            shards.append(lax.psum_scatter(parts.astype(f32), "dp", scatter_dimension=0, tiled=True))
        far_da = core_swap(project_far_half(scal, dqkv, qkv_w))

    grad_two = jnp.sum(grad_w_in * w_in.astype(f32), axis=(0, 2)) / ln2_gain.astype(f32)
    grad_tokens = final_rows(scal, dqkv, qkv_w, row, far_da, grad_hidden, gains)

    grad_qkv = jnp.stack(
        [jnp.concatenate([s[:, c * PAIR : (c + 1) * PAIR] for s in shards], axis=1) for c in range(3)]
    )
    grad_out = jnp.concatenate([s[:, 3 * PAIR :] for s in shards], axis=1).T
    partial = jnp.sum(grad_qkv * w_qkv.astype(f32), axis=(0, 2))
    rows_here = ln1_gain.shape[0]
    low, high = partial[:rows_here], partial[rows_here:]
    grad_one = (pick(low, high) + core_swap(pick(high, low))) / ln1_gain.astype(f32)
    return (
        result[None],
        grad_tokens[None],
        grad_qkv,
        grad_out,
        grad_w_in,
        grad_down,
        grad_one,
        grad_two,
    )


def solution(mesh):
    placed = (
        P("dp", None, None),
        P("dp", None),
        P("dp"),
        P(None, "dp", "head"),
        P("head", "dp"),
        P(None, ("dp", "head"), None),
        P(None, ("dp", "head")),
        P(("dp", "head")),
        P(("dp", "head")),
        P("dp", "head", None),
    )
    return jax.shard_map(
        local,
        mesh=mesh,
        in_specs=placed,
        out_specs=(
            P("dp", "head", None),
            P("dp", "head", None),
            P(None, "dp", "head"),
            P("head", "dp"),
            P(None, ("dp", "head"), None),
            P(None, ("dp", "head")),
            P(("dp", "head")),
            P(("dp", "head")),
        ),
        check_vma=False,
    )
```

```python
import functools
import math

import jax
import jax.numpy as jnp
import numpy as np
from jax import lax
from jax.experimental import pallas as pl
from jax.experimental.pallas import tpu as pltpu
from jax.sharding import PartitionSpec as P

HEAD_DIM = 64
PAIR = 2 * HEAD_DIM
LAYER_EPS = 1e-05
ROPE_THETA = 160000.0
BIG = 1e30
LOG2_SCALE = math.log2(math.e) / math.sqrt(HEAD_DIM)
SCORE_SCALE = 1.0 / math.sqrt(HEAD_DIM)
ROW_BLOCK = 256
FWD_MIB, BWD_MIB, FFN_MIB = 20, 23, 18
FWD_BQ, FWD_STEP = 512, 256
BWD_BQ, BWD_STEP, BWD_CHUNK = 256, 128, 12
NT = (((1,), (1,)), ((), ()))
TN = (((0,), (0,)), ((), ()))
bf16 = jnp.bfloat16
f32 = jnp.float32


def vmem():
    return pl.BlockSpec(memory_space=pltpu.VMEM)


def smem():
    return pl.BlockSpec(memory_space=pltpu.SMEM)


def hbm():
    return pl.BlockSpec(memory_space=pltpu.HBM)


def anywhere():
    return pl.BlockSpec(memory_space=pl.ANY)


def params(mib=10):
    return pltpu.CompilerParams(vmem_limit_bytes=mib << 20)


def lasts(micros):
    return pl.CostEstimate(flops=int(micros * 1e8), bytes_accessed=0, transcendentals=0)


def passing(kernel, inputs, deps):
    def run(*refs):
        kernel(*refs[:inputs], *refs[inputs + deps :])

    return run


def bit_groups(count):
    bits = count.bit_length() - 1
    shifts = []
    low = 0
    while low < bits:
        wide = min(2, bits - low)
        shifts.append((low, wide))
        low += wide
    return shifts[::-1]


def xor_permute(value, count, mask):
    return lax.ppermute(value, "dp", [(i, i ^ mask) for i in range(count)])


def core_swap(value):
    return lax.ppermute(value, "head", [(0, 1), (1, 0)])


def stack_kernel(*refs):
    ins, out = refs[:-1], refs[-1]
    wide = len(ins)
    for j, one in enumerate(ins):
        for h in range(one.shape[0]):
            out[h * wide + j] = one[h]


def stack_parts(parts, deps=()):
    m, rows, cols = parts[0].shape
    return pl.pallas_call(
        passing(stack_kernel, len(parts), len(deps)),
        out_shape=jax.ShapeDtypeStruct((m * len(parts), rows, cols), parts[0].dtype),
        in_specs=[vmem()] * len(parts) + [anywhere()] * len(deps),
        out_specs=vmem(),
        compiler_params=params(),
        cost_estimate=lasts(1),
        name="stack_parts",
    )(*parts, *deps)


def gather_step(current, count, group):
    shift, wide = group
    return [current] + [xor_permute(current, count, j << shift) for j in range(1, 1 << wide)]


def sum_kernel(count, *refs):
    ins, outs = refs[:count], refs[count:]
    for i, out in enumerate(outs):
        total = ins[0][i].astype(f32)
        for one in ins[1:]:
            total = total + one[i].astype(f32)
        out[...] = total.astype(out.dtype)


def sum_parts(arrays, deps=()):
    m, rows, cols = arrays[0].shape
    return pl.pallas_call(
        passing(functools.partial(sum_kernel, len(arrays)), len(arrays), len(deps)),
        out_shape=tuple(
            jax.ShapeDtypeStruct((rows, cols), f32 if i == 0 else bf16) for i in range(m)
        ),
        in_specs=[vmem()] * len(arrays) + [anywhere()] * len(deps),
        out_specs=(vmem(),) * m,
        compiler_params=params(),
        cost_estimate=lasts(2),
        name="sum_parts",
    )(*arrays, *deps)


def reduce_near(parts, count):
    return [parts[0]] + [xor_permute(parts[j], count, j) for j in range(1, len(parts))]


def far_pieces(pieces, count, wide):
    shift = wide.bit_length() - 1
    return [pieces[0]] + [xor_permute(pieces[h], count, h << shift) for h in range(1, len(pieces))]


def reduce_far(pieces, count, wide):
    total, *others = far_pieces(pieces, count, wide)
    for one in others:
        total = total + one.astype(f32)
    return total


def load_kernel(pairs, scal, w_qkv, out_turned, mine, other, head, rest):
    for c in range(3):
        head[:, c * PAIR : (c + 1) * PAIR] = w_qkv[c, :, :PAIR]
        for i in range(1, pairs):
            at = (3 * (i - 1) + c) * PAIR
            rest[:, at : at + PAIR] = w_qkv[c, :, i * PAIR : (i + 1) * PAIR]
    rest[:, 3 * PAIR * (pairs - 1) :] = out_turned[...]
    mine, other = mine[...].astype(f32), other[...].astype(f32)
    first = scal[0] == 0
    gains = jnp.concatenate([jnp.where(first, mine, other), jnp.where(first, other, mine)], axis=0)
    low = lax.broadcasted_iota(jnp.int32, (gains.shape[0], PAIR), 1) < HEAD_DIM
    head[:, 3 * PAIR :] = jnp.where(low, gains[:, 0:1], gains[:, 1:2]).astype(bf16)


def attention_loads(scal, w_qkv, out_turned, mine, other):
    rows, cols = w_qkv.shape[1:]
    pairs = cols // PAIR
    shape = jax.ShapeDtypeStruct
    return pl.pallas_call(
        functools.partial(load_kernel, pairs),
        out_shape=(shape((rows, 4 * PAIR), bf16), shape((rows, 3 * PAIR * (pairs - 1) + cols), bf16)),
        in_specs=[smem()] + [vmem()] * 4,
        out_specs=(vmem(),) * 2,
        compiler_params=params(),
        cost_estimate=lasts(1),
        name="attention_loads",
    )(scal, w_qkv, out_turned, mine, other)


def placed_copies(parts, target, sems, me, rows, cols):
    if len(parts) == 1:
        return [pltpu.make_async_copy(parts[0].at[:, cols], target.at[:, cols], sems.at[0])]
    copies = []
    wide = len(parts)
    for h in range(parts[0].shape[0]):
        for j in range(wide):
            own = jnp.bitwise_xor(me, h * wide + j)
            copies.append(
                pltpu.make_async_copy(
                    parts[j].at[h, :, cols],
                    target.at[pl.ds(pl.multiple_of(own * rows, 16), rows), cols],
                    sems.at[h * wide + j],
                )
            )
    return copies


def document_starts(scal, length):
    return [jnp.int32(0), scal[3], scal[4], scal[5], jnp.int32(length)]


def key_range(starts, live, first, size, length):
    last = jnp.minimum(first + size, live) - 1
    low = jnp.int32(0)
    high = jnp.int32(length)
    for d in (1, 2, 3):
        low = jnp.where(starts[d] <= first, starts[d], low)
    for d in (3, 2, 1):
        high = jnp.where(starts[d] > last, starts[d], high)
    high = jnp.minimum(high, live)
    seen = first < live
    return jnp.where(seen, low, 0), jnp.where(seen, high, 0)


def each_query_block(starts, live, length, size, step, work, empty):
    @pl.loop(0, length // size)
    def _(i):
        first = pl.multiple_of(i * size, size)
        low, high = key_range(starts, live, first, size, length)
        base = low // 16 * 16
        steps = (high - base + step - 1) // step
        base = pl.multiple_of(jnp.maximum(jnp.minimum(base, length - steps * step), 0), 16)
        rows = pl.ds(first, size)
        for w in range(1, length // step + 1):

            @pl.when(steps == w)
            def _():
                work(rows, pl.ds(base, w * step))

        @pl.when(steps <= 0)
        def _():
            empty(rows)


def each_key_chunk(starts, live, length, size, step, most, work):
    @pl.loop(0, length // size)
    def _(i):
        first = pl.multiple_of(i * size, size)
        low, high = key_range(starts, live, first, size, length)
        base = low // 16 * 16
        steps = (high - base + step - 1) // step
        base = jnp.maximum(jnp.minimum(base, length - steps * step), 0)
        rows = pl.ds(first, size)

        @pl.loop(0, (steps + most - 1) // most)
        def _(c):
            at = pl.multiple_of(base + c * (most * step), 16)
            left = jnp.minimum(steps - c * most, most)
            for w in range(1, most + 1):

                @pl.when(left == w)
                def _():
                    work(rows, pl.ds(at, w * step))


def lane_bounds(starts, live, length):
    column = lax.broadcasted_iota(jnp.int32, (1, PAIR), 1) & (HEAD_DIM - 1)
    low = jnp.zeros((1, PAIR), jnp.int32)
    high = jnp.where(column == 4, live, length)
    for d in range(4):
        low = jnp.where(column == d, starts[d], low)
        high = jnp.where(column == d, starts[d + 1], high)
    return column, low, high


def mask_features(bounds, first, size):
    column, low, high = bounds
    position = first + lax.broadcasted_iota(jnp.int32, (size, PAIR), 0)
    inside = (position >= low) & (position < high)
    column = jnp.broadcast_to(column, (size, PAIR))
    query = jnp.where((inside & (column < 4)) | (column == 4), 1.0, 0.0)
    return query, jnp.where(inside, 0.0, -BIG)


def rotary_block(table, turns, block):
    cos, sin = table[0], table[1]
    cos_at, sin_at = turns[0, pl.ds(block, 1), :], turns[1, pl.ds(block, 1), :]
    return cos * cos_at - sin * sin_at, sin * cos_at + cos * sin_at


def norm_stats(values):
    center = values - jnp.mean(values, axis=-1, keepdims=True)
    spread = jnp.mean(center * center, axis=-1, keepdims=True)
    inv = lax.rsqrt(spread + LAYER_EPS)
    return center * inv, inv


def norm_back(grad, normed, inv):
    return inv * (
        grad
        - jnp.mean(grad, axis=-1, keepdims=True)
        - normed * jnp.mean(grad * normed, axis=-1, keepdims=True)
    )


def half_swap(values, in_first):
    return jnp.where(in_first, pltpu.roll(values, PAIR - HEAD_DIM // 2, 1), pltpu.roll(values, HEAD_DIM // 2, 1))


def split3(values):
    a = values.astype(bf16)
    left = values - a.astype(f32)
    b = left.astype(bf16)
    return a, b, (left - b.astype(f32)).astype(bf16)


def forward_kernel(first, part_count, at, *refs):
    scal, src, table, turns = refs[:4]
    parts = refs[4 : 4 + max(part_count, 1)]
    outs = refs[4 + max(part_count, 1) :]
    if first:
        a1, gains = outs[:2]
        outs = outs[2:]
    if part_count:
        w, outs = outs[0], outs[1:]
    else:
        w = parts[0]
    q_out, k_out, v_out, o_out, lse_out, qx, kx, vx, sems = outs
    length, width = src.shape
    live, me = scal[0], scal[1]

    copies, later = [], []
    if part_count:
        soon = 4 * PAIR if first else 3 * PAIR
        copies = placed_copies(parts, w, sems.at[0], me, parts[0].shape[-2], slice(0, soon))
        if w.shape[1] > soon:
            later = placed_copies(parts, w, sems.at[1], me, parts[0].shape[-2], slice(soon, w.shape[1]))
    for copy in copies + later:
        copy.start()
    starts = document_starts(scal, length)
    bounds = lane_bounds(starts, live, length)
    for copy in copies:
        copy.wait()
    if first:
        turned = jnp.transpose(w[:, 3 * PAIR : 4 * PAIR].astype(f32))
        gains[0:8, :] = turned[0:8]
        gains[8:16, :] = turned[HEAD_DIM : HEAD_DIM + 8]
    lane = lax.broadcasted_iota(jnp.int32, (ROW_BLOCK, PAIR), 1)
    low_head = lane < HEAD_DIM
    in_first = (lane & (HEAD_DIM - 1)) < HEAD_DIM // 2
    zero = jnp.zeros((ROW_BLOCK, PAIR), bf16)

    @pl.loop(0, length // ROW_BLOCK)
    def _(b):
        rows = pl.ds(pl.multiple_of(b * ROW_BLOCK, ROW_BLOCK), ROW_BLOCK)
        if first:
            normed, _ = norm_stats(src[rows, :].astype(f32))
            a = (normed * gains[0:1, :]).astype(bf16)
            a1[rows, :] = a
        else:
            a = src[rows, :]
        qkv = jnp.dot(a, w[:, at : at + 3 * PAIR], preferred_element_type=f32)
        cos, sin = rotary_block(table, turns, b)
        query_mask, key_mask = mask_features(bounds, b * ROW_BLOCK, ROW_BLOCK)
        query_mask, key_mask = query_mask.astype(bf16), key_mask.astype(bf16)
        u = qkv[:, :PAIR]
        q = (u * cos + half_swap(u, in_first) * sin).astype(bf16)
        u = qkv[:, PAIR : 2 * PAIR]
        k = (u * cos + half_swap(u, in_first) * sin).astype(bf16)
        v = qkv[:, 2 * PAIR :].astype(bf16)
        q_out[rows, :] = q
        k_out[rows, :] = k
        v_out[rows, :] = v
        scaled = q.astype(f32) * LOG2_SCALE
        high = scaled.astype(bf16)
        rest = (scaled - high.astype(f32)).astype(bf16)
        for h in (0, 1):
            mine = low_head if h == 0 else ~low_head
            qx[h, rows, :PAIR] = jnp.where(mine, high, zero)
            qx[h, rows, PAIR:] = jnp.where(mine, rest, query_mask)
            kx[h, rows, :PAIR] = k
            kx[h, rows, PAIR:] = jnp.where(mine, k, key_mask)
        vx[rows, :PAIR] = v
        vx[rows, PAIR:] = jnp.ones((ROW_BLOCK, PAIR), bf16)

    lane_q = lax.broadcasted_iota(jnp.int32, (FWD_BQ, PAIR), 1) < HEAD_DIM

    def work(rows, keys):
        values = vx[keys, :]
        scores = [
            lax.dot_general(qx[h, rows, :], kx[h, keys, :], NT, preferred_element_type=f32) for h in (0, 1)
        ]
        tops, sums = [], []
        for h in (0, 1):
            top = jnp.max(scores[h], axis=1, keepdims=True)
            probs = jnp.exp2(scores[h] - top).astype(bf16)
            tops.append(top)
            sums.append(jnp.dot(probs, values, preferred_element_type=f32))
        total = jnp.where(lane_q, sums[0][:, PAIR:], sums[1][:, PAIR:])
        out = jnp.where(lane_q, sums[0][:, :PAIR], sums[1][:, :PAIR])
        o_out[rows, :] = (out / total).astype(bf16)
        lse_out[rows, :] = jnp.maximum(jnp.where(lane_q, tops[0], tops[1]) + jnp.log2(total), -1e20)

    def empty(rows):
        o_out[rows, :] = jnp.zeros((FWD_BQ, PAIR), bf16)
        lse_out[rows, :] = jnp.zeros((FWD_BQ, PAIR), f32)

    each_query_block(starts, live, length, FWD_BQ, FWD_STEP, work, empty)
    for copy in later:
        copy.wait()


def forward_pair(first, scal, src, tables, parts, at, deps=()):
    length, width = src.shape
    shape = jax.ShapeDtypeStruct
    outs = [shape((length, PAIR), bf16)] * 4 + [shape((length, PAIR), f32)]
    pieces = isinstance(parts, list)
    operands = parts if pieces else [parts]
    if pieces:
        outs = [shape((width, parts[0].shape[-1]), bf16)] + outs
    if first:
        outs = [shape((length, width), bf16), shape((16, width), f32)] + outs
    kernel = functools.partial(forward_kernel, first, len(parts) if pieces else 0, at)
    return pl.pallas_call(
        passing(kernel, 4 + len(operands), len(deps)),
        out_shape=tuple(outs),
        in_specs=[smem(), vmem(), vmem(), vmem()]
        + [hbm() if pieces else vmem()] * len(operands)
        + [anywhere()] * len(deps),
        out_specs=(vmem(),) * len(outs),
        scratch_shapes=[
            pltpu.VMEM((2, length, 2 * PAIR), bf16),
            pltpu.VMEM((2, length, 2 * PAIR), bf16),
            pltpu.VMEM((length, 2 * PAIR), bf16),
            pltpu.SemaphoreType.DMA((2, 16)),
        ],
        compiler_params=params(FWD_MIB),
        cost_estimate=lasts(18),
        name="attention_forward_first" if first else "attention_forward",
    )(scal, src, *tables, *operands, *deps)


def backward_kernel(part_count, carried, *refs):
    scal, a1, near, far, w, q_in, k_in, v_in, o_in, lse, table, turns = refs[:12]
    before = refs[12 : 12 + carried]
    refs = refs[12 + carried :]
    dqkv, parts = refs[0], refs[1 : 1 + part_count]
    (qx, kx, dx, vx, qm, km, dq, dk, dv, grads, sems) = refs[1 + part_count :]
    length, width = a1.shape
    half = length // 2
    live, me, core = scal[0], scal[1], scal[2]
    starts = document_starts(scal, length)
    bounds = lane_bounds(starts, live, length)
    halves = ((near, core), (far, 1 - core))
    lane = lax.broadcasted_iota(jnp.int32, (ROW_BLOCK, PAIR), 1)
    in_head = lane & (HEAD_DIM - 1)
    low_head = lane < HEAD_DIM
    in_first = in_head < HEAD_DIM // 2
    zero = jnp.zeros((ROW_BLOCK, PAIR), bf16)
    minus = jnp.full((ROW_BLOCK, PAIR), -1, bf16)

    def prepare(source, at, b):
        first = pl.multiple_of(at * half + b * ROW_BLOCK, ROW_BLOCK)
        rows = pl.ds(first, ROW_BLOCK)
        grad = jnp.dot(source[pl.ds(pl.multiple_of(b * ROW_BLOCK, ROW_BLOCK), ROW_BLOCK), :], w[...], preferred_element_type=f32).astype(bf16)
        query_mask, key_mask = mask_features(bounds, first, ROW_BLOCK)
        q, k = q_in[rows, :], k_in[rows, :]
        scaled = q.astype(f32) * LOG2_SCALE
        high = scaled.astype(bf16)
        rest = (scaled - high.astype(f32)).astype(bf16)
        la, lb, lc = split3(pltpu.roll(lse[rows, :], HEAD_DIM, 1))
        fq_b = jnp.where(
            in_head == 5, la, jnp.where(in_head == 6, lb, jnp.where(in_head == 7, lc, query_mask.astype(bf16)))
        )
        fk_b = jnp.where((in_head >= 5) & (in_head < 8), minus, key_mask.astype(bf16))
        inner = grad.astype(f32) * o_in[rows, :].astype(f32)
        for h in (0, 1):
            mine = low_head if h == 0 else ~low_head
            qx[h, rows, :PAIR] = jnp.where(mine, high, zero)
            qx[h, rows, PAIR:] = jnp.where(mine, rest, fq_b)
            kx[h, rows, :PAIR] = k
            kx[h, rows, PAIR:] = jnp.where(mine, k, fk_b)
            qm[h, rows, :] = jnp.where(mine, q, zero)
            km[h, rows, :] = jnp.where(mine, k, zero)
            dx[h, rows, :PAIR] = jnp.where(mine, grad, zero)
            delta = jnp.sum(jnp.where(mine, inner, 0.0), axis=1, keepdims=True)
            da, db, dc = split3(jnp.broadcast_to(delta, (ROW_BLOCK, PAIR)))
            dx[h, rows, PAIR:] = jnp.where(
                lane == 0, da, jnp.where(lane == 1, db, jnp.where(lane == 2, dc, zero))
            )
        vx[rows, :PAIR] = v_in[rows, :]
        vx[rows, PAIR:] = jnp.where(lane < 3, minus, zero)
        dq[rows, :] = jnp.zeros((ROW_BLOCK, PAIR), f32)
        dk[rows, :] = jnp.zeros((ROW_BLOCK, PAIR), f32)
        dv[rows, :] = jnp.zeros((ROW_BLOCK, PAIR), f32)

    for source, at in halves:

        @pl.loop(0, half // ROW_BLOCK)
        def _(b):
            prepare(source, at, b)

    def work(rows, keys):
        grad_q = dq[rows, :]
        grad_k = grad_v = None
        for h in (0, 1):
            scores = lax.dot_general(qx[h, rows, :], kx[h, keys, :], NT, preferred_element_type=f32)
            pulled = lax.dot_general(dx[h, rows, :], vx[keys, :], NT, preferred_element_type=f32)
            probs = jnp.exp2(scores)
            grad_s = (probs * pulled).astype(bf16)
            one_q = jnp.dot(grad_s, km[h, keys, :], preferred_element_type=f32)
            one_v = lax.dot_general(probs.astype(bf16), dx[h, rows, :PAIR], TN, preferred_element_type=f32)
            one_k = lax.dot_general(grad_s, qm[h, rows, :], TN, preferred_element_type=f32)
            grad_q = grad_q + one_q
            grad_v = one_v if h == 0 else grad_v + one_v
            grad_k = one_k if h == 0 else grad_k + one_k
        dq[rows, :] = grad_q
        dv[keys, :] = dv[keys, :] + grad_v
        dk[keys, :] = dk[keys, :] + grad_k

    each_key_chunk(starts, live, length, BWD_BQ, BWD_STEP, BWD_CHUNK, work)

    @pl.loop(0, length // ROW_BLOCK)
    def _(b):
        rows = pl.ds(pl.multiple_of(b * ROW_BLOCK, ROW_BLOCK), ROW_BLOCK)
        cos, sin = rotary_block(table, turns, b)
        u = dq[rows, :] * SCORE_SCALE
        dqkv[rows, :PAIR] = (u * cos - half_swap(u, in_first) * sin).astype(bf16)
        u = dk[rows, :] * SCORE_SCALE
        dqkv[rows, PAIR : 2 * PAIR] = (u * cos - half_swap(u, in_first) * sin).astype(bf16)
        dqkv[rows, 2 * PAIR :] = dv[rows, :].astype(bf16)

    for m in range(width // ROW_BLOCK):
        part = slice(m * ROW_BLOCK, (m + 1) * ROW_BLOCK)
        grads[part, : 3 * PAIR] = lax.dot_general(
            a1[:, part], dqkv[...], TN, preferred_element_type=f32
        ).astype(bf16)
        total = None
        for source, at in halves:
            rows = pl.ds(pl.multiple_of(at * half, half), half)
            term = lax.dot_general(source[:, part], o_in[rows, :], TN, preferred_element_type=f32)
            total = term if total is None else total + term
        grads[part, 3 * PAIR :] = total.astype(bf16)
    made = [*before, grads]
    cols = grads.shape[1]
    stores = []
    for n, one in enumerate(made):
        at = slice(n * cols, (n + 1) * cols)
        if part_count == 1:
            stores.append(pltpu.make_async_copy(one, parts[0].at[:, at], sems.at[n, 0]))
            continue
        rows_each = parts[0].shape[1]
        for h in range(parts[0].shape[0]):
            for j in range(part_count):
                own = jnp.bitwise_xor(me, h * part_count + j)
                stores.append(
                    pltpu.make_async_copy(
                        one.at[pl.ds(pl.multiple_of(own * rows_each, 16), rows_each)],
                        parts[j].at[h, :, at],
                        sems.at[n, h * part_count + j],
                    )
                )
    for copy in stores:
        copy.start()
    for copy in stores:
        copy.wait()


def backward_pair(scal, a1, near, far, w, saved, tables, part_shapes, before=(), deps=()):
    length, width = a1.shape
    shape = jax.ShapeDtypeStruct
    outs = [shape((length, 3 * PAIR), bf16)] + [shape(s, bf16) for s in part_shapes]
    return pl.pallas_call(
        passing(functools.partial(backward_kernel, len(part_shapes), len(before)), 12 + len(before), len(deps)),
        out_shape=tuple(outs),
        in_specs=[smem()] + [vmem()] * 11 + [anywhere()] * (len(before) + len(deps)),
        out_specs=(vmem(),) + (anywhere(),) * len(part_shapes),
        scratch_shapes=[
            pltpu.VMEM((2, length, 2 * PAIR), bf16),
            pltpu.VMEM((2, length, 2 * PAIR), bf16),
            pltpu.VMEM((2, length, 2 * PAIR), bf16),
            pltpu.VMEM((length, 2 * PAIR), bf16),
            pltpu.VMEM((2, length, PAIR), bf16),
            pltpu.VMEM((2, length, PAIR), bf16),
            pltpu.VMEM((length, PAIR), f32),
            pltpu.VMEM((length, PAIR), f32),
            pltpu.VMEM((length, PAIR), f32),
            pltpu.VMEM((width, 4 * PAIR), bf16),
            pltpu.SemaphoreType.DMA((len(before) + 1, 16)),
        ],
        compiler_params=params(BWD_MIB),
        cost_estimate=lasts(30),
        name="attention_backward",
    )(scal, a1, near, far, w, *saved, *tables, *before, *deps)


def project_kernel(count, scal, *refs):
    rows, weights, out = refs[:count], refs[count : 2 * count], refs[2 * count]
    total = None
    for one, w in zip(rows, weights):
        term = lax.dot_general(one[...], w[...], NT, preferred_element_type=f32)
        total = term if total is None else total + term
    out[...] = total.astype(out.dtype)


def columns_of(weight, at, cols):
    return pl.BlockSpec((weight.shape[0], cols), lambda b, s: (0, at // cols))


def project_far_half(scal, rows, weights, deps=()):
    length, cols = rows[0].shape
    width = weights[0][0].shape[0]
    blocks = length // 2 // ROW_BLOCK
    count = len(rows)
    return pl.pallas_call(
        passing(functools.partial(project_kernel, count), 1 + 2 * count, len(deps)),
        out_shape=jax.ShapeDtypeStruct((length // 2, width), bf16),
        grid_spec=pltpu.PrefetchScalarGridSpec(
            num_scalar_prefetch=1,
            grid=(blocks,),
            in_specs=[pl.BlockSpec((ROW_BLOCK, cols), lambda b, s: (b + (1 - s[2]) * blocks, 0))] * count
            + [columns_of(w, at, cols) for w, at in weights]
            + [anywhere()] * len(deps),
            out_specs=pl.BlockSpec((ROW_BLOCK, width), lambda b, s: (b, 0)),
        ),
        compiler_params=params(),
        cost_estimate=lasts(4),
        name="project_far_half",
    )(scal, *rows, *[w for w, _ in weights], *deps)


def final_kernel(count, scal, *refs):
    rows, weights = refs[:count], refs[count : 2 * count]
    tokens, far, grad_hidden, gains, out = refs[2 * count :]
    total = far[...].astype(f32)
    for one, w in zip(rows, weights):
        total = total + lax.dot_general(one[...], w[...], NT, preferred_element_type=f32)
    normed, inv = norm_stats(tokens[...].astype(f32))
    out[...] = grad_hidden[...] + norm_back(total * gains[0:1, :], normed, inv)


def final_rows(scal, rows, weights, tokens, far, grad_hidden, gains, deps=()):
    length, cols = rows[0].shape
    width = tokens.shape[1]
    blocks = length // 2 // ROW_BLOCK
    whole = lambda a: pl.BlockSpec(a.shape, lambda b, s: (0, 0))
    near = lambda a: pl.BlockSpec((ROW_BLOCK, a.shape[1]), lambda b, s: (b + s[2] * blocks, 0))
    plain = pl.BlockSpec((ROW_BLOCK, width), lambda b, s: (b, 0))
    return pl.pallas_call(
        passing(functools.partial(final_kernel, len(rows)), 5 + 2 * len(rows), len(deps)),
        out_shape=jax.ShapeDtypeStruct((length // 2, width), f32),
        grid_spec=pltpu.PrefetchScalarGridSpec(
            num_scalar_prefetch=1,
            grid=(blocks,),
            in_specs=[near(r) for r in rows]
            + [columns_of(w, at, cols) for w, at in weights]
            + [near(tokens), plain, plain, whole(gains)]
            + [anywhere()] * len(deps),
            out_specs=plain,
        ),
        compiler_params=params(),
        cost_estimate=lasts(7),
        name="final_rows",
    )(scal, *rows, *[w for w, _ in weights], tokens, far, grad_hidden, gains, *deps)


def finish_kernel(sizes, *refs):
    groups, at = [], 0
    for size in sizes:
        groups.append(refs[at : at + size])
        at += size
    w_qkv, grad_qkv, grad_out, partial = refs[at:]
    pair = 0
    inner = None
    for group in groups:
        total = group[0][...]
        for one in group[1:]:
            total = total + one[...].astype(f32)
        for i in range(total.shape[1] // (4 * PAIR)):
            cols = slice(pair * PAIR, (pair + 1) * PAIR)
            for c in range(3):
                grad = total[:, (4 * i + c) * PAIR : (4 * i + c + 1) * PAIR]
                grad_qkv[c, :, cols] = grad
                term = grad * w_qkv[c, :, cols].astype(f32)
                inner = term if inner is None else inner + term
            grad_out[:, cols] = total[:, (4 * i + 3) * PAIR : (4 * i + 4) * PAIR]
            pair += 1
    partial[...] = jnp.broadcast_to(jnp.sum(inner, axis=1, keepdims=True), partial.shape)


def finish(groups, w_qkv, deps):
    rows, cols = w_qkv.shape[1:]
    shape = jax.ShapeDtypeStruct
    sizes = [len(g) for g in groups]
    flat = [x for g in groups for x in g]
    return pl.pallas_call(
        passing(functools.partial(finish_kernel, sizes), len(flat) + 1, len(deps)),
        out_shape=(shape((3, rows, cols), f32), shape((rows, cols), f32), shape((rows, PAIR), f32)),
        in_specs=[vmem()] * (len(flat) + 1) + [anywhere()] * len(deps),
        out_specs=(vmem(),) * 3,
        compiler_params=params(),
        cost_estimate=lasts(2),
        name="finish",
    )(*flat, w_qkv, *deps)


def ffn_kernel(count, scal, *refs):
    outs_of, weights = refs[:count], refs[count : 2 * count]
    tokens, far, cot, gains, ffn_w = refs[2 * count : 2 * count + 5]
    result, dattn, grad_hidden, z_all, pair_all, a2_all, dff_all = refs[2 * count + 5 :]
    width, ff = ffn_w.shape[1:]
    live, me, core = scal[0], scal[1], scal[2]
    step = pl.program_id(0)
    block = result.shape[0]

    here = core * (block * pl.num_programs(0)) + step * block
    position = here + lax.broadcasted_iota(jnp.int32, (block, 1), 0)
    valid = (position < live).astype(f32)
    attn = far[...].astype(f32)
    for one, w in zip(outs_of, weights):
        attn = attn + lax.dot_general(one[...], w[...], NT, preferred_element_type=f32)
    hidden = tokens[...].astype(f32) + valid * attn
    normed, inv = norm_stats(hidden)
    gain = gains[8:9, :]
    a2 = (normed * gain).astype(bf16)
    up = jnp.dot(a2, ffn_w[0], preferred_element_type=f32)
    gate = jnp.dot(a2, ffn_w[1], preferred_element_type=f32)
    below = 0.5 * (1.0 + lax.erf(up * math.sqrt(0.5)))
    act = up * below
    slope = below + up * jnp.exp(up * up * -0.5) * (1.0 / math.sqrt(2.0 * math.pi))
    z = (act * gate).astype(bf16)
    result[...] = (
        hidden + valid * lax.dot_general(z, ffn_w[2], NT, preferred_element_type=f32)
    ).astype(bf16)
    dy = cot[...].astype(f32)
    dff = (valid * dy).astype(bf16)
    dz = jnp.dot(dff, ffn_w[2], preferred_element_type=f32)
    du = (dz * gate * slope).astype(bf16)
    dg = (dz * act).astype(bf16)
    da2 = lax.dot_general(du, ffn_w[0], NT, preferred_element_type=f32) + lax.dot_general(
        dg, ffn_w[1], NT, preferred_element_type=f32
    )
    grad = dy + norm_back(da2 * gain, normed, inv)
    grad_hidden[...] = grad
    dattn[...] = (valid * grad).astype(bf16)
    z_all[...] = z
    pair_all[0] = du
    pair_all[1] = dg
    a2_all[...] = a2
    dff_all[...] = dff


def weight_grad_kernel(split, own, down_cols, scal, z, pair, a2, dff, *outs):
    width, ff = a2.shape[1], z.shape[1]
    core = scal[2]
    for m in range(width // ROW_BLOCK):
        part = slice(m * ROW_BLOCK, (m + 1) * ROW_BLOCK)
        left, down = a2[:, part], dff[:, part]
        if split:
            who = core if own else 1 - core
            at = pl.multiple_of(who * (ff - down_cols), PAIR)
            outs[0][part, :ff] = lax.dot_general(left, pair[who], TN, preferred_element_type=f32).astype(bf16)
            outs[0][part, ff:] = lax.dot_general(
                down, z[:, pl.ds(at, down_cols)], TN, preferred_element_type=f32
            ).astype(bf16)
        else:
            for i in (0, 1):
                outs[0][i, part, :] = lax.dot_general(
                    left, pair[i], TN, preferred_element_type=f32
                ).astype(bf16)
            outs[1][part, :] = lax.dot_general(down, z[...], TN, preferred_element_type=f32).astype(bf16)


def weight_grads(split, own, down_cols, scal, z, pair, a2, dff, deps=()):
    width, ff = a2.shape[1], z.shape[1]
    shape = jax.ShapeDtypeStruct
    if split:
        outs = (shape((width, ff + down_cols), bf16),)
    else:
        outs = (shape((2, width, ff), bf16), shape((width, ff), bf16))
    return pl.pallas_call(
        passing(functools.partial(weight_grad_kernel, split, own, down_cols), 5, len(deps)),
        out_shape=outs,
        in_specs=[smem()] + [vmem()] * 4 + [anywhere()] * len(deps),
        out_specs=(vmem(),) * len(outs),
        compiler_params=params(10 if split else 32),
        cost_estimate=lasts(5),
        name="weight_grads",
    )(scal, z, pair, a2, dff, *deps)


def feed_forward(scal, outs_of, weights, tokens, far, cot, gains, ffn_w):
    length = tokens.shape[0]
    width, ff = ffn_w.shape[1:]
    half = length // 2
    blocks = half // ROW_BLOCK
    shape = jax.ShapeDtypeStruct
    whole = lambda a: pl.BlockSpec(a.shape, lambda b, s: (0,) * len(a.shape))
    near = lambda a: pl.BlockSpec((ROW_BLOCK, a.shape[1]), lambda b, s: (b + s[2] * blocks, 0))
    plain = lambda cols: pl.BlockSpec((ROW_BLOCK, cols), lambda b, s: (b, 0))
    return pl.pallas_call(
        functools.partial(ffn_kernel, len(outs_of)),
        out_shape=(
            shape((half, width), bf16),
            shape((half, width), bf16),
            shape((half, width), f32),
            shape((half, ff), bf16),
            shape((2, half, ff), bf16),
            shape((half, width), bf16),
            shape((half, width), bf16),
        ),
        grid_spec=pltpu.PrefetchScalarGridSpec(
            num_scalar_prefetch=1,
            grid=(blocks,),
            in_specs=[near(o) for o in outs_of]
            + [columns_of(w, at, PAIR) for w, at in weights]
            + [near(tokens), plain(width), plain(width), whole(gains)]
            + [vmem()],
            out_specs=(
                plain(width),
                plain(width),
                plain(width),
                plain(ff),
                pl.BlockSpec((2, ROW_BLOCK, ff), lambda b, s: (0, b, 0)),
                plain(width),
                plain(width),
            ),
        ),
        compiler_params=params(FFN_MIB),
        cost_estimate=lasts(25),
        name="feed_forward",
    )(scal, *outs_of, *[w for w, _ in weights], tokens, far, cot, gains, ffn_w)


def pack_kernel(wide, scal, keep, got, *outs):
    me = scal[1]
    for j in range(wide):
        for h in range(outs[0].shape[0]):
            own = jnp.bitwise_xor(me, h * wide + j)
            outs[j][h] = (keep[own].astype(f32) + got[own].astype(f32)).astype(bf16)


def pack_parts(scal, keep, got, count, deps=()):
    width, cols = keep.shape
    rows = width // count
    wide = 1 << bit_groups(count)[-1][1]
    shape = jax.ShapeDtypeStruct((count // wide, rows, cols), bf16)
    return pl.pallas_call(
        passing(functools.partial(pack_kernel, wide), 3, len(deps)),
        out_shape=(shape,) * wide,
        in_specs=[smem(), vmem(), vmem()] + [anywhere()] * len(deps),
        out_specs=(vmem(),) * wide,
        compiler_params=params(),
        cost_estimate=lasts(4),
        name="pack_parts",
    )(scal, keep.reshape(count, rows, cols), got.reshape(count, rows, cols), *deps)


def rotary_tables(length):
    freqs = ROPE_THETA ** (-np.arange(0, HEAD_DIM, 2) / HEAD_DIM)
    freqs = np.tile(np.float32(freqs).astype(np.float64), 4)
    sign = np.where(np.arange(PAIR) % HEAD_DIM < HEAD_DIM // 2, -1.0, 1.0)

    def both(positions):
        angles = positions[:, None] * freqs[None, :]
        return jnp.asarray(np.stack([np.cos(angles), np.sin(angles) * sign]), f32)

    return both(np.arange(ROW_BLOCK)), both(np.arange(0, length, ROW_BLOCK))


def local(tokens, segment_ids, counts, w_qkv, w_out, w_in, w_down, ln1_gain, ln2_gain, cotangent):
    count = lax.axis_size("dp")
    dp, core = lax.axis_index("dp"), lax.axis_index("head")
    length, width = tokens.shape[1:]
    ff = w_in.shape[2]
    rows_each = width // count
    fast = rows_each % 16 == 0 and count & (count - 1) == 0 and len(bit_groups(count)) == 2
    pairs = w_qkv.shape[2] // PAIR
    first_core = core == 0
    pick = lambda a, b: jnp.where(first_core, a, b)
    join = lambda mine, other: jnp.concatenate([pick(mine, other), pick(other, mine)], axis=0)
    row, cot = tokens[0], cotangent[0]
    seg = segment_ids[0]
    live = counts[0]
    begins = jnp.sum(seg[None, :] < jnp.arange(1, 4)[:, None], axis=1)
    scal = jnp.concatenate([jnp.stack([live, dp, core]), begins]).astype(jnp.int32)

    both = jnp.stack([ln1_gain, ln2_gain], axis=1)
    head_load, rest_load = attention_loads(core.astype(jnp.int32)[None], w_qkv, w_out.T, both, core_swap(both))
    down_turned = w_down.T
    down_cols = -(-(ff // 2) // 128) * 128
    offset = ff - down_cols
    tables = rotary_tables(length)
    out_at = 3 * PAIR * (pairs - 1)
    everyone = ("dp", "head")
    ffn_w = lax.all_gather(jnp.concatenate([w_in, down_turned[None]]), everyone, axis=1, tiled=True)

    if fast:
        high_bits, low_bits = bit_groups(count)
        head_high = gather_step(head_load[None], count, high_bits)
        rest_load = stack_parts([rest_load[None]], head_high[1:])
        head_parts = gather_step(stack_parts(head_high), count, low_bits)
        rest_high = gather_step(rest_load, count, high_bits)
        rest_all = stack_parts(rest_high, head_parts[1:])
        a1, gains, *kept = forward_pair(
            True, scal, row, tables, head_parts, 0, [rest_all]
        )
        rest_parts = gather_step(rest_all, count, low_bits)
    else:
        head_parts = [lax.all_gather(head_load, "dp", axis=0, tiled=True)]
        rest_parts = [lax.all_gather(rest_load, "dp", axis=0, tiled=True)]
        a1, gains, *kept = forward_pair(True, scal, row, tables, head_parts, 0)

    head_w, saved = kept[0], [kept[1:]]
    rest_w, *kept = forward_pair(False, scal, a1, tables, rest_parts, 0)
    saved.append(kept)
    for i in range(2, pairs):
        saved.append(forward_pair(False, scal, a1, tables, rest_w, 3 * PAIR * (i - 1)))
    qkv_w = [(head_w, 0)] + [(rest_w, 3 * PAIR * (i - 1)) for i in range(1, pairs)]
    out_w = [(rest_w, out_at + i * PAIR) for i in range(pairs)]
    outs_of = [s[3] for s in saved]

    far = core_swap(project_far_half(scal, outs_of, out_w))
    result, near_grad, grad_hidden, *kept = feed_forward(scal, outs_of, out_w, row, far, cot, gains, ffn_w)
    far_grad = core_swap(near_grad)

    def backward(i, part_shapes, before=(), deps=()):
        q, k, v, o, lse = saved[i]
        w, at = out_w[i]
        w = w[:, at : at + PAIR]
        return backward_pair(
            scal, a1, near_grad, far_grad, w, (q, k, v, o, lse), tables, part_shapes, before, deps
        )

    if fast:
        wide = 1 << low_bits[1]
        parts_of = lambda n: [(count // wide, rows_each, n * 4 * PAIR)] * wide
        got = core_swap(weight_grads(True, False, down_cols, scal, *kept)[0])
        keep = weight_grads(True, True, down_cols, scal, *kept)[0]
        deps = pack_parts(scal, keep, got, count)
        ffn_near = reduce_near(deps, count)
        dqkv, before = [], []
        pieces = None
        for i in range(pairs - 1):
            last = i == pairs - 2
            one, *parts = backward(
                i, parts_of(pairs - 1) if last else [(width, 4 * PAIR)], before if last else [], deps
            )
            dqkv.append(one)
            before += parts
            if i == 0:
                pieces = sum_parts(ffn_near, [one])
                deps = pieces
        done = reduce_far(pieces, count, wide)
        early_near = reduce_near(parts, count)
        one, *parts = backward(pairs - 1, parts_of(1), (), [done])
        dqkv.append(one)
        late_near = reduce_near(parts, count)
        pieces = sum_parts(early_near, [one])
        early = far_pieces(pieces, count, wide)
        far_da = project_far_half(scal, dqkv, qkv_w, pieces)
        pieces = sum_parts(late_near, [far_da])
        shards = [early, far_pieces(pieces, count, wide)]
        far_da = core_swap(far_da)
        grad_tokens = final_rows(scal, dqkv, qkv_w, row, far_da, grad_hidden, gains, pieces)
        rows_here = w_in.shape[1]
        low, high = done[:rows_here], done[rows_here:]
        mine = pick(low, high)
        other = core_swap(pick(high, low))
        grad_w_in = jnp.stack(
            [pick(mine[:, :ff], other[:, :ff]), pick(other[:, :ff], mine[:, :ff])]
        )
        grad_down = jnp.concatenate(
            [pick(mine[:, ff:], other[:, ff:]), pick(other[:, ff:], mine[:, ff:])[:, down_cols - offset :]],
            axis=1,
        ).T
    else:
        keep, send = weight_grads(False, True, down_cols, scal, *kept)
        grad_w_in = lax.psum_scatter(keep.astype(f32), everyone, scatter_dimension=1, tiled=True)
        grad_down = lax.psum_scatter(send.astype(f32), everyone, scatter_dimension=0, tiled=True).T
        dqkv, shards = [], []
        for i in range(pairs):
            one, parts = backward(i, [(width, 4 * PAIR)])
            dqkv.append(one)
            shards.append([lax.psum_scatter(parts.astype(f32), "dp", scatter_dimension=0, tiled=True)])
        far_da = core_swap(project_far_half(scal, dqkv, qkv_w))
        grad_tokens = final_rows(scal, dqkv, qkv_w, row, far_da, grad_hidden, gains)

    grad_two = jnp.sum(grad_w_in * w_in.astype(f32), axis=(0, 2)) / ln2_gain.astype(f32)

    grad_qkv, grad_out, partial = finish(shards, w_qkv, [grad_tokens])
    rows_here = ln1_gain.shape[0]
    partial = partial[:, 0]
    low, high = partial[:rows_here], partial[rows_here:]
    grad_one = (pick(low, high) + core_swap(pick(high, low))) / ln1_gain.astype(f32)
    return (
        result[None],
        grad_tokens[None],
        grad_qkv,
        grad_out.T,
        grad_w_in,
        grad_down,
        grad_one,
        grad_two,
    )


def solution(mesh):
    placed = (
        P("dp", None, None),
        P("dp", None),
        P("dp"),
        P(None, "dp", "head"),
        P("head", "dp"),
        P(None, ("dp", "head"), None),
        P(None, ("dp", "head")),
        P(("dp", "head")),
        P(("dp", "head")),
        P("dp", "head", None),
    )
    return jax.shard_map(
        local,
        mesh=mesh,
        in_specs=placed,
        out_specs=(
            P("dp", "head", None),
            P("dp", "head", None),
            P(None, "dp", "head"),
            P("head", "dp"),
            P(None, ("dp", "head"), None),
            P(None, ("dp", "head")),
            P(("dp", "head")),
            P(("dp", "head")),
        ),
        check_vma=False,
    )
```

```python
import functools
import math

import jax
import jax.numpy as jnp
import numpy as np
from jax import lax
from jax.experimental import pallas as pl
from jax.experimental.pallas import tpu as pltpu
from jax.sharding import PartitionSpec as P

HEAD_DIM = 64
PAIR = 2 * HEAD_DIM
LAYER_EPS = 1e-05
ROPE_THETA = 160000.0
BIG = 1e30
LOG2_SCALE = math.log2(math.e) / math.sqrt(HEAD_DIM)
SCORE_SCALE = 1.0 / math.sqrt(HEAD_DIM)
ROW_BLOCK = 256
FWD_MIB, BWD_MIB, FFN_MIB = 20, 23, 25
FWD_BQ, FWD_STEP = 512, 256
BWD_BQ, BWD_STEP, BWD_CHUNK = 256, 128, 12
NT = (((1,), (1,)), ((), ()))
TN = (((0,), (0,)), ((), ()))
bf16 = jnp.bfloat16
f32 = jnp.float32


def vmem():
    return pl.BlockSpec(memory_space=pltpu.VMEM)


def smem():
    return pl.BlockSpec(memory_space=pltpu.SMEM)


def hbm():
    return pl.BlockSpec(memory_space=pltpu.HBM)


def anywhere():
    return pl.BlockSpec(memory_space=pl.ANY)


def params(mib=10):
    return pltpu.CompilerParams(vmem_limit_bytes=mib << 20)


def lasts(micros):
    return pl.CostEstimate(flops=int(micros * 1e8), bytes_accessed=0, transcendentals=0)


def passing(kernel, inputs, deps):
    def run(*refs):
        kernel(*refs[:inputs], *refs[inputs + deps :])

    return run


def bit_groups(count):
    bits = count.bit_length() - 1
    shifts = []
    low = 0
    while low < bits:
        wide = min(2, bits - low)
        shifts.append((low, wide))
        low += wide
    return shifts[::-1]


def xor_permute(value, count, mask):
    return lax.ppermute(value, "dp", [(i, i ^ mask) for i in range(count)])


def core_swap(value):
    return lax.ppermute(value, "head", [(0, 1), (1, 0)])


def stack_kernel(*refs):
    ins, out = refs[:-1], refs[-1]
    wide = len(ins)
    for j, one in enumerate(ins):
        for h in range(one.shape[0]):
            out[h * wide + j] = one[h]


def stack_parts(parts, deps=()):
    m, rows, cols = parts[0].shape
    return pl.pallas_call(
        passing(stack_kernel, len(parts), len(deps)),
        out_shape=jax.ShapeDtypeStruct((m * len(parts), rows, cols), parts[0].dtype),
        in_specs=[vmem()] * len(parts) + [anywhere()] * len(deps),
        out_specs=vmem(),
        compiler_params=params(),
        cost_estimate=lasts(1),
        name="stack_parts",
    )(*parts, *deps)


def gather_step(current, count, group):
    shift, wide = group
    return [current] + [xor_permute(current, count, j << shift) for j in range(1, 1 << wide)]


def sum_kernel(count, *refs):
    ins, outs = refs[:count], refs[count:]
    for i, out in enumerate(outs):
        total = ins[0][i].astype(f32)
        for one in ins[1:]:
            total = total + one[i].astype(f32)
        out[...] = total.astype(out.dtype)


def sum_parts(arrays, deps=()):
    m, rows, cols = arrays[0].shape
    return pl.pallas_call(
        passing(functools.partial(sum_kernel, len(arrays)), len(arrays), len(deps)),
        out_shape=tuple(
            jax.ShapeDtypeStruct((rows, cols), f32 if i == 0 else bf16) for i in range(m)
        ),
        in_specs=[vmem()] * len(arrays) + [anywhere()] * len(deps),
        out_specs=(vmem(),) * m,
        compiler_params=params(),
        cost_estimate=lasts(2),
        name="sum_parts",
    )(*arrays, *deps)


def reduce_near(parts, count):
    return [parts[0]] + [xor_permute(parts[j], count, j) for j in range(1, len(parts))]


def far_pieces(pieces, count, wide):
    shift = wide.bit_length() - 1
    return [pieces[0]] + [xor_permute(pieces[h], count, h << shift) for h in range(1, len(pieces))]


def reduce_far(pieces, count, wide):
    total, *others = far_pieces(pieces, count, wide)
    for one in others:
        total = total + one.astype(f32)
    return total


def load_kernel(pairs, scal, w_qkv, out_turned, mine, other, head, rest):
    for c in range(3):
        head[:, c * PAIR : (c + 1) * PAIR] = w_qkv[c, :, :PAIR]
        for i in range(1, pairs):
            at = (3 * (i - 1) + c) * PAIR
            rest[:, at : at + PAIR] = w_qkv[c, :, i * PAIR : (i + 1) * PAIR]
    rest[:, 3 * PAIR * (pairs - 1) :] = out_turned[...]
    mine, other = mine[...].astype(f32), other[...].astype(f32)
    first = scal[0] == 0
    gains = jnp.concatenate([jnp.where(first, mine, other), jnp.where(first, other, mine)], axis=0)
    low = lax.broadcasted_iota(jnp.int32, (gains.shape[0], PAIR), 1) < HEAD_DIM
    head[:, 3 * PAIR :] = jnp.where(low, gains[:, 0:1], gains[:, 1:2]).astype(bf16)


def attention_loads(scal, w_qkv, out_turned, mine, other):
    rows, cols = w_qkv.shape[1:]
    pairs = cols // PAIR
    shape = jax.ShapeDtypeStruct
    return pl.pallas_call(
        functools.partial(load_kernel, pairs),
        out_shape=(shape((rows, 4 * PAIR), bf16), shape((rows, 3 * PAIR * (pairs - 1) + cols), bf16)),
        in_specs=[smem()] + [vmem()] * 4,
        out_specs=(vmem(),) * 2,
        compiler_params=params(),
        cost_estimate=lasts(1),
        name="attention_loads",
    )(scal, w_qkv, out_turned, mine, other)


def placed_copies(parts, target, sems, me, rows, cols):
    if len(parts) == 1:
        return [pltpu.make_async_copy(parts[0].at[:, cols], target.at[:, cols], sems.at[0])]
    copies = []
    wide = len(parts)
    for h in range(parts[0].shape[0]):
        for j in range(wide):
            own = jnp.bitwise_xor(me, h * wide + j)
            copies.append(
                pltpu.make_async_copy(
                    parts[j].at[h, :, cols],
                    target.at[pl.ds(pl.multiple_of(own * rows, 16), rows), cols],
                    sems.at[h * wide + j],
                )
            )
    return copies


def document_starts(scal, length):
    return [jnp.int32(0), scal[3], scal[4], scal[5], jnp.int32(length)]


def key_range(starts, live, first, size, length):
    last = jnp.minimum(first + size, live) - 1
    low = jnp.int32(0)
    high = jnp.int32(length)
    for d in (1, 2, 3):
        low = jnp.where(starts[d] <= first, starts[d], low)
    for d in (3, 2, 1):
        high = jnp.where(starts[d] > last, starts[d], high)
    high = jnp.minimum(high, live)
    seen = first < live
    return jnp.where(seen, low, 0), jnp.where(seen, high, 0)


def each_query_block(starts, live, length, size, step, work, empty):
    @pl.loop(0, length // size)
    def _(i):
        first = pl.multiple_of(i * size, size)
        low, high = key_range(starts, live, first, size, length)
        base = low // 16 * 16
        steps = (high - base + step - 1) // step
        base = pl.multiple_of(jnp.maximum(jnp.minimum(base, length - steps * step), 0), 16)
        rows = pl.ds(first, size)
        for w in range(1, length // step + 1):

            @pl.when(steps == w)
            def _():
                work(rows, pl.ds(base, w * step))

        @pl.when(steps <= 0)
        def _():
            empty(rows)


def each_key_chunk(starts, live, length, size, step, most, work):
    @pl.loop(0, length // size)
    def _(i):
        first = pl.multiple_of(i * size, size)
        low, high = key_range(starts, live, first, size, length)
        base = low // 16 * 16
        steps = (high - base + step - 1) // step
        base = jnp.maximum(jnp.minimum(base, length - steps * step), 0)
        rows = pl.ds(first, size)

        @pl.loop(0, (steps + most - 1) // most)
        def _(c):
            at = pl.multiple_of(base + c * (most * step), 16)
            left = jnp.minimum(steps - c * most, most)
            for w in range(1, most + 1):

                @pl.when(left == w)
                def _():
                    work(rows, pl.ds(at, w * step))


def lane_bounds(starts, live, length):
    column = lax.broadcasted_iota(jnp.int32, (1, PAIR), 1) & (HEAD_DIM - 1)
    low = jnp.zeros((1, PAIR), jnp.int32)
    high = jnp.where(column == 4, live, length)
    for d in range(4):
        low = jnp.where(column == d, starts[d], low)
        high = jnp.where(column == d, starts[d + 1], high)
    return column, low, high


def mask_features(bounds, first, size):
    column, low, high = bounds
    position = first + lax.broadcasted_iota(jnp.int32, (size, PAIR), 0)
    inside = (position >= low) & (position < high)
    column = jnp.broadcast_to(column, (size, PAIR))
    query = jnp.where((inside & (column < 4)) | (column == 4), 1.0, 0.0)
    return query, jnp.where(inside, 0.0, -BIG)


def rotary_block(table, turns, block):
    cos, sin = table[0], table[1]
    cos_at, sin_at = turns[0, pl.ds(block, 1), :], turns[1, pl.ds(block, 1), :]
    return cos * cos_at - sin * sin_at, sin * cos_at + cos * sin_at


def norm_stats(values):
    center = values - jnp.mean(values, axis=-1, keepdims=True)
    spread = jnp.mean(center * center, axis=-1, keepdims=True)
    inv = lax.rsqrt(spread + LAYER_EPS)
    return center * inv, inv


def norm_back(grad, normed, inv):
    return inv * (
        grad
        - jnp.mean(grad, axis=-1, keepdims=True)
        - normed * jnp.mean(grad * normed, axis=-1, keepdims=True)
    )


def half_swap(values, in_first):
    return jnp.where(in_first, pltpu.roll(values, PAIR - HEAD_DIM // 2, 1), pltpu.roll(values, HEAD_DIM // 2, 1))


def split3(values):
    a = values.astype(bf16)
    left = values - a.astype(f32)
    b = left.astype(bf16)
    return a, b, (left - b.astype(f32)).astype(bf16)


def forward_kernel(first, part_count, at, *refs):
    scal, src, table, turns = refs[:4]
    parts = refs[4 : 4 + max(part_count, 1)]
    outs = refs[4 + max(part_count, 1) :]
    if first:
        a1, gains = outs[:2]
        outs = outs[2:]
    if part_count:
        w, outs = outs[0], outs[1:]
    else:
        w = parts[0]
    q_out, k_out, v_out, o_out, lse_out, qx, kx, vx, sems = outs
    length, width = src.shape
    live, me = scal[0], scal[1]

    copies, later = [], []
    if part_count:
        soon = 4 * PAIR if first else 3 * PAIR
        copies = placed_copies(parts, w, sems.at[0], me, parts[0].shape[-2], slice(0, soon))
        if w.shape[1] > soon:
            later = placed_copies(parts, w, sems.at[1], me, parts[0].shape[-2], slice(soon, w.shape[1]))
    for copy in copies + later:
        copy.start()
    starts = document_starts(scal, length)
    bounds = lane_bounds(starts, live, length)
    for copy in copies:
        copy.wait()
    if first:
        turned = jnp.transpose(w[:, 3 * PAIR : 4 * PAIR].astype(f32))
        gains[0:8, :] = turned[0:8]
        gains[8:16, :] = turned[HEAD_DIM : HEAD_DIM + 8]
    lane = lax.broadcasted_iota(jnp.int32, (ROW_BLOCK, PAIR), 1)
    low_head = lane < HEAD_DIM
    in_first = (lane & (HEAD_DIM - 1)) < HEAD_DIM // 2
    zero = jnp.zeros((ROW_BLOCK, PAIR), bf16)

    @pl.loop(0, length // ROW_BLOCK)
    def _(b):
        rows = pl.ds(pl.multiple_of(b * ROW_BLOCK, ROW_BLOCK), ROW_BLOCK)
        if first:
            normed, _ = norm_stats(src[rows, :].astype(f32))
            a = (normed * gains[0:1, :]).astype(bf16)
            a1[rows, :] = a
        else:
            a = src[rows, :]
        qkv = jnp.dot(a, w[:, at : at + 3 * PAIR], preferred_element_type=f32)
        cos, sin = rotary_block(table, turns, b)
        query_mask, key_mask = mask_features(bounds, b * ROW_BLOCK, ROW_BLOCK)
        query_mask, key_mask = query_mask.astype(bf16), key_mask.astype(bf16)
        u = qkv[:, :PAIR]
        q = (u * cos + half_swap(u, in_first) * sin).astype(bf16)
        u = qkv[:, PAIR : 2 * PAIR]
        k = (u * cos + half_swap(u, in_first) * sin).astype(bf16)
        v = qkv[:, 2 * PAIR :].astype(bf16)
        q_out[rows, :] = q
        k_out[rows, :] = k
        v_out[rows, :] = v
        scaled = q.astype(f32) * LOG2_SCALE
        high = scaled.astype(bf16)
        rest = (scaled - high.astype(f32)).astype(bf16)
        for h in (0, 1):
            mine = low_head if h == 0 else ~low_head
            qx[h, rows, :PAIR] = jnp.where(mine, high, zero)
            qx[h, rows, PAIR:] = jnp.where(mine, rest, query_mask)
            kx[h, rows, :PAIR] = k
            kx[h, rows, PAIR:] = jnp.where(mine, k, key_mask)
        vx[rows, :PAIR] = v
        vx[rows, PAIR:] = jnp.ones((ROW_BLOCK, PAIR), bf16)

    lane_q = lax.broadcasted_iota(jnp.int32, (FWD_BQ, PAIR), 1) < HEAD_DIM

    def work(rows, keys):
        values = vx[keys, :]
        scores = [
            lax.dot_general(qx[h, rows, :], kx[h, keys, :], NT, preferred_element_type=f32) for h in (0, 1)
        ]
        tops, sums = [], []
        for h in (0, 1):
            top = jnp.max(scores[h], axis=1, keepdims=True)
            probs = jnp.exp2(scores[h] - top).astype(bf16)
            tops.append(top)
            sums.append(jnp.dot(probs, values, preferred_element_type=f32))
        total = jnp.where(lane_q, sums[0][:, PAIR:], sums[1][:, PAIR:])
        out = jnp.where(lane_q, sums[0][:, :PAIR], sums[1][:, :PAIR])
        o_out[rows, :] = (out / total).astype(bf16)
        lse_out[rows, :] = jnp.maximum(jnp.where(lane_q, tops[0], tops[1]) + jnp.log2(total), -1e20)

    def empty(rows):
        o_out[rows, :] = jnp.zeros((FWD_BQ, PAIR), bf16)
        lse_out[rows, :] = jnp.zeros((FWD_BQ, PAIR), f32)

    each_query_block(starts, live, length, FWD_BQ, FWD_STEP, work, empty)
    for copy in later:
        copy.wait()


def forward_pair(first, scal, src, tables, parts, at, deps=()):
    length, width = src.shape
    shape = jax.ShapeDtypeStruct
    outs = [shape((length, PAIR), bf16)] * 4 + [shape((length, PAIR), f32)]
    pieces = isinstance(parts, list)
    operands = parts if pieces else [parts]
    if pieces:
        outs = [shape((width, parts[0].shape[-1]), bf16)] + outs
    if first:
        outs = [shape((length, width), bf16), shape((16, width), f32)] + outs
    kernel = functools.partial(forward_kernel, first, len(parts) if pieces else 0, at)
    return pl.pallas_call(
        passing(kernel, 4 + len(operands), len(deps)),
        out_shape=tuple(outs),
        in_specs=[smem(), vmem(), vmem(), vmem()]
        + [hbm() if pieces else vmem()] * len(operands)
        + [anywhere()] * len(deps),
        out_specs=(vmem(),) * len(outs),
        scratch_shapes=[
            pltpu.VMEM((2, length, 2 * PAIR), bf16),
            pltpu.VMEM((2, length, 2 * PAIR), bf16),
            pltpu.VMEM((length, 2 * PAIR), bf16),
            pltpu.SemaphoreType.DMA((2, 16)),
        ],
        compiler_params=params(FWD_MIB),
        cost_estimate=lasts(18),
        name="attention_forward_first" if first else "attention_forward",
    )(scal, src, *tables, *operands, *deps)


def backward_kernel(part_count, carried, *refs):
    scal, a1, near, far, w, q_in, k_in, v_in, o_in, lse, table, turns = refs[:12]
    before = refs[12 : 12 + carried]
    refs = refs[12 + carried :]
    dqkv, parts = refs[0], refs[1 : 1 + part_count]
    (qx, kx, dx, vx, qm, km, dq, dk, dv, grads, sems) = refs[1 + part_count :]
    length, width = a1.shape
    half = length // 2
    live, me, core = scal[0], scal[1], scal[2]
    starts = document_starts(scal, length)
    bounds = lane_bounds(starts, live, length)
    halves = ((near, core), (far, 1 - core))
    lane = lax.broadcasted_iota(jnp.int32, (ROW_BLOCK, PAIR), 1)
    in_head = lane & (HEAD_DIM - 1)
    low_head = lane < HEAD_DIM
    in_first = in_head < HEAD_DIM // 2
    zero = jnp.zeros((ROW_BLOCK, PAIR), bf16)
    minus = jnp.full((ROW_BLOCK, PAIR), -1, bf16)

    def prepare(source, at, b):
        first = pl.multiple_of(at * half + b * ROW_BLOCK, ROW_BLOCK)
        rows = pl.ds(first, ROW_BLOCK)
        grad = jnp.dot(source[pl.ds(pl.multiple_of(b * ROW_BLOCK, ROW_BLOCK), ROW_BLOCK), :], w[...], preferred_element_type=f32).astype(bf16)
        query_mask, key_mask = mask_features(bounds, first, ROW_BLOCK)
        q, k = q_in[rows, :], k_in[rows, :]
        scaled = q.astype(f32) * LOG2_SCALE
        high = scaled.astype(bf16)
        rest = (scaled - high.astype(f32)).astype(bf16)
        la, lb, lc = split3(pltpu.roll(lse[rows, :], HEAD_DIM, 1))
        fq_b = jnp.where(
            in_head == 5, la, jnp.where(in_head == 6, lb, jnp.where(in_head == 7, lc, query_mask.astype(bf16)))
        )
        fk_b = jnp.where((in_head >= 5) & (in_head < 8), minus, key_mask.astype(bf16))
        inner = grad.astype(f32) * o_in[rows, :].astype(f32)
        for h in (0, 1):
            mine = low_head if h == 0 else ~low_head
            qx[h, rows, :PAIR] = jnp.where(mine, high, zero)
            qx[h, rows, PAIR:] = jnp.where(mine, rest, fq_b)
            kx[h, rows, :PAIR] = k
            kx[h, rows, PAIR:] = jnp.where(mine, k, fk_b)
            qm[h, rows, :] = jnp.where(mine, q, zero)
            km[h, rows, :] = jnp.where(mine, k, zero)
            dx[h, rows, :PAIR] = jnp.where(mine, grad, zero)
            delta = jnp.sum(jnp.where(mine, inner, 0.0), axis=1, keepdims=True)
            da, db, dc = split3(jnp.broadcast_to(delta, (ROW_BLOCK, PAIR)))
            dx[h, rows, PAIR:] = jnp.where(
                lane == 0, da, jnp.where(lane == 1, db, jnp.where(lane == 2, dc, zero))
            )
        vx[rows, :PAIR] = v_in[rows, :]
        vx[rows, PAIR:] = jnp.where(lane < 3, minus, zero)
        dq[rows, :] = jnp.zeros((ROW_BLOCK, PAIR), f32)
        dk[rows, :] = jnp.zeros((ROW_BLOCK, PAIR), f32)
        dv[rows, :] = jnp.zeros((ROW_BLOCK, PAIR), f32)

    for source, at in halves:

        @pl.loop(0, half // ROW_BLOCK)
        def _(b):
            prepare(source, at, b)

    def work(rows, keys):
        grad_q = dq[rows, :]
        grad_k = grad_v = None
        for h in (0, 1):
            scores = lax.dot_general(qx[h, rows, :], kx[h, keys, :], NT, preferred_element_type=f32)
            pulled = lax.dot_general(dx[h, rows, :], vx[keys, :], NT, preferred_element_type=f32)
            probs = jnp.exp2(scores)
            grad_s = (probs * pulled).astype(bf16)
            one_q = jnp.dot(grad_s, km[h, keys, :], preferred_element_type=f32)
            one_v = lax.dot_general(probs.astype(bf16), dx[h, rows, :PAIR], TN, preferred_element_type=f32)
            one_k = lax.dot_general(grad_s, qm[h, rows, :], TN, preferred_element_type=f32)
            grad_q = grad_q + one_q
            grad_v = one_v if h == 0 else grad_v + one_v
            grad_k = one_k if h == 0 else grad_k + one_k
        dq[rows, :] = grad_q
        dv[keys, :] = dv[keys, :] + grad_v
        dk[keys, :] = dk[keys, :] + grad_k

    each_key_chunk(starts, live, length, BWD_BQ, BWD_STEP, BWD_CHUNK, work)

    @pl.loop(0, length // ROW_BLOCK)
    def _(b):
        rows = pl.ds(pl.multiple_of(b * ROW_BLOCK, ROW_BLOCK), ROW_BLOCK)
        cos, sin = rotary_block(table, turns, b)
        u = dq[rows, :] * SCORE_SCALE
        dqkv[rows, :PAIR] = (u * cos - half_swap(u, in_first) * sin).astype(bf16)
        u = dk[rows, :] * SCORE_SCALE
        dqkv[rows, PAIR : 2 * PAIR] = (u * cos - half_swap(u, in_first) * sin).astype(bf16)
        dqkv[rows, 2 * PAIR :] = dv[rows, :].astype(bf16)

    for m in range(width // ROW_BLOCK):
        part = slice(m * ROW_BLOCK, (m + 1) * ROW_BLOCK)
        grads[part, : 3 * PAIR] = lax.dot_general(
            a1[:, part], dqkv[...], TN, preferred_element_type=f32
        ).astype(bf16)
        total = None
        for source, at in halves:
            rows = pl.ds(pl.multiple_of(at * half, half), half)
            term = lax.dot_general(source[:, part], o_in[rows, :], TN, preferred_element_type=f32)
            total = term if total is None else total + term
        grads[part, 3 * PAIR :] = total.astype(bf16)
    made = [*before, grads]
    cols = grads.shape[1]
    stores = []
    for n, one in enumerate(made):
        at = slice(n * cols, (n + 1) * cols)
        if part_count == 1:
            stores.append(pltpu.make_async_copy(one, parts[0].at[:, at], sems.at[n, 0]))
            continue
        rows_each = parts[0].shape[1]
        for h in range(parts[0].shape[0]):
            for j in range(part_count):
                own = jnp.bitwise_xor(me, h * part_count + j)
                stores.append(
                    pltpu.make_async_copy(
                        one.at[pl.ds(pl.multiple_of(own * rows_each, 16), rows_each)],
                        parts[j].at[h, :, at],
                        sems.at[n, h * part_count + j],
                    )
                )
    for copy in stores:
        copy.start()
    for copy in stores:
        copy.wait()


def backward_pair(scal, a1, near, far, w, saved, tables, part_shapes, before=(), deps=()):
    length, width = a1.shape
    shape = jax.ShapeDtypeStruct
    outs = [shape((length, 3 * PAIR), bf16)] + [shape(s, bf16) for s in part_shapes]
    return pl.pallas_call(
        passing(functools.partial(backward_kernel, len(part_shapes), len(before)), 12 + len(before), len(deps)),
        out_shape=tuple(outs),
        in_specs=[smem()] + [vmem()] * 11 + [anywhere()] * (len(before) + len(deps)),
        out_specs=(vmem(),) + (anywhere(),) * len(part_shapes),
        scratch_shapes=[
            pltpu.VMEM((2, length, 2 * PAIR), bf16),
            pltpu.VMEM((2, length, 2 * PAIR), bf16),
            pltpu.VMEM((2, length, 2 * PAIR), bf16),
            pltpu.VMEM((length, 2 * PAIR), bf16),
            pltpu.VMEM((2, length, PAIR), bf16),
            pltpu.VMEM((2, length, PAIR), bf16),
            pltpu.VMEM((length, PAIR), f32),
            pltpu.VMEM((length, PAIR), f32),
            pltpu.VMEM((length, PAIR), f32),
            pltpu.VMEM((width, 4 * PAIR), bf16),
            pltpu.SemaphoreType.DMA((len(before) + 1, 16)),
        ],
        compiler_params=params(BWD_MIB),
        cost_estimate=lasts(30),
        name="attention_backward",
    )(scal, a1, near, far, w, *saved, *tables, *before, *deps)


def project_kernel(count, scal, *refs):
    rows, weights, out = refs[:count], refs[count : 2 * count], refs[2 * count]
    total = None
    for one, w in zip(rows, weights):
        term = lax.dot_general(one[...], w[...], NT, preferred_element_type=f32)
        total = term if total is None else total + term
    out[...] = total.astype(out.dtype)


def columns_of(weight, at, cols):
    return pl.BlockSpec((weight.shape[0], cols), lambda b, s: (0, at // cols))


def project_far_half(scal, rows, weights, deps=()):
    length, cols = rows[0].shape
    width = weights[0][0].shape[0]
    blocks = length // 2 // ROW_BLOCK
    count = len(rows)
    return pl.pallas_call(
        passing(functools.partial(project_kernel, count), 1 + 2 * count, len(deps)),
        out_shape=jax.ShapeDtypeStruct((length // 2, width), bf16),
        grid_spec=pltpu.PrefetchScalarGridSpec(
            num_scalar_prefetch=1,
            grid=(blocks,),
            in_specs=[pl.BlockSpec((ROW_BLOCK, cols), lambda b, s: (b + (1 - s[2]) * blocks, 0))] * count
            + [columns_of(w, at, cols) for w, at in weights]
            + [anywhere()] * len(deps),
            out_specs=pl.BlockSpec((ROW_BLOCK, width), lambda b, s: (b, 0)),
        ),
        compiler_params=params(),
        cost_estimate=lasts(4),
        name="project_far_half",
    )(scal, *rows, *[w for w, _ in weights], *deps)


def final_kernel(count, scal, *refs):
    rows, weights = refs[:count], refs[count : 2 * count]
    tokens, far, grad_hidden, gains, out, mark = refs[2 * count :]
    mark[...] = jnp.zeros(mark.shape, mark.dtype)
    total = far[...].astype(f32)
    for one, w in zip(rows, weights):
        total = total + lax.dot_general(one[...], w[...], NT, preferred_element_type=f32)
    normed, inv = norm_stats(tokens[...].astype(f32))
    out[...] = grad_hidden[...] + norm_back(total * gains[0:1, :], normed, inv)


def final_rows(scal, rows, weights, tokens, far, grad_hidden, gains, deps=()):
    length, cols = rows[0].shape
    width = tokens.shape[1]
    blocks = length // 2 // ROW_BLOCK
    whole = lambda a: pl.BlockSpec(a.shape, lambda b, s: (0, 0))
    near = lambda a: pl.BlockSpec((ROW_BLOCK, a.shape[1]), lambda b, s: (b + s[2] * blocks, 0))
    plain = pl.BlockSpec((ROW_BLOCK, width), lambda b, s: (b, 0))
    return pl.pallas_call(
        passing(functools.partial(final_kernel, len(rows)), 5 + 2 * len(rows), len(deps)),
        out_shape=(jax.ShapeDtypeStruct((length // 2, width), f32), jax.ShapeDtypeStruct((8, PAIR), f32)),
        grid_spec=pltpu.PrefetchScalarGridSpec(
            num_scalar_prefetch=1,
            grid=(blocks,),
            in_specs=[near(r) for r in rows]
            + [columns_of(w, at, cols) for w, at in weights]
            + [near(tokens), plain, plain, whole(gains)]
            + [anywhere()] * len(deps),
            out_specs=(plain, pl.BlockSpec((8, PAIR), lambda b, s: (0, 0))),
        ),
        compiler_params=params(),
        cost_estimate=lasts(7),
        name="final_rows",
    )(scal, *rows, *[w for w, _ in weights], tokens, far, grad_hidden, gains, *deps)


def finish_kernel(sizes, *refs):
    groups, at = [], 0
    for size in sizes:
        groups.append(refs[at : at + size])
        at += size
    w_qkv, grad_qkv, grad_out, partial = refs[at:]
    pair = 0
    inner = None
    for group in groups:
        total = group[0][...]
        for one in group[1:]:
            total = total + one[...].astype(f32)
        for i in range(total.shape[1] // (4 * PAIR)):
            cols = slice(pair * PAIR, (pair + 1) * PAIR)
            for c in range(3):
                grad = total[:, (4 * i + c) * PAIR : (4 * i + c + 1) * PAIR]
                grad_qkv[c, :, cols] = grad
                term = grad * w_qkv[c, :, cols].astype(f32)
                inner = term if inner is None else inner + term
            grad_out[:, cols] = total[:, (4 * i + 3) * PAIR : (4 * i + 4) * PAIR]
            pair += 1
    partial[...] = jnp.broadcast_to(jnp.sum(inner, axis=1, keepdims=True), partial.shape)


def finish(groups, w_qkv, deps):
    rows, cols = w_qkv.shape[1:]
    shape = jax.ShapeDtypeStruct
    sizes = [len(g) for g in groups]
    flat = [x for g in groups for x in g]
    return pl.pallas_call(
        passing(functools.partial(finish_kernel, sizes), len(flat) + 1, len(deps)),
        out_shape=(shape((3, rows, cols), f32), shape((rows, cols), f32), shape((rows, PAIR), f32)),
        in_specs=[vmem()] * (len(flat) + 1) + [anywhere()] * len(deps),
        out_specs=(vmem(),) * 3,
        compiler_params=params(),
        cost_estimate=lasts(2),
        name="finish",
    )(*flat, w_qkv, *deps)


def ffn_kernel(count, part_count, down_cols, scal, *refs):
    outs_of, weights = refs[:count], refs[count : 2 * count]
    tokens, far, cot, gains = refs[2 * count : 2 * count + 4]
    sources = refs[2 * count + 4 : -9]
    result, dattn, grad_hidden, z_all, pair_all, a2_all, dff_all, ffn_w, sems = refs[-9:]
    width, ff = ffn_w.shape[1:]
    live, me, core = scal[0], scal[1], scal[2]
    step = pl.program_id(0)
    block = result.shape[0]

    @pl.when(step == 0)
    def _():
        copies = []
        if part_count == 1:
            copies.append(pltpu.make_async_copy(sources[0], ffn_w.at[pl.ds(0, 2)], sems.at[0]))
            copies.append(pltpu.make_async_copy(sources[1], ffn_w.at[2], sems.at[1]))
        else:
            offset = ff - down_cols
            rows_each = sources[0].shape[1]
            near_at = pl.multiple_of(core * offset, PAIR)
            far_from = pl.multiple_of(ff + (1 - core) * (down_cols - offset), PAIR)
            far_at = pl.multiple_of((1 - core) * down_cols, PAIR)
            for h in range(sources[0].shape[0]):
                for j in range(part_count):
                    own = jnp.bitwise_xor(me, h * part_count + j)
                    at = pl.ds(pl.multiple_of(own * rows_each, 16), rows_each)
                    number = 4 * (h * part_count + j)
                    mine, other = sources[j].at[h], sources[part_count + j].at[h]
                    copies += [
                        pltpu.make_async_copy(mine.at[:, :ff], ffn_w.at[core, at], sems.at[number]),
                        pltpu.make_async_copy(other.at[:, :ff], ffn_w.at[1 - core, at], sems.at[number + 1]),
                        pltpu.make_async_copy(
                            mine.at[:, ff:], ffn_w.at[2, at, pl.ds(near_at, down_cols)], sems.at[number + 2]
                        ),
                        pltpu.make_async_copy(
                            other.at[:, pl.ds(far_from, offset)],
                            ffn_w.at[2, at, pl.ds(far_at, offset)],
                            sems.at[number + 3],
                        ),
                    ]
        for copy in copies:
            copy.start()
        for copy in copies:
            copy.wait()

    here = core * (block * pl.num_programs(0)) + step * block
    position = here + lax.broadcasted_iota(jnp.int32, (block, 1), 0)
    valid = (position < live).astype(f32)
    attn = far[...].astype(f32)
    for one, w in zip(outs_of, weights):
        attn = attn + lax.dot_general(one[...], w[...], NT, preferred_element_type=f32)
    hidden = tokens[...].astype(f32) + valid * attn
    normed, inv = norm_stats(hidden)
    gain = gains[8:9, :]
    a2 = (normed * gain).astype(bf16)
    up = jnp.dot(a2, ffn_w[0], preferred_element_type=f32)
    gate = jnp.dot(a2, ffn_w[1], preferred_element_type=f32)
    below = 0.5 * (1.0 + lax.erf(up * math.sqrt(0.5)))
    act = up * below
    slope = below + up * jnp.exp(up * up * -0.5) * (1.0 / math.sqrt(2.0 * math.pi))
    z = (act * gate).astype(bf16)
    result[...] = (
        hidden + valid * lax.dot_general(z, ffn_w[2], NT, preferred_element_type=f32)
    ).astype(bf16)
    dy = cot[...].astype(f32)
    dff = (valid * dy).astype(bf16)
    dz = jnp.dot(dff, ffn_w[2], preferred_element_type=f32)
    du = (dz * gate * slope).astype(bf16)
    dg = (dz * act).astype(bf16)
    da2 = lax.dot_general(du, ffn_w[0], NT, preferred_element_type=f32) + lax.dot_general(
        dg, ffn_w[1], NT, preferred_element_type=f32
    )
    grad = dy + norm_back(da2 * gain, normed, inv)
    grad_hidden[...] = grad
    dattn[...] = (valid * grad).astype(bf16)
    z_all[...] = z
    pair_all[0] = du
    pair_all[1] = dg
    a2_all[...] = a2
    dff_all[...] = dff


def weight_grad_kernel(split, own, down_cols, scal, z, pair, a2, dff, *outs):
    width, ff = a2.shape[1], z.shape[1]
    core = scal[2]
    for m in range(width // ROW_BLOCK):
        part = slice(m * ROW_BLOCK, (m + 1) * ROW_BLOCK)
        left, down = a2[:, part], dff[:, part]
        if split:
            who = core if own else 1 - core
            at = pl.multiple_of(who * (ff - down_cols), PAIR)
            outs[0][part, :ff] = lax.dot_general(left, pair[who], TN, preferred_element_type=f32).astype(bf16)
            outs[0][part, ff:] = lax.dot_general(
                down, z[:, pl.ds(at, down_cols)], TN, preferred_element_type=f32
            ).astype(bf16)
        else:
            for i in (0, 1):
                outs[0][i, part, :] = lax.dot_general(
                    left, pair[i], TN, preferred_element_type=f32
                ).astype(bf16)
            outs[1][part, :] = lax.dot_general(down, z[...], TN, preferred_element_type=f32).astype(bf16)


def weight_grads(split, own, down_cols, scal, z, pair, a2, dff, deps=()):
    width, ff = a2.shape[1], z.shape[1]
    shape = jax.ShapeDtypeStruct
    if split:
        outs = (shape((width, ff + down_cols), bf16),)
    else:
        outs = (shape((2, width, ff), bf16), shape((width, ff), bf16))
    return pl.pallas_call(
        passing(functools.partial(weight_grad_kernel, split, own, down_cols), 5, len(deps)),
        out_shape=outs,
        in_specs=[smem()] + [vmem()] * 4 + [anywhere()] * len(deps),
        out_specs=(vmem(),) * len(outs),
        compiler_params=params(10 if split else 32),
        cost_estimate=lasts(5),
        name="weight_grads",
    )(scal, z, pair, a2, dff, *deps)


def feed_forward(scal, outs_of, weights, tokens, far, cot, gains, sources, ff, down_cols):
    length, width = tokens.shape
    part_count = len(sources) // 2
    half = length // 2
    blocks = half // ROW_BLOCK
    shape = jax.ShapeDtypeStruct
    whole = lambda a: pl.BlockSpec(a.shape, lambda b, s: (0,) * len(a.shape))
    near = lambda a: pl.BlockSpec((ROW_BLOCK, a.shape[1]), lambda b, s: (b + s[2] * blocks, 0))
    plain = lambda cols: pl.BlockSpec((ROW_BLOCK, cols), lambda b, s: (b, 0))
    return pl.pallas_call(
        functools.partial(ffn_kernel, len(outs_of), part_count, down_cols),
        out_shape=(
            shape((half, width), bf16),
            shape((half, width), bf16),
            shape((half, width), f32),
            shape((half, ff), bf16),
            shape((2, half, ff), bf16),
            shape((half, width), bf16),
            shape((half, width), bf16),
        ),
        grid_spec=pltpu.PrefetchScalarGridSpec(
            num_scalar_prefetch=1,
            grid=(blocks,),
            in_specs=[near(o) for o in outs_of]
            + [columns_of(w, at, PAIR) for w, at in weights]
            + [near(tokens), plain(width), plain(width), whole(gains)]
            + [anywhere()] * len(sources),
            out_specs=(
                plain(width),
                plain(width),
                plain(width),
                plain(ff),
                pl.BlockSpec((2, ROW_BLOCK, ff), lambda b, s: (0, b, 0)),
                plain(width),
                plain(width),
            ),
            scratch_shapes=[pltpu.VMEM((3, width, ff), bf16), pltpu.SemaphoreType.DMA((64,))],
        ),
        compiler_params=params(FFN_MIB),
        cost_estimate=lasts(25),
        name="feed_forward",
    )(scal, *outs_of, *[w for w, _ in weights], tokens, far, cot, gains, *sources)


def pack_kernel(wide, scal, keep, got, *outs):
    me = scal[1]
    for j in range(wide):
        for h in range(outs[0].shape[0]):
            own = jnp.bitwise_xor(me, h * wide + j)
            outs[j][h] = (keep[own].astype(f32) + got[own].astype(f32)).astype(bf16)


def pack_parts(scal, keep, got, count, deps=()):
    width, cols = keep.shape
    rows = width // count
    wide = 1 << bit_groups(count)[-1][1]
    shape = jax.ShapeDtypeStruct((count // wide, rows, cols), bf16)
    return pl.pallas_call(
        passing(functools.partial(pack_kernel, wide), 3, len(deps)),
        out_shape=(shape,) * wide,
        in_specs=[smem(), vmem(), vmem()] + [anywhere()] * len(deps),
        out_specs=(vmem(),) * wide,
        compiler_params=params(),
        cost_estimate=lasts(4),
        name="pack_parts",
    )(scal, keep.reshape(count, rows, cols), got.reshape(count, rows, cols), *deps)


def rotary_tables(length):
    freqs = ROPE_THETA ** (-np.arange(0, HEAD_DIM, 2) / HEAD_DIM)
    freqs = np.tile(np.float32(freqs).astype(np.float64), 4)
    sign = np.where(np.arange(PAIR) % HEAD_DIM < HEAD_DIM // 2, -1.0, 1.0)

    def both(positions):
        angles = positions[:, None] * freqs[None, :]
        return jnp.asarray(np.stack([np.cos(angles), np.sin(angles) * sign]), f32)

    return both(np.arange(ROW_BLOCK)), both(np.arange(0, length, ROW_BLOCK))


def local(tokens, segment_ids, counts, w_qkv, w_out, w_in, w_down, ln1_gain, ln2_gain, cotangent):
    count = lax.axis_size("dp")
    dp, core = lax.axis_index("dp"), lax.axis_index("head")
    length, width = tokens.shape[1:]
    ff = w_in.shape[2]
    rows_each = width // count
    fast = rows_each % 16 == 0 and count & (count - 1) == 0 and len(bit_groups(count)) == 2
    pairs = w_qkv.shape[2] // PAIR
    first_core = core == 0
    pick = lambda a, b: jnp.where(first_core, a, b)
    join = lambda mine, other: jnp.concatenate([pick(mine, other), pick(other, mine)], axis=0)
    row, cot = tokens[0], cotangent[0]
    seg = segment_ids[0]
    live = counts[0]
    begins = jnp.sum(seg[None, :] < jnp.arange(1, 4)[:, None], axis=1)
    scal = jnp.concatenate([jnp.stack([live, dp, core]), begins]).astype(jnp.int32)

    both = jnp.stack([ln1_gain, ln2_gain], axis=1)
    head_load, rest_load = attention_loads(core.astype(jnp.int32)[None], w_qkv, w_out.T, both, core_swap(both))
    down_turned = w_down.T
    down_cols = -(-(ff // 2) // 128) * 128
    offset = ff - down_cols
    tables = rotary_tables(length)
    out_at = 3 * PAIR * (pairs - 1)
    everyone = ("dp", "head")

    if fast:
        high_bits, low_bits = bit_groups(count)
        head_high = gather_step(head_load[None], count, high_bits)
        rest_load = stack_parts([rest_load[None]], head_high[1:])
        head_parts = gather_step(stack_parts(head_high), count, low_bits)
        rest_high = gather_step(rest_load, count, high_bits)
        rest_all = stack_parts(rest_high, head_parts[1:])
        zero_one = jnp.concatenate([w_in[0], down_turned[:, :down_cols]], axis=1)
        one_two = jnp.concatenate([w_in[1], down_turned[:, offset:]], axis=1)
        ffn_load = join(pick(zero_one, one_two), core_swap(pick(one_two, zero_one)))
        ffn_load = stack_parts([ffn_load[None]], rest_high[1:])
        ffn_high = gather_step(ffn_load, count, high_bits)
        a1, gains, *kept = forward_pair(
            True, scal, row, tables, head_parts, 0, [rest_all, ffn_load]
        )
        rest_parts = gather_step(rest_all, count, low_bits)
        ffn_all = stack_parts(ffn_high, [a1])
        ffn_parts = gather_step(ffn_all, count, low_bits)
        sources = ffn_parts + [core_swap(p) for p in ffn_parts]
        deps, late_deps = [ffn_all], ffn_parts[1:]
    else:
        head_parts = [lax.all_gather(head_load, "dp", axis=0, tiled=True)]
        rest_parts = [lax.all_gather(rest_load, "dp", axis=0, tiled=True)]
        sources = [
            lax.all_gather(w_in, everyone, axis=1, tiled=True),
            lax.all_gather(down_turned, everyone, axis=0, tiled=True),
        ]
        a1, gains, *kept = forward_pair(True, scal, row, tables, head_parts, 0)
        deps, late_deps = [], []

    head_w, saved = kept[0], [kept[1:]]
    rest_w, *kept = forward_pair(False, scal, a1, tables, rest_parts, 0, deps)
    saved.append(kept)
    for i in range(2, pairs):
        saved.append(forward_pair(False, scal, a1, tables, rest_w, 3 * PAIR * (i - 1)))
    qkv_w = [(head_w, 0)] + [(rest_w, 3 * PAIR * (i - 1)) for i in range(1, pairs)]
    out_w = [(rest_w, out_at + i * PAIR) for i in range(pairs)]
    outs_of = [s[3] for s in saved]

    far = core_swap(project_far_half(scal, outs_of, out_w, late_deps))
    result, near_grad, grad_hidden, *kept = feed_forward(scal, outs_of, out_w, row, far, cot, gains, sources, ff, down_cols)
    far_grad = core_swap(near_grad)

    def backward(i, part_shapes, before=(), deps=()):
        q, k, v, o, lse = saved[i]
        w, at = out_w[i]
        w = w[:, at : at + PAIR]
        return backward_pair(
            scal, a1, near_grad, far_grad, w, (q, k, v, o, lse), tables, part_shapes, before, deps
        )

    if fast:
        wide = 1 << low_bits[1]
        parts_of = lambda n: [(count // wide, rows_each, n * 4 * PAIR)] * wide
        got = core_swap(weight_grads(True, False, down_cols, scal, *kept)[0])
        keep = weight_grads(True, True, down_cols, scal, *kept)[0]
        deps = pack_parts(scal, keep, got, count)
        ffn_near = reduce_near(deps, count)
        dqkv, before = [], []
        pieces = None
        for i in range(pairs - 1):
            last = i == pairs - 2
            one, *parts = backward(
                i, parts_of(pairs - 1) if last else [(width, 4 * PAIR)], before if last else [], deps
            )
            dqkv.append(one)
            before += parts
            if i == 0:
                pieces = sum_parts(ffn_near, [one])
                deps = pieces
        done = reduce_far(pieces, count, wide)
        early_near = reduce_near(parts, count)
        one, *parts = backward(pairs - 1, parts_of(1), (), [done])
        dqkv.append(one)
        late_near = reduce_near(parts, count)
        pieces = sum_parts(early_near, [one])
        early = far_pieces(pieces, count, wide)
        far_da = project_far_half(scal, dqkv, qkv_w, pieces)
        pieces = sum_parts(late_near, [far_da])
        shards = [early, far_pieces(pieces, count, wide)]
        far_da = core_swap(far_da)
        grad_tokens, mark = final_rows(scal, dqkv, qkv_w, row, far_da, grad_hidden, gains, pieces)
        rows_here = w_in.shape[1]
        low, high = done[:rows_here], done[rows_here:]
        mine = pick(low, high)
        other = core_swap(pick(high, low))
        grad_w_in = jnp.stack(
            [pick(mine[:, :ff], other[:, :ff]), pick(other[:, :ff], mine[:, :ff])]
        )
        grad_down = jnp.concatenate(
            [pick(mine[:, ff:], other[:, ff:]), pick(other[:, ff:], mine[:, ff:])[:, down_cols - offset :]],
            axis=1,
        ).T
    else:
        keep, send = weight_grads(False, True, down_cols, scal, *kept)
        grad_w_in = lax.psum_scatter(keep.astype(f32), everyone, scatter_dimension=1, tiled=True)
        grad_down = lax.psum_scatter(send.astype(f32), everyone, scatter_dimension=0, tiled=True).T
        dqkv, shards = [], []
        for i in range(pairs):
            one, parts = backward(i, [(width, 4 * PAIR)])
            dqkv.append(one)
            shards.append([lax.psum_scatter(parts.astype(f32), "dp", scatter_dimension=0, tiled=True)])
        far_da = core_swap(project_far_half(scal, dqkv, qkv_w))
        grad_tokens, mark = final_rows(scal, dqkv, qkv_w, row, far_da, grad_hidden, gains)

    grad_two = jnp.sum(grad_w_in * w_in.astype(f32), axis=(0, 2)) / ln2_gain.astype(f32)

    grad_qkv, grad_out, partial = finish(shards, w_qkv, [mark])
    rows_here = ln1_gain.shape[0]
    partial = partial[:, 0]
    low, high = partial[:rows_here], partial[rows_here:]
    grad_one = (pick(low, high) + core_swap(pick(high, low))) / ln1_gain.astype(f32)
    return (
        result[None],
        grad_tokens[None],
        grad_qkv,
        grad_out.T,
        grad_w_in,
        grad_down,
        grad_one,
        grad_two,
    )


def solution(mesh):
    placed = (
        P("dp", None, None),
        P("dp", None),
        P("dp"),
        P(None, "dp", "head"),
        P("head", "dp"),
        P(None, ("dp", "head"), None),
        P(None, ("dp", "head")),
        P(("dp", "head")),
        P(("dp", "head")),
        P("dp", "head", None),
    )
    return jax.shard_map(
        local,
        mesh=mesh,
        in_specs=placed,
        out_specs=(
            P("dp", "head", None),
            P("dp", "head", None),
            P(None, "dp", "head"),
            P("head", "dp"),
            P(None, ("dp", "head"), None),
            P(None, ("dp", "head")),
            P(("dp", "head")),
            P(("dp", "head")),
        ),
        check_vma=False,
    )
```

```python
import functools
import math

import jax
import jax.numpy as jnp
import numpy as np
from jax import lax
from jax.experimental import pallas as pl
from jax.experimental.pallas import tpu as pltpu
from jax.sharding import PartitionSpec as P

HEAD_DIM = 64
PAIR = 2 * HEAD_DIM
LAYER_EPS = 1e-05
ROPE_THETA = 160000.0
BIG = 1e30
LOG2_SCALE = math.log2(math.e) / math.sqrt(HEAD_DIM)
SCORE_SCALE = 1.0 / math.sqrt(HEAD_DIM)
ROW_BLOCK = 256
PREP_BLOCK = 512
FWD_MIB, BWD_MIB, FFN_MIB = 20, 23, 25
FWD_BQ, FWD_STEP = 512, 256
BWD_BQ, BWD_STEP, BWD_CHUNK = 256, 128, 12
NT = (((1,), (1,)), ((), ()))
TN = (((0,), (0,)), ((), ()))
bf16 = jnp.bfloat16
f32 = jnp.float32


def vmem():
    return pl.BlockSpec(memory_space=pltpu.VMEM)


def smem():
    return pl.BlockSpec(memory_space=pltpu.SMEM)


def hbm():
    return pl.BlockSpec(memory_space=pltpu.HBM)


def anywhere():
    return pl.BlockSpec(memory_space=pl.ANY)


def params(mib=10):
    return pltpu.CompilerParams(vmem_limit_bytes=mib << 20)


def lasts(micros):
    return pl.CostEstimate(flops=int(micros * 1e8), bytes_accessed=0, transcendentals=0)


def passing(kernel, inputs, deps):
    def run(*refs):
        kernel(*refs[:inputs], *refs[inputs + deps :])

    return run


def bit_groups(count):
    bits = count.bit_length() - 1
    shifts = []
    low = 0
    while low < bits:
        wide = min(2, bits - low)
        shifts.append((low, wide))
        low += wide
    return shifts[::-1]


def xor_permute(value, count, mask):
    return lax.ppermute(value, "dp", [(i, i ^ mask) for i in range(count)])


def core_swap(value):
    return lax.ppermute(value, "head", [(0, 1), (1, 0)])


def stack_kernel(at, *refs):
    ins, out = refs[:-1], refs[-1]
    for j, one in enumerate(ins):
        out[jnp.bitwise_xor(at[0], j) if len(ins) > 1 else 0] = one[0]


def stack_parts(at, parts, deps=()):
    _, rows, cols = parts[0].shape
    return pl.pallas_call(
        passing(stack_kernel, 1 + len(parts), len(deps)),
        out_shape=jax.ShapeDtypeStruct((len(parts), rows, cols), parts[0].dtype),
        in_specs=[smem()] + [vmem()] * len(parts) + [anywhere()] * len(deps),
        out_specs=vmem(),
        compiler_params=params(),
        cost_estimate=lasts(1),
        name="stack_parts",
    )(at, *parts, *deps)


def gather_step(current, count, group):
    shift, wide = group
    return [current] + [xor_permute(current, count, j << shift) for j in range(1, 1 << wide)]


def sum_kernel(count, at, *refs):
    ins, outs = refs[:count], refs[count:]
    for i, out in enumerate(outs):
        entry = jnp.bitwise_xor(at[0], i)
        total = ins[0][entry].astype(f32)
        for one in ins[1:]:
            total = total + one[entry].astype(f32)
        out[...] = total.astype(out.dtype)


def sum_parts(at, arrays, deps=()):
    m, rows, cols = arrays[0].shape
    return pl.pallas_call(
        passing(functools.partial(sum_kernel, len(arrays)), 1 + len(arrays), len(deps)),
        out_shape=tuple(
            jax.ShapeDtypeStruct((rows, cols), f32 if i == 0 else bf16) for i in range(m)
        ),
        in_specs=[smem()] + [vmem()] * len(arrays) + [anywhere()] * len(deps),
        out_specs=(vmem(),) * m,
        compiler_params=params(),
        cost_estimate=lasts(2),
        name="sum_parts",
    )(at, *arrays, *deps)


def reduce_near(parts, count):
    return [parts[0]] + [xor_permute(parts[j], count, j) for j in range(1, len(parts))]


def far_pieces(pieces, count, wide):
    shift = wide.bit_length() - 1
    return [pieces[0]] + [xor_permute(pieces[h], count, h << shift) for h in range(1, len(pieces))]


def reduce_far(pieces, count, wide):
    total, *others = far_pieces(pieces, count, wide)
    for one in others:
        total = total + one.astype(f32)
    return total


def load_kernel(pairs, scal, w_qkv, out_turned, mine, other, head, rest):
    for c in range(3):
        head[:, c * PAIR : (c + 1) * PAIR] = w_qkv[c, :, :PAIR]
        for i in range(1, pairs):
            at = (3 * (i - 1) + c) * PAIR
            rest[:, at : at + PAIR] = w_qkv[c, :, i * PAIR : (i + 1) * PAIR]
    rest[:, 3 * PAIR * (pairs - 1) :] = out_turned[...]
    mine, other = mine[...].astype(f32), other[...].astype(f32)
    first = scal[0] == 0
    gains = jnp.concatenate([jnp.where(first, mine, other), jnp.where(first, other, mine)], axis=0)
    low = lax.broadcasted_iota(jnp.int32, (gains.shape[0], PAIR), 1) < HEAD_DIM
    head[:, 3 * PAIR :] = jnp.where(low, gains[:, 0:1], gains[:, 1:2]).astype(bf16)


def attention_loads(scal, w_qkv, out_turned, mine, other):
    rows, cols = w_qkv.shape[1:]
    pairs = cols // PAIR
    shape = jax.ShapeDtypeStruct
    return pl.pallas_call(
        functools.partial(load_kernel, pairs),
        out_shape=(shape((rows, 4 * PAIR), bf16), shape((rows, 3 * PAIR * (pairs - 1) + cols), bf16)),
        in_specs=[smem()] + [vmem()] * 4,
        out_specs=(vmem(),) * 2,
        compiler_params=params(),
        cost_estimate=lasts(1),
        name="attention_loads",
    )(scal, w_qkv, out_turned, mine, other)


def placed_copies(parts, target, sems, me, cols):
    if len(parts) == 1:
        return [pltpu.make_async_copy(parts[0].at[:, cols], target.at[:, cols], sems.at[0])]
    wide = len(parts)
    copies = []
    for j in range(wide):
        low = jnp.bitwise_xor(me & (wide - 1), j)
        copies.append(
            pltpu.make_async_copy(parts[j].at[:, :, cols], target.at[:, low, :, cols], sems.at[j])
        )
    return copies


def document_starts(scal, length):
    return [jnp.int32(0), scal[3], scal[4], scal[5], jnp.int32(length)]


def key_range(starts, live, first, size, length):
    last = jnp.minimum(first + size, live) - 1
    low = jnp.int32(0)
    high = jnp.int32(length)
    for d in (1, 2, 3):
        low = jnp.where(starts[d] <= first, starts[d], low)
    for d in (3, 2, 1):
        high = jnp.where(starts[d] > last, starts[d], high)
    high = jnp.minimum(high, live)
    seen = first < live
    return jnp.where(seen, low, 0), jnp.where(seen, high, 0)


def each_query_block(starts, live, length, size, step, work, empty):
    @pl.loop(0, length // size)
    def _(i):
        first = pl.multiple_of(i * size, size)
        low, high = key_range(starts, live, first, size, length)
        base = low // 16 * 16
        steps = (high - base + step - 1) // step
        base = pl.multiple_of(jnp.maximum(jnp.minimum(base, length - steps * step), 0), 16)
        rows = pl.ds(first, size)
        for w in range(1, length // step + 1):

            @pl.when(steps == w)
            def _():
                work(rows, pl.ds(base, w * step))

        @pl.when(steps <= 0)
        def _():
            empty(rows)


def each_key_chunk(starts, live, length, size, step, most, work):
    @pl.loop(0, length // size)
    def _(i):
        first = pl.multiple_of(i * size, size)
        low, high = key_range(starts, live, first, size, length)
        base = low // 16 * 16
        steps = (high - base + step - 1) // step
        base = jnp.maximum(jnp.minimum(base, length - steps * step), 0)
        rows = pl.ds(first, size)

        @pl.loop(0, (steps + most - 1) // most)
        def _(c):
            at = pl.multiple_of(base + c * (most * step), 16)
            left = jnp.minimum(steps - c * most, most)
            for w in range(1, most + 1):

                @pl.when(left == w)
                def _():
                    work(rows, pl.ds(at, w * step))


def lane_bounds(starts, live, length):
    column = lax.broadcasted_iota(jnp.int32, (1, PAIR), 1) & (HEAD_DIM - 1)
    low = jnp.zeros((1, PAIR), jnp.int32)
    high = jnp.where(column == 4, live, length)
    for d in range(4):
        low = jnp.where(column == d, starts[d], low)
        high = jnp.where(column == d, starts[d + 1], high)
    return column, low, high


def mask_features(bounds, first, size):
    column, low, high = bounds
    position = first + lax.broadcasted_iota(jnp.int32, (size, PAIR), 0)
    inside = (position >= low) & (position < high)
    column = jnp.broadcast_to(column, (size, PAIR))
    query = jnp.where((inside & (column < 4)) | (column == 4), 1.0, 0.0)
    return query, jnp.where(inside, 0.0, -BIG)


def rotary_block(table, turns, block):
    cos, sin = table[0], table[1]
    cos_at, sin_at = turns[0, pl.ds(block, 1), :], turns[1, pl.ds(block, 1), :]
    return cos * cos_at - sin * sin_at, sin * cos_at + cos * sin_at


def norm_stats(values):
    center = values - jnp.mean(values, axis=-1, keepdims=True)
    spread = jnp.mean(center * center, axis=-1, keepdims=True)
    inv = lax.rsqrt(spread + LAYER_EPS)
    return center * inv, inv


def norm_back(grad, normed, inv):
    return inv * (
        grad
        - jnp.mean(grad, axis=-1, keepdims=True)
        - normed * jnp.mean(grad * normed, axis=-1, keepdims=True)
    )


def half_swap(values, in_first):
    return jnp.where(in_first, pltpu.roll(values, PAIR - HEAD_DIM // 2, 1), pltpu.roll(values, HEAD_DIM // 2, 1))


def split3(values):
    a = values.astype(bf16)
    left = values - a.astype(f32)
    b = left.astype(bf16)
    return a, b, (left - b.astype(f32)).astype(bf16)


def forward_kernel(first, part_count, at, *refs):
    scal, src, table, turns = refs[:4]
    parts = refs[4 : 4 + max(part_count, 1)]
    outs = refs[4 + max(part_count, 1) :]
    if first:
        a1, gains = outs[:2]
        outs = outs[2:]
    if part_count:
        w, outs = outs[0], outs[1:]
    else:
        w = parts[0]
    q_out, k_out, v_out, o_out, lse_out, qx, kx, vx, sems = outs
    length, width = src.shape
    live, me = scal[0], scal[1]

    copies, later = [], []
    if part_count:
        soon = 4 * PAIR if first else 3 * PAIR
        copies = placed_copies(parts, w, sems.at[0], me, slice(0, soon))
        if w.shape[-1] > soon:
            later = placed_copies(parts, w, sems.at[1], me, slice(soon, w.shape[-1]))
        w = w.reshape(width, w.shape[-1])
    for copy in copies + later:
        copy.start()
    starts = document_starts(scal, length)
    bounds = lane_bounds(starts, live, length)
    for copy in copies:
        copy.wait()
    if first:
        turned = jnp.transpose(w[:, 3 * PAIR : 4 * PAIR].astype(f32))
        gains[0:8, :] = turned[0:8]
        gains[8:16, :] = turned[HEAD_DIM : HEAD_DIM + 8]
    lane = lax.broadcasted_iota(jnp.int32, (PREP_BLOCK, PAIR), 1)
    low_head = lane < HEAD_DIM
    in_first = (lane & (HEAD_DIM - 1)) < HEAD_DIM // 2
    zero = jnp.zeros((PREP_BLOCK, PAIR), bf16)

    @pl.loop(0, length // PREP_BLOCK)
    def _(b):
        rows = pl.ds(pl.multiple_of(b * PREP_BLOCK, PREP_BLOCK), PREP_BLOCK)
        if first:
            normed, _ = norm_stats(src[rows, :].astype(f32))
            a = (normed * gains[0:1, :]).astype(bf16)
            a1[rows, :] = a
        else:
            a = src[rows, :]
        qkv = jnp.dot(a, w[:, at : at + 3 * PAIR], preferred_element_type=f32)
        cos, sin = rotary_block(table, turns, b)
        query_mask, key_mask = mask_features(bounds, b * PREP_BLOCK, PREP_BLOCK)
        query_mask, key_mask = query_mask.astype(bf16), key_mask.astype(bf16)
        u = qkv[:, :PAIR]
        q = (u * cos + half_swap(u, in_first) * sin).astype(bf16)
        u = qkv[:, PAIR : 2 * PAIR]
        k = (u * cos + half_swap(u, in_first) * sin).astype(bf16)
        v = qkv[:, 2 * PAIR :].astype(bf16)
        q_out[rows, :] = q
        k_out[rows, :] = k
        v_out[rows, :] = v
        scaled = q.astype(f32) * LOG2_SCALE
        high = scaled.astype(bf16)
        rest = (scaled - high.astype(f32)).astype(bf16)
        for h in (0, 1):
            mine = low_head if h == 0 else ~low_head
            qx[h, rows, :PAIR] = jnp.where(mine, high, zero)
            qx[h, rows, PAIR:] = jnp.where(mine, rest, query_mask)
            kx[h, rows, :PAIR] = k
            kx[h, rows, PAIR:] = jnp.where(mine, k, key_mask)
        vx[rows, :PAIR] = v
        vx[rows, PAIR:] = jnp.ones((PREP_BLOCK, PAIR), bf16)

    lane_q = lax.broadcasted_iota(jnp.int32, (FWD_BQ, PAIR), 1) < HEAD_DIM

    def work(rows, keys):
        values = vx[keys, :]
        scores = [
            lax.dot_general(qx[h, rows, :], kx[h, keys, :], NT, preferred_element_type=f32) for h in (0, 1)
        ]
        tops, sums = [], []
        for h in (0, 1):
            top = jnp.max(scores[h], axis=1, keepdims=True)
            probs = jnp.exp2(scores[h] - top).astype(bf16)
            tops.append(top)
            sums.append(jnp.dot(probs, values, preferred_element_type=f32))
        total = jnp.where(lane_q, sums[0][:, PAIR:], sums[1][:, PAIR:])
        out = jnp.where(lane_q, sums[0][:, :PAIR], sums[1][:, :PAIR])
        o_out[rows, :] = (out / total).astype(bf16)
        lse_out[rows, :] = jnp.maximum(jnp.where(lane_q, tops[0], tops[1]) + jnp.log2(total), -1e20)

    def empty(rows):
        o_out[rows, :] = jnp.zeros((FWD_BQ, PAIR), bf16)
        lse_out[rows, :] = jnp.zeros((FWD_BQ, PAIR), f32)

    each_query_block(starts, live, length, FWD_BQ, FWD_STEP, work, empty)
    for copy in later:
        copy.wait()


def forward_pair(first, scal, src, tables, parts, at, deps=()):
    length, width = src.shape
    shape = jax.ShapeDtypeStruct
    outs = [shape((length, PAIR), bf16)] * 4 + [shape((length, PAIR), f32)]
    pieces = isinstance(parts, list)
    operands = parts if pieces else [parts]
    if pieces:
        placed = (width,) if len(parts) == 1 else (parts[0].shape[0], len(parts), parts[0].shape[1])
        outs = [shape(placed + (parts[0].shape[-1],), bf16)] + outs
    if first:
        outs = [shape((length, width), bf16), shape((16, width), f32)] + outs
    kernel = functools.partial(forward_kernel, first, len(parts) if pieces else 0, at)
    made = pl.pallas_call(
        passing(kernel, 4 + len(operands), len(deps)),
        out_shape=tuple(outs),
        in_specs=[smem(), vmem(), vmem(), vmem()]
        + [hbm() if pieces else vmem()] * len(operands)
        + [anywhere()] * len(deps),
        out_specs=(vmem(),) * len(outs),
        scratch_shapes=[
            pltpu.VMEM((2, length, 2 * PAIR), bf16),
            pltpu.VMEM((2, length, 2 * PAIR), bf16),
            pltpu.VMEM((length, 2 * PAIR), bf16),
            pltpu.SemaphoreType.DMA((2, 4)),
        ],
        compiler_params=params(FWD_MIB),
        cost_estimate=lasts(18),
        name="attention_forward_first" if first else "attention_forward",
    )(scal, src, *tables, *operands, *deps)
    made = list(made)
    if pieces:
        number = 2 if first else 0
        made[number] = made[number].reshape(width, -1)
    return made


def backward_kernel(part_count, carried, *refs):
    scal, a1, near, far, w, q_in, k_in, v_in, o_in, lse, table, turns = refs[:12]
    before = refs[12 : 12 + carried]
    refs = refs[12 + carried :]
    dqkv, parts = refs[0], refs[1 : 1 + part_count]
    (qx, kx, dx, vx, qm, km, dq, dk, dv, grads, sems) = refs[1 + part_count :]
    length, width = a1.shape
    half = length // 2
    live, me, core = scal[0], scal[1], scal[2]
    starts = document_starts(scal, length)
    bounds = lane_bounds(starts, live, length)
    halves = ((near, core), (far, 1 - core))
    lane = lax.broadcasted_iota(jnp.int32, (PREP_BLOCK, PAIR), 1)
    in_head = lane & (HEAD_DIM - 1)
    low_head = lane < HEAD_DIM
    in_first = in_head < HEAD_DIM // 2
    zero = jnp.zeros((PREP_BLOCK, PAIR), bf16)
    minus = jnp.full((PREP_BLOCK, PAIR), -1, bf16)

    def prepare(source, at, b):
        first = pl.multiple_of(at * half + b * PREP_BLOCK, PREP_BLOCK)
        rows = pl.ds(first, PREP_BLOCK)
        grad = jnp.dot(source[pl.ds(pl.multiple_of(b * PREP_BLOCK, PREP_BLOCK), PREP_BLOCK), :], w[...], preferred_element_type=f32).astype(bf16)
        query_mask, key_mask = mask_features(bounds, first, PREP_BLOCK)
        q, k = q_in[rows, :], k_in[rows, :]
        scaled = q.astype(f32) * LOG2_SCALE
        high = scaled.astype(bf16)
        rest = (scaled - high.astype(f32)).astype(bf16)
        la, lb, lc = split3(pltpu.roll(lse[rows, :], HEAD_DIM, 1))
        fq_b = jnp.where(
            in_head == 5, la, jnp.where(in_head == 6, lb, jnp.where(in_head == 7, lc, query_mask.astype(bf16)))
        )
        fk_b = jnp.where((in_head >= 5) & (in_head < 8), minus, key_mask.astype(bf16))
        inner = grad.astype(f32) * o_in[rows, :].astype(f32)
        for h in (0, 1):
            mine = low_head if h == 0 else ~low_head
            qx[h, rows, :PAIR] = jnp.where(mine, high, zero)
            qx[h, rows, PAIR:] = jnp.where(mine, rest, fq_b)
            kx[h, rows, :PAIR] = k
            kx[h, rows, PAIR:] = jnp.where(mine, k, fk_b)
            qm[h, rows, :] = jnp.where(mine, q, zero)
            km[h, rows, :] = jnp.where(mine, k, zero)
            dx[h, rows, :PAIR] = jnp.where(mine, grad, zero)
            delta = jnp.sum(jnp.where(mine, inner, 0.0), axis=1, keepdims=True)
            da, db, dc = split3(jnp.broadcast_to(delta, (PREP_BLOCK, PAIR)))
            dx[h, rows, PAIR:] = jnp.where(
                lane == 0, da, jnp.where(lane == 1, db, jnp.where(lane == 2, dc, zero))
            )
        vx[rows, :PAIR] = v_in[rows, :]
        vx[rows, PAIR:] = jnp.where(lane < 3, minus, zero)
        dq[rows, :] = jnp.zeros((PREP_BLOCK, PAIR), f32)
        dk[rows, :] = jnp.zeros((PREP_BLOCK, PAIR), f32)
        dv[rows, :] = jnp.zeros((PREP_BLOCK, PAIR), f32)

    for source, at in halves:

        @pl.loop(0, half // PREP_BLOCK)
        def _(b):
            prepare(source, at, b)

    def work(rows, keys):
        grad_q = dq[rows, :]
        grad_k = grad_v = None
        for h in (0, 1):
            scores = lax.dot_general(qx[h, rows, :], kx[h, keys, :], NT, preferred_element_type=f32)
            pulled = lax.dot_general(dx[h, rows, :], vx[keys, :], NT, preferred_element_type=f32)
            probs = jnp.exp2(scores)
            grad_s = (probs * pulled).astype(bf16)
            one_q = jnp.dot(grad_s, km[h, keys, :], preferred_element_type=f32)
            one_v = lax.dot_general(probs.astype(bf16), dx[h, rows, :PAIR], TN, preferred_element_type=f32)
            one_k = lax.dot_general(grad_s, qm[h, rows, :], TN, preferred_element_type=f32)
            grad_q = grad_q + one_q
            grad_v = one_v if h == 0 else grad_v + one_v
            grad_k = one_k if h == 0 else grad_k + one_k
        dq[rows, :] = grad_q
        dv[keys, :] = dv[keys, :] + grad_v
        dk[keys, :] = dk[keys, :] + grad_k

    each_key_chunk(starts, live, length, BWD_BQ, BWD_STEP, BWD_CHUNK, work)

    @pl.loop(0, length // PREP_BLOCK)
    def _(b):
        rows = pl.ds(pl.multiple_of(b * PREP_BLOCK, PREP_BLOCK), PREP_BLOCK)
        cos, sin = rotary_block(table, turns, b)
        u = dq[rows, :] * SCORE_SCALE
        dqkv[rows, :PAIR] = (u * cos - half_swap(u, in_first) * sin).astype(bf16)
        u = dk[rows, :] * SCORE_SCALE
        dqkv[rows, PAIR : 2 * PAIR] = (u * cos - half_swap(u, in_first) * sin).astype(bf16)
        dqkv[rows, 2 * PAIR :] = dv[rows, :].astype(bf16)

    grad_sums = grads if len(grads.shape) == 2 else grads.reshape(width, grads.shape[-1])
    for m in range(width // ROW_BLOCK):
        part = slice(m * ROW_BLOCK, (m + 1) * ROW_BLOCK)
        grad_sums[part, : 3 * PAIR] = lax.dot_general(
            a1[:, part], dqkv[...], TN, preferred_element_type=f32
        ).astype(bf16)
        total = None
        for source, at in halves:
            rows = pl.ds(pl.multiple_of(at * half, half), half)
            term = lax.dot_general(source[:, part], o_in[rows, :], TN, preferred_element_type=f32)
            total = term if total is None else total + term
        grad_sums[part, 3 * PAIR :] = total.astype(bf16)
    made = [*before, grads]
    cols = grads.shape[-1]
    stores = []
    for n, one in enumerate(made):
        at = slice(n * cols, (n + 1) * cols)
        if part_count == 1:
            stores.append(pltpu.make_async_copy(one, parts[0], sems.at[n, 0]))
            continue
        for j in range(part_count):
            low = jnp.bitwise_xor(me & (part_count - 1), j)
            stores.append(pltpu.make_async_copy(one.at[:, low], parts[j].at[:, :, at], sems.at[n, j]))
    for copy in stores:
        copy.start()
    for copy in stores:
        copy.wait()


def backward_pair(scal, a1, near, far, w, saved, tables, part_shapes, before=(), deps=()):
    length, width = a1.shape
    shape = jax.ShapeDtypeStruct
    outs = [shape((length, 3 * PAIR), bf16)] + [shape(s, bf16) for s in part_shapes]
    grads_shape = (width, 4 * PAIR)
    if len(part_shapes) > 1:
        high, rows_each, _ = part_shapes[0]
        grads_shape = (high, len(part_shapes), rows_each, 4 * PAIR)
        before = [x.reshape(grads_shape) for x in before]
    return pl.pallas_call(
        passing(functools.partial(backward_kernel, len(part_shapes), len(before)), 12 + len(before), len(deps)),
        out_shape=tuple(outs),
        in_specs=[smem()] + [vmem()] * 11 + [anywhere()] * (len(before) + len(deps)),
        out_specs=(vmem(),) + (anywhere(),) * len(part_shapes),
        scratch_shapes=[
            pltpu.VMEM((2, length, 2 * PAIR), bf16),
            pltpu.VMEM((2, length, 2 * PAIR), bf16),
            pltpu.VMEM((2, length, 2 * PAIR), bf16),
            pltpu.VMEM((length, 2 * PAIR), bf16),
            pltpu.VMEM((2, length, PAIR), bf16),
            pltpu.VMEM((2, length, PAIR), bf16),
            pltpu.VMEM((length, PAIR), f32),
            pltpu.VMEM((length, PAIR), f32),
            pltpu.VMEM((length, PAIR), f32),
            pltpu.VMEM(grads_shape, bf16),
            pltpu.SemaphoreType.DMA((len(before) + 1, len(part_shapes))),
        ],
        compiler_params=params(BWD_MIB),
        cost_estimate=lasts(30),
        name="attention_backward",
    )(scal, a1, near, far, w, *saved, *tables, *before, *deps)


def project_kernel(count, scal, *refs):
    rows, weights, out = refs[:count], refs[count : 2 * count], refs[2 * count]
    total = None
    for one, w in zip(rows, weights):
        term = lax.dot_general(one[...], w[...], NT, preferred_element_type=f32)
        total = term if total is None else total + term
    out[...] = total.astype(out.dtype)


def columns_of(weight, at, cols):
    return pl.BlockSpec((weight.shape[0], cols), lambda b, s: (0, at // cols))


def project_far_half(scal, rows, weights, deps=()):
    length, cols = rows[0].shape
    width = weights[0][0].shape[0]
    blocks = length // 2 // ROW_BLOCK
    count = len(rows)
    return pl.pallas_call(
        passing(functools.partial(project_kernel, count), 1 + 2 * count, len(deps)),
        out_shape=jax.ShapeDtypeStruct((length // 2, width), bf16),
        grid_spec=pltpu.PrefetchScalarGridSpec(
            num_scalar_prefetch=1,
            grid=(blocks,),
            in_specs=[pl.BlockSpec((ROW_BLOCK, cols), lambda b, s: (b + (1 - s[2]) * blocks, 0))] * count
            + [columns_of(w, at, cols) for w, at in weights]
            + [anywhere()] * len(deps),
            out_specs=pl.BlockSpec((ROW_BLOCK, width), lambda b, s: (b, 0)),
        ),
        compiler_params=params(),
        cost_estimate=lasts(4),
        name="project_far_half",
    )(scal, *rows, *[w for w, _ in weights], *deps)


def final_kernel(count, scal, *refs):
    rows, weights = refs[:count], refs[count : 2 * count]
    tokens, far, grad_hidden, gains, out, mark = refs[2 * count :]
    mark[...] = jnp.zeros(mark.shape, mark.dtype)
    total = far[...].astype(f32)
    for one, w in zip(rows, weights):
        total = total + lax.dot_general(one[...], w[...], NT, preferred_element_type=f32)
    normed, inv = norm_stats(tokens[...].astype(f32))
    out[...] = grad_hidden[...] + norm_back(total * gains[0:1, :], normed, inv)


def final_rows(scal, rows, weights, tokens, far, grad_hidden, gains, deps=()):
    length, cols = rows[0].shape
    width = tokens.shape[1]
    blocks = length // 2 // ROW_BLOCK
    whole = lambda a: pl.BlockSpec(a.shape, lambda b, s: (0, 0))
    near = lambda a: pl.BlockSpec((ROW_BLOCK, a.shape[1]), lambda b, s: (b + s[2] * blocks, 0))
    plain = pl.BlockSpec((ROW_BLOCK, width), lambda b, s: (b, 0))
    return pl.pallas_call(
        passing(functools.partial(final_kernel, len(rows)), 5 + 2 * len(rows), len(deps)),
        out_shape=(jax.ShapeDtypeStruct((length // 2, width), f32), jax.ShapeDtypeStruct((8, PAIR), f32)),
        grid_spec=pltpu.PrefetchScalarGridSpec(
            num_scalar_prefetch=1,
            grid=(blocks,),
            in_specs=[near(r) for r in rows]
            + [columns_of(w, at, cols) for w, at in weights]
            + [near(tokens), plain, plain, whole(gains)]
            + [anywhere()] * len(deps),
            out_specs=(plain, pl.BlockSpec((8, PAIR), lambda b, s: (0, 0))),
        ),
        compiler_params=params(),
        cost_estimate=lasts(7),
        name="final_rows",
    )(scal, *rows, *[w for w, _ in weights], tokens, far, grad_hidden, gains, *deps)


def finish_kernel(sizes, *refs):
    groups, at = [], 0
    for size in sizes:
        groups.append(refs[at : at + size])
        at += size
    w_qkv, grad_qkv, grad_out, partial = refs[at:]
    pair = 0
    inner = None
    for group in groups:
        total = group[0][...]
        for one in group[1:]:
            total = total + one[...].astype(f32)
        for i in range(total.shape[1] // (4 * PAIR)):
            cols = slice(pair * PAIR, (pair + 1) * PAIR)
            for c in range(3):
                grad = total[:, (4 * i + c) * PAIR : (4 * i + c + 1) * PAIR]
                grad_qkv[c, :, cols] = grad
                term = grad * w_qkv[c, :, cols].astype(f32)
                inner = term if inner is None else inner + term
            grad_out[:, cols] = total[:, (4 * i + 3) * PAIR : (4 * i + 4) * PAIR]
            pair += 1
    partial[...] = jnp.broadcast_to(jnp.sum(inner, axis=1, keepdims=True), partial.shape)


def finish(groups, w_qkv, deps):
    rows, cols = w_qkv.shape[1:]
    shape = jax.ShapeDtypeStruct
    sizes = [len(g) for g in groups]
    flat = [x for g in groups for x in g]
    return pl.pallas_call(
        passing(functools.partial(finish_kernel, sizes), len(flat) + 1, len(deps)),
        out_shape=(shape((3, rows, cols), f32), shape((rows, cols), f32), shape((rows, PAIR), f32)),
        in_specs=[vmem()] * (len(flat) + 1) + [anywhere()] * len(deps),
        out_specs=(vmem(),) * 3,
        compiler_params=params(),
        cost_estimate=lasts(2),
        name="finish",
    )(*flat, w_qkv, *deps)


def ffn_kernel(count, part_count, down_cols, scal, *refs):
    outs_of, weights = refs[:count], refs[count : 2 * count]
    tokens, far, cot, gains = refs[2 * count : 2 * count + 4]
    sources = refs[2 * count + 4 : -9]
    result, dattn, grad_hidden, z_all, pair_all, a2_all, dff_all, ffn_w, sems = refs[-9:]
    width, ff = result.shape[1], z_all.shape[1]
    live, me, core = scal[0], scal[1], scal[2]
    step = pl.program_id(0)
    block = result.shape[0]

    def loads():
        if part_count == 1:
            return [
                pltpu.make_async_copy(sources[0], ffn_w.at[pl.ds(0, 2)], sems.at[0]),
                pltpu.make_async_copy(sources[1], ffn_w.at[2], sems.at[1]),
            ]
        copies = []
        offset = ff - down_cols
        near_at = pl.multiple_of(core * offset, PAIR)
        far_from = pl.multiple_of(ff + (1 - core) * (down_cols - offset), PAIR)
        far_at = pl.multiple_of((1 - core) * down_cols, PAIR)
        for j in range(part_count):
            low = jnp.bitwise_xor(me & (part_count - 1), j)
            mine, other = sources[j], sources[part_count + j]
            copies += [
                pltpu.make_async_copy(mine.at[:, :, :ff], ffn_w.at[core, :, low], sems.at[4 * j]),
                pltpu.make_async_copy(other.at[:, :, :ff], ffn_w.at[1 - core, :, low], sems.at[4 * j + 1]),
                pltpu.make_async_copy(
                    mine.at[:, :, ff:], ffn_w.at[2, :, low, :, pl.ds(near_at, down_cols)], sems.at[4 * j + 2]
                ),
                pltpu.make_async_copy(
                    other.at[:, :, pl.ds(far_from, offset)],
                    ffn_w.at[2, :, low, :, pl.ds(far_at, offset)],
                    sems.at[4 * j + 3],
                ),
            ]
        return copies

    @pl.when(step == 0)
    def _():
        for copy in loads():
            copy.start()

    here = core * (block * pl.num_programs(0)) + step * block
    position = here + lax.broadcasted_iota(jnp.int32, (block, 1), 0)
    valid = (position < live).astype(f32)
    attn = far[...].astype(f32)
    for one, w in zip(outs_of, weights):
        attn = attn + lax.dot_general(one[...], w[...], NT, preferred_element_type=f32)
    hidden = tokens[...].astype(f32) + valid * attn
    normed, inv = norm_stats(hidden)
    gain = gains[8:9, :]
    a2 = (normed * gain).astype(bf16)

    @pl.when(step == 0)
    def _():
        for copy in loads():
            copy.wait()

    weights_in = ffn_w.reshape(3, width, ff) if part_count > 1 else ffn_w
    up = jnp.dot(a2, weights_in[0], preferred_element_type=f32)
    gate = jnp.dot(a2, weights_in[1], preferred_element_type=f32)
    below = 0.5 * (1.0 + lax.erf(up * math.sqrt(0.5)))
    act = up * below
    slope = below + up * jnp.exp(up * up * -0.5) * (1.0 / math.sqrt(2.0 * math.pi))
    z = (act * gate).astype(bf16)
    result[...] = (
        hidden + valid * lax.dot_general(z, weights_in[2], NT, preferred_element_type=f32)
    ).astype(bf16)
    dy = cot[...].astype(f32)
    dff = (valid * dy).astype(bf16)
    dz = jnp.dot(dff, weights_in[2], preferred_element_type=f32)
    du = (dz * gate * slope).astype(bf16)
    dg = (dz * act).astype(bf16)
    da2 = lax.dot_general(du, weights_in[0], NT, preferred_element_type=f32) + lax.dot_general(
        dg, weights_in[1], NT, preferred_element_type=f32
    )
    grad = dy + norm_back(da2 * gain, normed, inv)
    grad_hidden[...] = grad
    dattn[...] = (valid * grad).astype(bf16)
    z_all[...] = z
    pair_all[0] = du
    pair_all[1] = dg
    a2_all[...] = a2
    dff_all[...] = dff


def weight_grad_kernel(split, own, down_cols, scal, z, pair, a2, dff, *outs):
    width, ff = a2.shape[1], z.shape[1]
    core = scal[2]
    for m in range(width // ROW_BLOCK):
        part = slice(m * ROW_BLOCK, (m + 1) * ROW_BLOCK)
        left, down = a2[:, part], dff[:, part]
        if split:
            who = core if own else 1 - core
            at = pl.multiple_of(who * (ff - down_cols), PAIR)
            outs[0][part, :ff] = lax.dot_general(left, pair[who], TN, preferred_element_type=f32).astype(bf16)
            outs[0][part, ff:] = lax.dot_general(
                down, z[:, pl.ds(at, down_cols)], TN, preferred_element_type=f32
            ).astype(bf16)
        else:
            for i in (0, 1):
                outs[0][i, part, :] = lax.dot_general(
                    left, pair[i], TN, preferred_element_type=f32
                ).astype(bf16)
            outs[1][part, :] = lax.dot_general(down, z[...], TN, preferred_element_type=f32).astype(bf16)


def weight_grads(split, own, down_cols, scal, z, pair, a2, dff, deps=()):
    width, ff = a2.shape[1], z.shape[1]
    shape = jax.ShapeDtypeStruct
    if split:
        outs = (shape((width, ff + down_cols), bf16),)
    else:
        outs = (shape((2, width, ff), bf16), shape((width, ff), bf16))
    return pl.pallas_call(
        passing(functools.partial(weight_grad_kernel, split, own, down_cols), 5, len(deps)),
        out_shape=outs,
        in_specs=[smem()] + [vmem()] * 4 + [anywhere()] * len(deps),
        out_specs=(vmem(),) * len(outs),
        compiler_params=params(10 if split else 32),
        cost_estimate=lasts(5),
        name="weight_grads",
    )(scal, z, pair, a2, dff, *deps)


def feed_forward(scal, outs_of, weights, tokens, far, cot, gains, sources, ff, down_cols):
    length, width = tokens.shape
    part_count = len(sources) // 2
    placed = (3, width, ff)
    if part_count > 1:
        placed = (3, sources[0].shape[0], part_count, sources[0].shape[1], ff)
    half = length // 2
    blocks = half // ROW_BLOCK
    shape = jax.ShapeDtypeStruct
    whole = lambda a: pl.BlockSpec(a.shape, lambda b, s: (0,) * len(a.shape))
    near = lambda a: pl.BlockSpec((ROW_BLOCK, a.shape[1]), lambda b, s: (b + s[2] * blocks, 0))
    plain = lambda cols: pl.BlockSpec((ROW_BLOCK, cols), lambda b, s: (b, 0))
    return pl.pallas_call(
        functools.partial(ffn_kernel, len(outs_of), part_count, down_cols),
        out_shape=(
            shape((half, width), bf16),
            shape((half, width), bf16),
            shape((half, width), f32),
            shape((half, ff), bf16),
            shape((2, half, ff), bf16),
            shape((half, width), bf16),
            shape((half, width), bf16),
        ),
        grid_spec=pltpu.PrefetchScalarGridSpec(
            num_scalar_prefetch=1,
            grid=(blocks,),
            in_specs=[near(o) for o in outs_of]
            + [columns_of(w, at, PAIR) for w, at in weights]
            + [near(tokens), plain(width), plain(width), whole(gains)]
            + [anywhere()] * len(sources),
            out_specs=(
                plain(width),
                plain(width),
                plain(width),
                plain(ff),
                pl.BlockSpec((2, ROW_BLOCK, ff), lambda b, s: (0, b, 0)),
                plain(width),
                plain(width),
            ),
            scratch_shapes=[pltpu.VMEM(placed, bf16), pltpu.SemaphoreType.DMA((16,))],
        ),
        compiler_params=params(FFN_MIB),
        cost_estimate=lasts(25),
        name="feed_forward",
    )(scal, *outs_of, *[w for w, _ in weights], tokens, far, cot, gains, *sources)


def pack_kernel(wide, scal, keep, got, *outs):
    me = scal[1]
    for j in range(wide):
        for h in range(outs[0].shape[0]):
            own = h * wide + jnp.bitwise_xor(me & (wide - 1), j)
            outs[j][h] = (keep[own].astype(f32) + got[own].astype(f32)).astype(bf16)


def pack_parts(scal, keep, got, count, deps=()):
    width, cols = keep.shape
    rows = width // count
    wide = 1 << bit_groups(count)[-1][1]
    shape = jax.ShapeDtypeStruct((count // wide, rows, cols), bf16)
    return pl.pallas_call(
        passing(functools.partial(pack_kernel, wide), 3, len(deps)),
        out_shape=(shape,) * wide,
        in_specs=[smem(), vmem(), vmem()] + [anywhere()] * len(deps),
        out_specs=(vmem(),) * wide,
        compiler_params=params(),
        cost_estimate=lasts(4),
        name="pack_parts",
    )(scal, keep.reshape(count, rows, cols), got.reshape(count, rows, cols), *deps)


def rotary_tables(length):
    freqs = ROPE_THETA ** (-np.arange(0, HEAD_DIM, 2) / HEAD_DIM)
    freqs = np.tile(np.float32(freqs).astype(np.float64), 4)
    sign = np.where(np.arange(PAIR) % HEAD_DIM < HEAD_DIM // 2, -1.0, 1.0)

    def both(positions):
        angles = positions[:, None] * freqs[None, :]
        return jnp.asarray(np.stack([np.cos(angles), np.sin(angles) * sign]), f32)

    return both(np.arange(PREP_BLOCK)), both(np.arange(0, length, PREP_BLOCK))


def local(tokens, segment_ids, counts, w_qkv, w_out, w_in, w_down, ln1_gain, ln2_gain, cotangent):
    count = lax.axis_size("dp")
    dp, core = lax.axis_index("dp"), lax.axis_index("head")
    length, width = tokens.shape[1:]
    ff = w_in.shape[2]
    rows_each = width // count
    fast = rows_each % 16 == 0 and count & (count - 1) == 0 and len(bit_groups(count)) == 2
    pairs = w_qkv.shape[2] // PAIR
    first_core = core == 0
    pick = lambda a, b: jnp.where(first_core, a, b)
    join = lambda mine, other: jnp.concatenate([pick(mine, other), pick(other, mine)], axis=0)
    row, cot = tokens[0], cotangent[0]
    seg = segment_ids[0]
    live = counts[0]
    begins = jnp.sum(seg[None, :] < jnp.arange(1, 4)[:, None], axis=1)
    scal = jnp.concatenate([jnp.stack([live, dp, core]), begins]).astype(jnp.int32)

    both = jnp.stack([ln1_gain, ln2_gain], axis=1)
    head_load, rest_load = attention_loads(core.astype(jnp.int32)[None], w_qkv, w_out.T, both, core_swap(both))
    down_turned = w_down.T
    down_cols = -(-(ff // 2) // 128) * 128
    offset = ff - down_cols
    tables = rotary_tables(length)
    out_at = 3 * PAIR * (pairs - 1)
    everyone = ("dp", "head")

    if fast:
        high_bits, low_bits = bit_groups(count)
        head_high = gather_step(head_load[None], count, high_bits)
        at = (dp >> low_bits[1]).astype(jnp.int32)[None]
        rest_load = stack_parts(at, [rest_load[None]], head_high[1:])
        head_parts = gather_step(stack_parts(at, head_high), count, low_bits)
        rest_high = gather_step(rest_load, count, high_bits)
        rest_all = stack_parts(at, rest_high, head_parts[1:])
        zero_one = jnp.concatenate([w_in[0], down_turned[:, :down_cols]], axis=1)
        one_two = jnp.concatenate([w_in[1], down_turned[:, offset:]], axis=1)
        ffn_load = join(pick(zero_one, one_two), core_swap(pick(one_two, zero_one)))
        ffn_load = stack_parts(at, [ffn_load[None]], rest_high[1:])
        ffn_high = gather_step(ffn_load, count, high_bits)
        a1, gains, *kept = forward_pair(
            True, scal, row, tables, head_parts, 0, [rest_all, ffn_load]
        )
        rest_parts = gather_step(rest_all, count, low_bits)
        ffn_all = stack_parts(at, ffn_high, [a1])
        ffn_parts = gather_step(ffn_all, count, low_bits)
        sources = ffn_parts + [core_swap(p) for p in ffn_parts]
        deps, late_deps = [ffn_all], ffn_parts[1:]
    else:
        head_parts = [lax.all_gather(head_load, "dp", axis=0, tiled=True)]
        rest_parts = [lax.all_gather(rest_load, "dp", axis=0, tiled=True)]
        sources = [
            lax.all_gather(w_in, everyone, axis=1, tiled=True),
            lax.all_gather(down_turned, everyone, axis=0, tiled=True),
        ]
        a1, gains, *kept = forward_pair(True, scal, row, tables, head_parts, 0)
        deps, late_deps = [], []

    head_w, saved = kept[0], [kept[1:]]
    rest_w, *kept = forward_pair(False, scal, a1, tables, rest_parts, 0, deps)
    saved.append(kept)
    for i in range(2, pairs):
        saved.append(forward_pair(False, scal, a1, tables, rest_w, 3 * PAIR * (i - 1)))
    qkv_w = [(head_w, 0)] + [(rest_w, 3 * PAIR * (i - 1)) for i in range(1, pairs)]
    out_w = [(rest_w, out_at + i * PAIR) for i in range(pairs)]
    outs_of = [s[3] for s in saved]

    far = core_swap(project_far_half(scal, outs_of, out_w, late_deps))
    result, near_grad, grad_hidden, *kept = feed_forward(scal, outs_of, out_w, row, far, cot, gains, sources, ff, down_cols)
    far_grad = core_swap(near_grad)

    def backward(i, part_shapes, before=(), deps=()):
        q, k, v, o, lse = saved[i]
        w, at = out_w[i]
        w = w[:, at : at + PAIR]
        return backward_pair(
            scal, a1, near_grad, far_grad, w, (q, k, v, o, lse), tables, part_shapes, before, deps
        )

    if fast:
        wide = 1 << low_bits[1]
        parts_of = lambda n: [(count // wide, rows_each, n * 4 * PAIR)] * wide
        got = core_swap(weight_grads(True, False, down_cols, scal, *kept)[0])
        keep = weight_grads(True, True, down_cols, scal, *kept)[0]
        deps = pack_parts(scal, keep, got, count)
        ffn_near = reduce_near(deps, count)
        dqkv, before = [], []
        pieces = None
        for i in range(pairs - 1):
            last = i == pairs - 2
            one, *parts = backward(
                i, parts_of(pairs - 1) if last else [(width, 4 * PAIR)], before if last else [], deps
            )
            dqkv.append(one)
            before += parts
        pieces = sum_parts(at, ffn_near, [one])
        done = reduce_far(pieces, count, wide)
        early_near = reduce_near(parts, count)
        one, *parts = backward(pairs - 1, parts_of(1), (), pieces)
        dqkv.append(one)
        late_near = reduce_near(parts, count)
        pieces = sum_parts(at, early_near, [one])
        early = far_pieces(pieces, count, wide)
        far_da = project_far_half(scal, dqkv, qkv_w, pieces)
        pieces = sum_parts(at, late_near, pieces)
        shards = [early, far_pieces(pieces, count, wide)]
        far_da = core_swap(far_da)
        grad_tokens, mark = final_rows(scal, dqkv, qkv_w, row, far_da, grad_hidden, gains, pieces)
        rows_here = w_in.shape[1]
        low, high = done[:rows_here], done[rows_here:]
        mine = pick(low, high)
        other = core_swap(pick(high, low))
        grad_w_in = jnp.stack(
            [pick(mine[:, :ff], other[:, :ff]), pick(other[:, :ff], mine[:, :ff])]
        )
        grad_down = jnp.concatenate(
            [pick(mine[:, ff:], other[:, ff:]), pick(other[:, ff:], mine[:, ff:])[:, down_cols - offset :]],
            axis=1,
        ).T
    else:
        keep, send = weight_grads(False, True, down_cols, scal, *kept)
        grad_w_in = lax.psum_scatter(keep.astype(f32), everyone, scatter_dimension=1, tiled=True)
        grad_down = lax.psum_scatter(send.astype(f32), everyone, scatter_dimension=0, tiled=True).T
        dqkv, shards = [], []
        for i in range(pairs):
            one, parts = backward(i, [(width, 4 * PAIR)])
            dqkv.append(one)
            shards.append([lax.psum_scatter(parts.astype(f32), "dp", scatter_dimension=0, tiled=True)])
        far_da = core_swap(project_far_half(scal, dqkv, qkv_w))
        grad_tokens, mark = final_rows(scal, dqkv, qkv_w, row, far_da, grad_hidden, gains)

    grad_two = jnp.sum(grad_w_in * w_in.astype(f32), axis=(0, 2)) / ln2_gain.astype(f32)

    grad_qkv, grad_out, partial = finish(shards, w_qkv, [mark])
    rows_here = ln1_gain.shape[0]
    partial = partial[:, 0]
    low, high = partial[:rows_here], partial[rows_here:]
    grad_one = (pick(low, high) + core_swap(pick(high, low))) / ln1_gain.astype(f32)
    return (
        result[None],
        grad_tokens[None],
        grad_qkv,
        grad_out.T,
        grad_w_in,
        grad_down,
        grad_one,
        grad_two,
    )


def solution(mesh):
    placed = (
        P("dp", None, None),
        P("dp", None),
        P("dp"),
        P(None, "dp", "head"),
        P("head", "dp"),
        P(None, ("dp", "head"), None),
        P(None, ("dp", "head")),
        P(("dp", "head")),
        P(("dp", "head")),
        P("dp", "head", None),
    )
    return jax.shard_map(
        local,
        mesh=mesh,
        in_specs=placed,
        out_specs=(
            P("dp", "head", None),
            P("dp", "head", None),
            P(None, "dp", "head"),
            P("head", "dp"),
            P(None, ("dp", "head"), None),
            P(None, ("dp", "head")),
            P(("dp", "head")),
            P(("dp", "head")),
        ),
        check_vma=False,
    )
```

```python
import functools
import math

import jax
import jax.numpy as jnp
import numpy as np
from jax import lax
from jax.experimental import pallas as pl
from jax.experimental.pallas import tpu as pltpu
from jax.sharding import PartitionSpec as P

HEAD_DIM = 64
PAIR = 2 * HEAD_DIM
LAYER_EPS = 1e-05
ROPE_THETA = 160000.0
BIG = 1e30
LOG2_SCALE = math.log2(math.e) / math.sqrt(HEAD_DIM)
SCORE_SCALE = 1.0 / math.sqrt(HEAD_DIM)
ROW_BLOCK = 256
PREP_BLOCK = 512
FWD_MIB, BWD_MIB, FFN_MIB = 20, 23, 25
FWD_BQ, FWD_STEP = 512, 256
BWD_BQ, BWD_STEP, BWD_CHUNK = 256, 128, 10
NT = (((1,), (1,)), ((), ()))
TN = (((0,), (0,)), ((), ()))
bf16 = jnp.bfloat16
f32 = jnp.float32


def vmem():
    return pl.BlockSpec(memory_space=pltpu.VMEM)


def smem():
    return pl.BlockSpec(memory_space=pltpu.SMEM)


def hbm():
    return pl.BlockSpec(memory_space=pltpu.HBM)


def anywhere():
    return pl.BlockSpec(memory_space=pl.ANY)


def params(mib=10):
    return pltpu.CompilerParams(vmem_limit_bytes=mib << 20)


def lasts(micros):
    return pl.CostEstimate(flops=int(micros * 1e8), bytes_accessed=0, transcendentals=0)


def passing(kernel, inputs, deps):
    def run(*refs):
        kernel(*refs[:inputs], *refs[inputs + deps :])

    return run


def bit_groups(count):
    bits = count.bit_length() - 1
    shifts = []
    low = 0
    while low < bits:
        wide = min(2, bits - low)
        shifts.append((low, wide))
        low += wide
    return shifts[::-1]


def xor_permute(value, count, mask):
    return lax.ppermute(value, "dp", [(i, i ^ mask) for i in range(count)])


def core_swap(value):
    return lax.ppermute(value, "head", [(0, 1), (1, 0)])


def stack_kernel(at, *refs):
    ins, out = refs[:-1], refs[-1]
    for j, one in enumerate(ins):
        out[jnp.bitwise_xor(at[0], j) if len(ins) > 1 else 0] = one[0]


def stack_parts(at, parts, deps=()):
    _, rows, cols = parts[0].shape
    return pl.pallas_call(
        passing(stack_kernel, 1 + len(parts), len(deps)),
        out_shape=jax.ShapeDtypeStruct((len(parts), rows, cols), parts[0].dtype),
        in_specs=[smem()] + [vmem()] * len(parts) + [anywhere()] * len(deps),
        out_specs=vmem(),
        compiler_params=params(),
        cost_estimate=lasts(1),
        name="stack_parts",
    )(at, *parts, *deps)


def gather_step(current, count, group):
    shift, wide = group
    return [current] + [xor_permute(current, count, j << shift) for j in range(1, 1 << wide)]


def sum_kernel(count, at, *refs):
    ins, outs = refs[:count], refs[count:]
    for i, out in enumerate(outs):
        entry = jnp.bitwise_xor(at[0], i)
        total = ins[0][entry].astype(f32)
        for one in ins[1:]:
            total = total + one[entry].astype(f32)
        out[...] = total.astype(out.dtype)


def sum_parts(at, arrays, deps=()):
    m, rows, cols = arrays[0].shape
    return pl.pallas_call(
        passing(functools.partial(sum_kernel, len(arrays)), 1 + len(arrays), len(deps)),
        out_shape=tuple(
            jax.ShapeDtypeStruct((rows, cols), f32 if i == 0 else bf16) for i in range(m)
        ),
        in_specs=[smem()] + [vmem()] * len(arrays) + [anywhere()] * len(deps),
        out_specs=(vmem(),) * m,
        compiler_params=params(),
        cost_estimate=lasts(2),
        name="sum_parts",
    )(at, *arrays, *deps)


def reduce_near(parts, count):
    return [parts[0]] + [xor_permute(parts[j], count, j) for j in range(1, len(parts))]


def far_pieces(pieces, count, wide):
    shift = wide.bit_length() - 1
    return [pieces[0]] + [xor_permute(pieces[h], count, h << shift) for h in range(1, len(pieces))]


def reduce_far(pieces, count, wide):
    total, *others = far_pieces(pieces, count, wide)
    for one in others:
        total = total + one.astype(f32)
    return total


def load_kernel(pairs, scal, w_qkv, out_turned, mine, other, head, rest):
    for c in range(3):
        head[:, c * PAIR : (c + 1) * PAIR] = w_qkv[c, :, :PAIR]
        for i in range(1, pairs):
            at = (3 * (i - 1) + c) * PAIR
            rest[:, at : at + PAIR] = w_qkv[c, :, i * PAIR : (i + 1) * PAIR]
    rest[:, 3 * PAIR * (pairs - 1) :] = out_turned[...]
    mine, other = mine[...].astype(f32), other[...].astype(f32)
    first = scal[0] == 0
    gains = jnp.concatenate([jnp.where(first, mine, other), jnp.where(first, other, mine)], axis=0)
    low = lax.broadcasted_iota(jnp.int32, (gains.shape[0], PAIR), 1) < HEAD_DIM
    head[:, 3 * PAIR :] = jnp.where(low, gains[:, 0:1], gains[:, 1:2]).astype(bf16)


def attention_loads(scal, w_qkv, out_turned, mine, other):
    rows, cols = w_qkv.shape[1:]
    pairs = cols // PAIR
    shape = jax.ShapeDtypeStruct
    return pl.pallas_call(
        functools.partial(load_kernel, pairs),
        out_shape=(shape((rows, 4 * PAIR), bf16), shape((rows, 3 * PAIR * (pairs - 1) + cols), bf16)),
        in_specs=[smem()] + [vmem()] * 4,
        out_specs=(vmem(),) * 2,
        compiler_params=params(),
        cost_estimate=lasts(1),
        name="attention_loads",
    )(scal, w_qkv, out_turned, mine, other)


def placed_copies(parts, target, sems, me, cols):
    if len(parts) == 1:
        return [pltpu.make_async_copy(parts[0].at[:, cols], target.at[:, cols], sems.at[0])]
    wide = len(parts)
    copies = []
    for j in range(wide):
        low = jnp.bitwise_xor(me & (wide - 1), j)
        copies.append(
            pltpu.make_async_copy(parts[j].at[:, :, cols], target.at[:, low, :, cols], sems.at[j])
        )
    return copies


def document_starts(scal, length):
    return [jnp.int32(0), scal[3], scal[4], scal[5], jnp.int32(length)]


def key_range(starts, live, first, size, length):
    last = jnp.minimum(first + size, live) - 1
    low = jnp.int32(0)
    high = jnp.int32(length)
    for d in (1, 2, 3):
        low = jnp.where(starts[d] <= first, starts[d], low)
    for d in (3, 2, 1):
        high = jnp.where(starts[d] > last, starts[d], high)
    high = jnp.minimum(high, live)
    seen = first < live
    return jnp.where(seen, low, 0), jnp.where(seen, high, 0)


def each_query_block(starts, live, length, size, step, work, empty):
    @pl.loop(0, length // size)
    def _(i):
        first = pl.multiple_of(i * size, size)
        low, high = key_range(starts, live, first, size, length)
        base = low // 16 * 16
        steps = (high - base + step - 1) // step
        base = pl.multiple_of(jnp.maximum(jnp.minimum(base, length - steps * step), 0), 16)
        rows = pl.ds(first, size)
        for w in range(1, length // step + 1):

            @pl.when(steps == w)
            def _():
                work(rows, pl.ds(base, w * step))

        @pl.when(steps <= 0)
        def _():
            empty(rows)


def each_key_chunk(starts, live, length, size, step, most, work):
    @pl.loop(0, length // size)
    def _(i):
        first = pl.multiple_of(i * size, size)
        low, high = key_range(starts, live, first, size, length)
        base = low // 16 * 16
        steps = (high - base + step - 1) // step
        base = jnp.maximum(jnp.minimum(base, length - steps * step), 0)
        rows = pl.ds(first, size)

        @pl.loop(0, (steps + most - 1) // most)
        def _(c):
            at = pl.multiple_of(base + c * (most * step), 16)
            left = jnp.minimum(steps - c * most, most)
            for w in range(1, most + 1):

                @pl.when(left == w)
                def _():
                    work(rows, pl.ds(at, w * step))


def lane_bounds(starts, live, length):
    column = lax.broadcasted_iota(jnp.int32, (1, PAIR), 1) & (HEAD_DIM - 1)
    low = jnp.zeros((1, PAIR), jnp.int32)
    high = jnp.where(column == 4, live, length)
    for d in range(4):
        low = jnp.where(column == d, starts[d], low)
        high = jnp.where(column == d, starts[d + 1], high)
    return column, low, high


def mask_features(bounds, first, size):
    column, low, high = bounds
    position = first + lax.broadcasted_iota(jnp.int32, (size, PAIR), 0)
    inside = (position >= low) & (position < high)
    column = jnp.broadcast_to(column, (size, PAIR))
    query = jnp.where((inside & (column < 4)) | (column == 4), 1.0, 0.0)
    return query, jnp.where(inside, 0.0, -BIG)


def rotary_block(table, turns, block):
    cos, sin = table[0], table[1]
    cos_at, sin_at = turns[0, pl.ds(block, 1), :], turns[1, pl.ds(block, 1), :]
    return cos * cos_at - sin * sin_at, sin * cos_at + cos * sin_at


def norm_stats(values):
    center = values - jnp.mean(values, axis=-1, keepdims=True)
    spread = jnp.mean(center * center, axis=-1, keepdims=True)
    inv = lax.rsqrt(spread + LAYER_EPS)
    return center * inv, inv


def norm_back(grad, normed, inv):
    return inv * (
        grad
        - jnp.mean(grad, axis=-1, keepdims=True)
        - normed * jnp.mean(grad * normed, axis=-1, keepdims=True)
    )


def half_swap(values, in_first):
    return jnp.where(in_first, pltpu.roll(values, PAIR - HEAD_DIM // 2, 1), pltpu.roll(values, HEAD_DIM // 2, 1))


def split3(values):
    a = values.astype(bf16)
    left = values - a.astype(f32)
    b = left.astype(bf16)
    return a, b, (left - b.astype(f32)).astype(bf16)


def forward_kernel(first, part_count, at, *refs):
    scal, src, table, turns = refs[:4]
    parts = refs[4 : 4 + max(part_count, 1)]
    outs = refs[4 + max(part_count, 1) :]
    if first:
        a1, gains = outs[:2]
        outs = outs[2:]
    if part_count:
        w, outs = outs[0], outs[1:]
    else:
        w = parts[0]
    q_out, k_out, v_out, o_out, lse_out, qx, kx, vx, sems = outs
    length, width = src.shape
    live, me = scal[0], scal[1]

    copies, later = [], []
    if part_count:
        soon = 4 * PAIR if first else 3 * PAIR
        copies = placed_copies(parts, w, sems.at[0], me, slice(0, soon))
        if w.shape[-1] > soon:
            later = placed_copies(parts, w, sems.at[1], me, slice(soon, w.shape[-1]))
        w = w.reshape(width, w.shape[-1])
    for copy in copies + later:
        copy.start()
    starts = document_starts(scal, length)
    bounds = lane_bounds(starts, live, length)
    for copy in copies:
        copy.wait()
    if first:
        turned = jnp.transpose(w[:, 3 * PAIR : 4 * PAIR].astype(f32))
        gains[0:8, :] = turned[0:8]
        gains[8:16, :] = turned[HEAD_DIM : HEAD_DIM + 8]
    lane = lax.broadcasted_iota(jnp.int32, (PREP_BLOCK, PAIR), 1)
    low_head = lane < HEAD_DIM
    in_first = (lane & (HEAD_DIM - 1)) < HEAD_DIM // 2
    zero = jnp.zeros((PREP_BLOCK, PAIR), bf16)

    @pl.loop(0, length // PREP_BLOCK)
    def _(b):
        rows = pl.ds(pl.multiple_of(b * PREP_BLOCK, PREP_BLOCK), PREP_BLOCK)
        if first:
            normed, _ = norm_stats(src[rows, :].astype(f32))
            a = (normed * gains[0:1, :]).astype(bf16)
            a1[rows, :] = a
        else:
            a = src[rows, :]
        qkv = jnp.dot(a, w[:, at : at + 3 * PAIR], preferred_element_type=f32)
        cos, sin = rotary_block(table, turns, b)
        query_mask, key_mask = mask_features(bounds, b * PREP_BLOCK, PREP_BLOCK)
        query_mask, key_mask = query_mask.astype(bf16), key_mask.astype(bf16)
        u = qkv[:, :PAIR]
        q = (u * cos + half_swap(u, in_first) * sin).astype(bf16)
        u = qkv[:, PAIR : 2 * PAIR]
        k = (u * cos + half_swap(u, in_first) * sin).astype(bf16)
        v = qkv[:, 2 * PAIR :].astype(bf16)
        q_out[rows, :] = q
        k_out[rows, :] = k
        v_out[rows, :] = v
        scaled = q.astype(f32) * LOG2_SCALE
        high = scaled.astype(bf16)
        rest = (scaled - high.astype(f32)).astype(bf16)
        for h in (0, 1):
            mine = low_head if h == 0 else ~low_head
            qx[h, rows, :PAIR] = jnp.where(mine, high, zero)
            qx[h, rows, PAIR:] = jnp.where(mine, rest, query_mask)
            kx[h, rows, :PAIR] = k
            kx[h, rows, PAIR:] = jnp.where(mine, k, key_mask)
        vx[rows, :PAIR] = v
        vx[rows, PAIR:] = jnp.ones((PREP_BLOCK, PAIR), bf16)

    lane_q = lax.broadcasted_iota(jnp.int32, (FWD_BQ, PAIR), 1) < HEAD_DIM

    def work(rows, keys):
        values = vx[keys, :]
        scores = [
            lax.dot_general(qx[h, rows, :], kx[h, keys, :], NT, preferred_element_type=f32) for h in (0, 1)
        ]
        tops, sums = [], []
        for h in (0, 1):
            top = jnp.max(scores[h], axis=1, keepdims=True)
            probs = jnp.exp2(scores[h] - top).astype(bf16)
            tops.append(top)
            sums.append(jnp.dot(probs, values, preferred_element_type=f32))
        total = jnp.where(lane_q, sums[0][:, PAIR:], sums[1][:, PAIR:])
        out = jnp.where(lane_q, sums[0][:, :PAIR], sums[1][:, :PAIR])
        o_out[rows, :] = (out / total).astype(bf16)
        lse_out[rows, :] = jnp.maximum(jnp.where(lane_q, tops[0], tops[1]) + jnp.log2(total), -1e20)

    def empty(rows):
        o_out[rows, :] = jnp.zeros((FWD_BQ, PAIR), bf16)
        lse_out[rows, :] = jnp.zeros((FWD_BQ, PAIR), f32)

    each_query_block(starts, live, length, FWD_BQ, FWD_STEP, work, empty)
    for copy in later:
        copy.wait()


def forward_pair(first, scal, src, tables, parts, at, deps=()):
    length, width = src.shape
    shape = jax.ShapeDtypeStruct
    outs = [shape((length, PAIR), bf16)] * 4 + [shape((length, PAIR), f32)]
    pieces = isinstance(parts, list)
    operands = parts if pieces else [parts]
    if pieces:
        placed = (width,) if len(parts) == 1 else (parts[0].shape[0], len(parts), parts[0].shape[1])
        outs = [shape(placed + (parts[0].shape[-1],), bf16)] + outs
    if first:
        outs = [shape((length, width), bf16), shape((16, width), f32)] + outs
    kernel = functools.partial(forward_kernel, first, len(parts) if pieces else 0, at)
    made = pl.pallas_call(
        passing(kernel, 4 + len(operands), len(deps)),
        out_shape=tuple(outs),
        in_specs=[smem(), vmem(), vmem(), vmem()]
        + [hbm() if pieces else vmem()] * len(operands)
        + [anywhere()] * len(deps),
        out_specs=(vmem(),) * len(outs),
        scratch_shapes=[
            pltpu.VMEM((2, length, 2 * PAIR), bf16),
            pltpu.VMEM((2, length, 2 * PAIR), bf16),
            pltpu.VMEM((length, 2 * PAIR), bf16),
            pltpu.SemaphoreType.DMA((2, 4)),
        ],
        compiler_params=params(FWD_MIB),
        cost_estimate=lasts(18),
        name="attention_forward_first" if first else "attention_forward",
    )(scal, src, *tables, *operands, *deps)
    made = list(made)
    if pieces:
        number = 2 if first else 0
        made[number] = made[number].reshape(width, -1)
    return made


def backward_kernel(part_count, carried, *refs):
    scal, a1, near, far, w, q_in, k_in, v_in, o_in, lse, table, turns = refs[:12]
    before = refs[12 : 12 + carried]
    refs = refs[12 + carried :]
    dqkv, parts = refs[0], refs[1 : 1 + part_count]
    (qx, kx, dx, vx, qm, km, dq, dk, dv, grads, sems) = refs[1 + part_count :]
    length, width = a1.shape
    half = length // 2
    live, me, core = scal[0], scal[1], scal[2]
    starts = document_starts(scal, length)
    bounds = lane_bounds(starts, live, length)
    halves = ((near, core), (far, 1 - core))
    lane = lax.broadcasted_iota(jnp.int32, (PREP_BLOCK, PAIR), 1)
    in_head = lane & (HEAD_DIM - 1)
    low_head = lane < HEAD_DIM
    in_first = in_head < HEAD_DIM // 2
    zero = jnp.zeros((PREP_BLOCK, PAIR), bf16)
    minus = jnp.full((PREP_BLOCK, PAIR), -1, bf16)

    def prepare(source, at, b):
        first = pl.multiple_of(at * half + b * PREP_BLOCK, PREP_BLOCK)
        rows = pl.ds(first, PREP_BLOCK)
        grad = jnp.dot(source[pl.ds(pl.multiple_of(b * PREP_BLOCK, PREP_BLOCK), PREP_BLOCK), :], w[...], preferred_element_type=f32).astype(bf16)
        query_mask, key_mask = mask_features(bounds, first, PREP_BLOCK)
        q, k = q_in[rows, :], k_in[rows, :]
        scaled = q.astype(f32) * LOG2_SCALE
        high = scaled.astype(bf16)
        rest = (scaled - high.astype(f32)).astype(bf16)
        la, lb, lc = split3(pltpu.roll(lse[rows, :], HEAD_DIM, 1))
        fq_b = jnp.where(
            in_head == 5, la, jnp.where(in_head == 6, lb, jnp.where(in_head == 7, lc, query_mask.astype(bf16)))
        )
        fk_b = jnp.where((in_head >= 5) & (in_head < 8), minus, key_mask.astype(bf16))
        inner = grad.astype(f32) * o_in[rows, :].astype(f32)
        for h in (0, 1):
            mine = low_head if h == 0 else ~low_head
            qx[h, rows, :PAIR] = jnp.where(mine, high, zero)
            qx[h, rows, PAIR:] = jnp.where(mine, rest, fq_b)
            kx[h, rows, :PAIR] = k
            kx[h, rows, PAIR:] = jnp.where(mine, k, fk_b)
            qm[h, rows, :] = jnp.where(mine, q, zero)
            km[h, rows, :] = jnp.where(mine, k, zero)
            dx[h, rows, :PAIR] = jnp.where(mine, grad, zero)
            delta = jnp.sum(jnp.where(mine, inner, 0.0), axis=1, keepdims=True)
            da, db, dc = split3(jnp.broadcast_to(delta, (PREP_BLOCK, PAIR)))
            dx[h, rows, PAIR:] = jnp.where(
                lane == 0, da, jnp.where(lane == 1, db, jnp.where(lane == 2, dc, zero))
            )
        vx[rows, :PAIR] = v_in[rows, :]
        vx[rows, PAIR:] = jnp.where(lane < 3, minus, zero)
        dq[rows, :] = jnp.zeros((PREP_BLOCK, PAIR), f32)
        dk[rows, :] = jnp.zeros((PREP_BLOCK, PAIR), f32)
        dv[rows, :] = jnp.zeros((PREP_BLOCK, PAIR), f32)

    for source, at in halves:

        @pl.loop(0, half // PREP_BLOCK)
        def _(b):
            prepare(source, at, b)

    def work(rows, keys):
        grad_q = dq[rows, :]
        grad_k = grad_v = None
        for h in (0, 1):
            scores = lax.dot_general(qx[h, rows, :], kx[h, keys, :], NT, preferred_element_type=f32)
            pulled = lax.dot_general(dx[h, rows, :], vx[keys, :], NT, preferred_element_type=f32)
            probs = jnp.exp2(scores)
            grad_s = (probs * pulled).astype(bf16)
            one_q = jnp.dot(grad_s, km[h, keys, :], preferred_element_type=f32)
            one_v = lax.dot_general(probs.astype(bf16), dx[h, rows, :PAIR], TN, preferred_element_type=f32)
            one_k = lax.dot_general(grad_s, qm[h, rows, :], TN, preferred_element_type=f32)
            grad_q = grad_q + one_q
            grad_v = one_v if h == 0 else grad_v + one_v
            grad_k = one_k if h == 0 else grad_k + one_k
        dq[rows, :] = grad_q
        dv[keys, :] = dv[keys, :] + grad_v
        dk[keys, :] = dk[keys, :] + grad_k

    each_key_chunk(starts, live, length, BWD_BQ, BWD_STEP, BWD_CHUNK, work)

    @pl.loop(0, length // PREP_BLOCK)
    def _(b):
        rows = pl.ds(pl.multiple_of(b * PREP_BLOCK, PREP_BLOCK), PREP_BLOCK)
        cos, sin = rotary_block(table, turns, b)
        u = dq[rows, :] * SCORE_SCALE
        dqkv[rows, :PAIR] = (u * cos - half_swap(u, in_first) * sin).astype(bf16)
        u = dk[rows, :] * SCORE_SCALE
        dqkv[rows, PAIR : 2 * PAIR] = (u * cos - half_swap(u, in_first) * sin).astype(bf16)
        dqkv[rows, 2 * PAIR :] = dv[rows, :].astype(bf16)

    grad_sums = grads if len(grads.shape) == 2 else grads.reshape(width, grads.shape[-1])
    for m in range(width // ROW_BLOCK):
        part = slice(m * ROW_BLOCK, (m + 1) * ROW_BLOCK)
        grad_sums[part, : 3 * PAIR] = lax.dot_general(
            a1[:, part], dqkv[...], TN, preferred_element_type=f32
        ).astype(bf16)
        total = None
        for source, at in halves:
            rows = pl.ds(pl.multiple_of(at * half, half), half)
            term = lax.dot_general(source[:, part], o_in[rows, :], TN, preferred_element_type=f32)
            total = term if total is None else total + term
        grad_sums[part, 3 * PAIR :] = total.astype(bf16)
    made = [*before, grads]
    cols = grads.shape[-1]
    stores = []
    for n, one in enumerate(made):
        at = slice(n * cols, (n + 1) * cols)
        if part_count == 1:
            stores.append(pltpu.make_async_copy(one, parts[0], sems.at[n, 0]))
            continue
        for j in range(part_count):
            low = jnp.bitwise_xor(me & (part_count - 1), j)
            stores.append(pltpu.make_async_copy(one.at[:, low], parts[j].at[:, :, at], sems.at[n, j]))
    for copy in stores:
        copy.start()
    for copy in stores:
        copy.wait()


def backward_pair(scal, a1, near, far, w, saved, tables, part_shapes, before=(), deps=()):
    length, width = a1.shape
    shape = jax.ShapeDtypeStruct
    outs = [shape((length, 3 * PAIR), bf16)] + [shape(s, bf16) for s in part_shapes]
    grads_shape = (width, 4 * PAIR)
    if len(part_shapes) > 1:
        high, rows_each, _ = part_shapes[0]
        grads_shape = (high, len(part_shapes), rows_each, 4 * PAIR)
        before = [x.reshape(grads_shape) for x in before]
    return pl.pallas_call(
        passing(functools.partial(backward_kernel, len(part_shapes), len(before)), 12 + len(before), len(deps)),
        out_shape=tuple(outs),
        in_specs=[smem()] + [vmem()] * 11 + [anywhere()] * (len(before) + len(deps)),
        out_specs=(vmem(),) + (anywhere(),) * len(part_shapes),
        scratch_shapes=[
            pltpu.VMEM((2, length, 2 * PAIR), bf16),
            pltpu.VMEM((2, length, 2 * PAIR), bf16),
            pltpu.VMEM((2, length, 2 * PAIR), bf16),
            pltpu.VMEM((length, 2 * PAIR), bf16),
            pltpu.VMEM((2, length, PAIR), bf16),
            pltpu.VMEM((2, length, PAIR), bf16),
            pltpu.VMEM((length, PAIR), f32),
            pltpu.VMEM((length, PAIR), f32),
            pltpu.VMEM((length, PAIR), f32),
            pltpu.VMEM(grads_shape, bf16),
            pltpu.SemaphoreType.DMA((len(before) + 1, len(part_shapes))),
        ],
        compiler_params=params(BWD_MIB),
        cost_estimate=lasts(30),
        name="attention_backward",
    )(scal, a1, near, far, w, *saved, *tables, *before, *deps)


def project_kernel(count, scal, *refs):
    rows, weights, out = refs[:count], refs[count : 2 * count], refs[2 * count]
    total = None
    for one, w in zip(rows, weights):
        term = lax.dot_general(one[...], w[...], NT, preferred_element_type=f32)
        total = term if total is None else total + term
    out[...] = total.astype(out.dtype)


def columns_of(weight, at, cols):
    return pl.BlockSpec((weight.shape[0], cols), lambda b, s: (0, at // cols))


def project_far_half(scal, rows, weights, deps=()):
    length, cols = rows[0].shape
    width = weights[0][0].shape[0]
    blocks = length // 2 // ROW_BLOCK
    count = len(rows)
    return pl.pallas_call(
        passing(functools.partial(project_kernel, count), 1 + 2 * count, len(deps)),
        out_shape=jax.ShapeDtypeStruct((length // 2, width), bf16),
        grid_spec=pltpu.PrefetchScalarGridSpec(
            num_scalar_prefetch=1,
            grid=(blocks,),
            in_specs=[pl.BlockSpec((ROW_BLOCK, cols), lambda b, s: (b + (1 - s[2]) * blocks, 0))] * count
            + [columns_of(w, at, cols) for w, at in weights]
            + [anywhere()] * len(deps),
            out_specs=pl.BlockSpec((ROW_BLOCK, width), lambda b, s: (b, 0)),
        ),
        compiler_params=params(),
        cost_estimate=lasts(4),
        name="project_far_half",
    )(scal, *rows, *[w for w, _ in weights], *deps)


def final_kernel(count, scal, *refs):
    rows, weights = refs[:count], refs[count : 2 * count]
    tokens, far, grad_hidden, gains, out, mark = refs[2 * count :]
    mark[...] = jnp.zeros(mark.shape, mark.dtype)
    total = far[...].astype(f32)
    for one, w in zip(rows, weights):
        total = total + lax.dot_general(one[...], w[...], NT, preferred_element_type=f32)
    normed, inv = norm_stats(tokens[...].astype(f32))
    out[...] = grad_hidden[...] + norm_back(total * gains[0:1, :], normed, inv)


def final_rows(scal, rows, weights, tokens, far, grad_hidden, gains, deps=()):
    length, cols = rows[0].shape
    width = tokens.shape[1]
    blocks = length // 2 // ROW_BLOCK
    whole = lambda a: pl.BlockSpec(a.shape, lambda b, s: (0, 0))
    near = lambda a: pl.BlockSpec((ROW_BLOCK, a.shape[1]), lambda b, s: (b + s[2] * blocks, 0))
    plain = pl.BlockSpec((ROW_BLOCK, width), lambda b, s: (b, 0))
    return pl.pallas_call(
        passing(functools.partial(final_kernel, len(rows)), 5 + 2 * len(rows), len(deps)),
        out_shape=(jax.ShapeDtypeStruct((length // 2, width), f32), jax.ShapeDtypeStruct((8, PAIR), f32)),
        grid_spec=pltpu.PrefetchScalarGridSpec(
            num_scalar_prefetch=1,
            grid=(blocks,),
            in_specs=[near(r) for r in rows]
            + [columns_of(w, at, cols) for w, at in weights]
            + [near(tokens), plain, plain, whole(gains)]
            + [anywhere()] * len(deps),
            out_specs=(plain, pl.BlockSpec((8, PAIR), lambda b, s: (0, 0))),
        ),
        compiler_params=params(),
        cost_estimate=lasts(7),
        name="final_rows",
    )(scal, *rows, *[w for w, _ in weights], tokens, far, grad_hidden, gains, *deps)


def finish_kernel(sizes, *refs):
    groups, at = [], 0
    for size in sizes:
        groups.append(refs[at : at + size])
        at += size
    w_qkv, grad_qkv, grad_out, partial = refs[at:]
    pair = 0
    inner = None
    for group in groups:
        total = group[0][...]
        for one in group[1:]:
            total = total + one[...].astype(f32)
        for i in range(total.shape[1] // (4 * PAIR)):
            cols = slice(pair * PAIR, (pair + 1) * PAIR)
            for c in range(3):
                grad = total[:, (4 * i + c) * PAIR : (4 * i + c + 1) * PAIR]
                grad_qkv[c, :, cols] = grad
                term = grad * w_qkv[c, :, cols].astype(f32)
                inner = term if inner is None else inner + term
            grad_out[:, cols] = total[:, (4 * i + 3) * PAIR : (4 * i + 4) * PAIR]
            pair += 1
    partial[...] = jnp.broadcast_to(jnp.sum(inner, axis=1, keepdims=True), partial.shape)


def finish(groups, w_qkv, deps):
    rows, cols = w_qkv.shape[1:]
    shape = jax.ShapeDtypeStruct
    sizes = [len(g) for g in groups]
    flat = [x for g in groups for x in g]
    return pl.pallas_call(
        passing(functools.partial(finish_kernel, sizes), len(flat) + 1, len(deps)),
        out_shape=(shape((3, rows, cols), f32), shape((rows, cols), f32), shape((rows, PAIR), f32)),
        in_specs=[vmem()] * (len(flat) + 1) + [anywhere()] * len(deps),
        out_specs=(vmem(),) * 3,
        compiler_params=params(),
        cost_estimate=lasts(2),
        name="finish",
    )(*flat, w_qkv, *deps)


def ffn_kernel(count, part_count, down_cols, scal, *refs):
    outs_of, weights = refs[:count], refs[count : 2 * count]
    tokens, far, cot, gains = refs[2 * count : 2 * count + 4]
    sources = refs[2 * count + 4 : -9]
    result, dattn, grad_hidden, z_all, pair_all, a2_all, dff_all, ffn_w, sems = refs[-9:]
    width, ff = result.shape[1], z_all.shape[1]
    live, me, core = scal[0], scal[1], scal[2]
    step = pl.program_id(0)
    block = result.shape[0]

    def loads():
        if part_count == 1:
            return [
                pltpu.make_async_copy(sources[0], ffn_w.at[pl.ds(0, 2)], sems.at[0]),
                pltpu.make_async_copy(sources[1], ffn_w.at[2], sems.at[1]),
            ]
        copies = []
        offset = ff - down_cols
        near_at = pl.multiple_of(core * offset, PAIR)
        far_from = pl.multiple_of(ff + (1 - core) * (down_cols - offset), PAIR)
        far_at = pl.multiple_of((1 - core) * down_cols, PAIR)
        for j in range(part_count):
            low = jnp.bitwise_xor(me & (part_count - 1), j)
            mine, other = sources[j], sources[part_count + j]
            copies += [
                pltpu.make_async_copy(mine.at[:, :, :ff], ffn_w.at[core, :, low], sems.at[4 * j]),
                pltpu.make_async_copy(other.at[:, :, :ff], ffn_w.at[1 - core, :, low], sems.at[4 * j + 1]),
                pltpu.make_async_copy(
                    mine.at[:, :, ff:], ffn_w.at[2, :, low, :, pl.ds(near_at, down_cols)], sems.at[4 * j + 2]
                ),
                pltpu.make_async_copy(
                    other.at[:, :, pl.ds(far_from, offset)],
                    ffn_w.at[2, :, low, :, pl.ds(far_at, offset)],
                    sems.at[4 * j + 3],
                ),
            ]
        return copies

    @pl.when(step == 0)
    def _():
        for copy in loads():
            copy.start()

    here = core * (block * pl.num_programs(0)) + step * block
    position = here + lax.broadcasted_iota(jnp.int32, (block, 1), 0)
    valid = (position < live).astype(f32)
    attn = far[...].astype(f32)
    for one, w in zip(outs_of, weights):
        attn = attn + lax.dot_general(one[...], w[...], NT, preferred_element_type=f32)
    hidden = tokens[...].astype(f32) + valid * attn
    normed, inv = norm_stats(hidden)
    gain = gains[8:9, :]
    a2 = (normed * gain).astype(bf16)

    @pl.when(step == 0)
    def _():
        for copy in loads():
            copy.wait()

    weights_in = ffn_w.reshape(3, width, ff) if part_count > 1 else ffn_w
    up = jnp.dot(a2, weights_in[0], preferred_element_type=f32)
    gate = jnp.dot(a2, weights_in[1], preferred_element_type=f32)
    below = 0.5 * (1.0 + lax.erf(up * math.sqrt(0.5)))
    act = up * below
    slope = below + up * jnp.exp(up * up * -0.5) * (1.0 / math.sqrt(2.0 * math.pi))
    z = (act * gate).astype(bf16)
    result[...] = (
        hidden + valid * lax.dot_general(z, weights_in[2], NT, preferred_element_type=f32)
    ).astype(bf16)
    dy = cot[...].astype(f32)
    dff = (valid * dy).astype(bf16)
    dz = jnp.dot(dff, weights_in[2], preferred_element_type=f32)
    du = (dz * gate * slope).astype(bf16)
    dg = (dz * act).astype(bf16)
    da2 = lax.dot_general(du, weights_in[0], NT, preferred_element_type=f32) + lax.dot_general(
        dg, weights_in[1], NT, preferred_element_type=f32
    )
    grad = dy + norm_back(da2 * gain, normed, inv)
    grad_hidden[...] = grad
    dattn[...] = (valid * grad).astype(bf16)
    z_all[...] = z
    pair_all[0] = du
    pair_all[1] = dg
    a2_all[...] = a2
    dff_all[...] = dff


def weight_grad_kernel(split, own, down_cols, scal, z, pair, a2, dff, *outs):
    width, ff = a2.shape[1], z.shape[1]
    core = scal[2]
    for m in range(width // ROW_BLOCK):
        part = slice(m * ROW_BLOCK, (m + 1) * ROW_BLOCK)
        left, down = a2[:, part], dff[:, part]
        if split:
            who = core if own else 1 - core
            at = pl.multiple_of(who * (ff - down_cols), PAIR)
            outs[0][part, :ff] = lax.dot_general(left, pair[who], TN, preferred_element_type=f32).astype(bf16)
            outs[0][part, ff:] = lax.dot_general(
                down, z[:, pl.ds(at, down_cols)], TN, preferred_element_type=f32
            ).astype(bf16)
        else:
            for i in (0, 1):
                outs[0][i, part, :] = lax.dot_general(
                    left, pair[i], TN, preferred_element_type=f32
                ).astype(bf16)
            outs[1][part, :] = lax.dot_general(down, z[...], TN, preferred_element_type=f32).astype(bf16)


def weight_grads(split, own, down_cols, scal, z, pair, a2, dff, deps=()):
    width, ff = a2.shape[1], z.shape[1]
    shape = jax.ShapeDtypeStruct
    if split:
        outs = (shape((width, ff + down_cols), bf16),)
    else:
        outs = (shape((2, width, ff), bf16), shape((width, ff), bf16))
    return pl.pallas_call(
        passing(functools.partial(weight_grad_kernel, split, own, down_cols), 5, len(deps)),
        out_shape=outs,
        in_specs=[smem()] + [vmem()] * 4 + [anywhere()] * len(deps),
        out_specs=(vmem(),) * len(outs),
        compiler_params=params(10 if split else 32),
        cost_estimate=lasts(5),
        name="weight_grads",
    )(scal, z, pair, a2, dff, *deps)


def feed_forward(scal, outs_of, weights, tokens, far, cot, gains, sources, ff, down_cols):
    length, width = tokens.shape
    part_count = len(sources) // 2
    placed = (3, width, ff)
    if part_count > 1:
        placed = (3, sources[0].shape[0], part_count, sources[0].shape[1], ff)
    half = length // 2
    blocks = half // ROW_BLOCK
    shape = jax.ShapeDtypeStruct
    whole = lambda a: pl.BlockSpec(a.shape, lambda b, s: (0,) * len(a.shape))
    near = lambda a: pl.BlockSpec((ROW_BLOCK, a.shape[1]), lambda b, s: (b + s[2] * blocks, 0))
    plain = lambda cols: pl.BlockSpec((ROW_BLOCK, cols), lambda b, s: (b, 0))
    return pl.pallas_call(
        functools.partial(ffn_kernel, len(outs_of), part_count, down_cols),
        out_shape=(
            shape((half, width), bf16),
            shape((half, width), bf16),
            shape((half, width), f32),
            shape((half, ff), bf16),
            shape((2, half, ff), bf16),
            shape((half, width), bf16),
            shape((half, width), bf16),
        ),
        grid_spec=pltpu.PrefetchScalarGridSpec(
            num_scalar_prefetch=1,
            grid=(blocks,),
            in_specs=[near(o) for o in outs_of]
            + [columns_of(w, at, PAIR) for w, at in weights]
            + [near(tokens), plain(width), plain(width), whole(gains)]
            + [anywhere()] * len(sources),
            out_specs=(
                plain(width),
                plain(width),
                plain(width),
                plain(ff),
                pl.BlockSpec((2, ROW_BLOCK, ff), lambda b, s: (0, b, 0)),
                plain(width),
                plain(width),
            ),
            scratch_shapes=[pltpu.VMEM(placed, bf16), pltpu.SemaphoreType.DMA((16,))],
        ),
        compiler_params=params(FFN_MIB),
        cost_estimate=lasts(25),
        name="feed_forward",
    )(scal, *outs_of, *[w for w, _ in weights], tokens, far, cot, gains, *sources)


def pack_kernel(wide, scal, keep, got, *outs):
    me = scal[1]
    for j in range(wide):
        for h in range(outs[0].shape[0]):
            own = h * wide + jnp.bitwise_xor(me & (wide - 1), j)
            outs[j][h] = (keep[own].astype(f32) + got[own].astype(f32)).astype(bf16)


def pack_parts(scal, keep, got, count, deps=()):
    width, cols = keep.shape
    rows = width // count
    wide = 1 << bit_groups(count)[-1][1]
    shape = jax.ShapeDtypeStruct((count // wide, rows, cols), bf16)
    return pl.pallas_call(
        passing(functools.partial(pack_kernel, wide), 3, len(deps)),
        out_shape=(shape,) * wide,
        in_specs=[smem(), vmem(), vmem()] + [anywhere()] * len(deps),
        out_specs=(vmem(),) * wide,
        compiler_params=params(),
        cost_estimate=lasts(4),
        name="pack_parts",
    )(scal, keep.reshape(count, rows, cols), got.reshape(count, rows, cols), *deps)


def rotary_tables(length):
    freqs = ROPE_THETA ** (-np.arange(0, HEAD_DIM, 2) / HEAD_DIM)
    freqs = np.tile(np.float32(freqs).astype(np.float64), 4)
    sign = np.where(np.arange(PAIR) % HEAD_DIM < HEAD_DIM // 2, -1.0, 1.0)

    def both(positions):
        angles = positions[:, None] * freqs[None, :]
        return jnp.asarray(np.stack([np.cos(angles), np.sin(angles) * sign]), f32)

    return both(np.arange(PREP_BLOCK)), both(np.arange(0, length, PREP_BLOCK))


def local(tokens, segment_ids, counts, w_qkv, w_out, w_in, w_down, ln1_gain, ln2_gain, cotangent):
    count = lax.axis_size("dp")
    dp, core = lax.axis_index("dp"), lax.axis_index("head")
    length, width = tokens.shape[1:]
    ff = w_in.shape[2]
    rows_each = width // count
    fast = rows_each % 16 == 0 and count & (count - 1) == 0 and len(bit_groups(count)) == 2
    pairs = w_qkv.shape[2] // PAIR
    first_core = core == 0
    pick = lambda a, b: jnp.where(first_core, a, b)
    join = lambda mine, other: jnp.concatenate([pick(mine, other), pick(other, mine)], axis=0)
    row, cot = tokens[0], cotangent[0]
    seg = segment_ids[0]
    live = counts[0]
    begins = jnp.sum(seg[None, :] < jnp.arange(1, 4)[:, None], axis=1)
    scal = jnp.concatenate([jnp.stack([live, dp, core]), begins]).astype(jnp.int32)

    both = jnp.stack([ln1_gain, ln2_gain], axis=1)
    head_load, rest_load = attention_loads(core.astype(jnp.int32)[None], w_qkv, w_out.T, both, core_swap(both))
    down_turned = w_down.T
    down_cols = -(-(ff // 2) // 128) * 128
    offset = ff - down_cols
    tables = rotary_tables(length)
    out_at = 3 * PAIR * (pairs - 1)
    everyone = ("dp", "head")

    if fast:
        high_bits, low_bits = bit_groups(count)
        head_high = gather_step(head_load[None], count, high_bits)
        at = (dp >> low_bits[1]).astype(jnp.int32)[None]
        rest_load = stack_parts(at, [rest_load[None]], head_high[1:])
        head_parts = gather_step(stack_parts(at, head_high), count, low_bits)
        rest_high = gather_step(rest_load, count, high_bits)
        rest_all = stack_parts(at, rest_high, head_parts[1:])
        zero_one = jnp.concatenate([w_in[0], down_turned[:, :down_cols]], axis=1)
        one_two = jnp.concatenate([w_in[1], down_turned[:, offset:]], axis=1)
        ffn_load = join(pick(zero_one, one_two), core_swap(pick(one_two, zero_one)))
        ffn_load = stack_parts(at, [ffn_load[None]], rest_high[1:])
        ffn_high = gather_step(ffn_load, count, high_bits)
        a1, gains, *kept = forward_pair(
            True, scal, row, tables, head_parts, 0, [rest_all, ffn_load]
        )
        rest_parts = gather_step(rest_all, count, low_bits)
        ffn_all = stack_parts(at, ffn_high, [a1])
        ffn_parts = gather_step(ffn_all, count, low_bits)
        sources = ffn_parts + [core_swap(p) for p in ffn_parts]
        deps, late_deps = [ffn_all], ffn_parts[1:]
    else:
        head_parts = [lax.all_gather(head_load, "dp", axis=0, tiled=True)]
        rest_parts = [lax.all_gather(rest_load, "dp", axis=0, tiled=True)]
        sources = [
            lax.all_gather(w_in, everyone, axis=1, tiled=True),
            lax.all_gather(down_turned, everyone, axis=0, tiled=True),
        ]
        a1, gains, *kept = forward_pair(True, scal, row, tables, head_parts, 0)
        deps, late_deps = [], []

    head_w, saved = kept[0], [kept[1:]]
    rest_w, *kept = forward_pair(False, scal, a1, tables, rest_parts, 0, deps)
    saved.append(kept)
    for i in range(2, pairs):
        saved.append(forward_pair(False, scal, a1, tables, rest_w, 3 * PAIR * (i - 1)))
    qkv_w = [(head_w, 0)] + [(rest_w, 3 * PAIR * (i - 1)) for i in range(1, pairs)]
    out_w = [(rest_w, out_at + i * PAIR) for i in range(pairs)]
    outs_of = [s[3] for s in saved]

    far = core_swap(project_far_half(scal, outs_of, out_w, late_deps))
    result, near_grad, grad_hidden, *kept = feed_forward(scal, outs_of, out_w, row, far, cot, gains, sources, ff, down_cols)
    far_grad = core_swap(near_grad)

    def backward(i, part_shapes, before=(), deps=()):
        q, k, v, o, lse = saved[i]
        w, at = out_w[i]
        w = w[:, at : at + PAIR]
        return backward_pair(
            scal, a1, near_grad, far_grad, w, (q, k, v, o, lse), tables, part_shapes, before, deps
        )

    if fast:
        wide = 1 << low_bits[1]
        parts_of = lambda n: [(count // wide, rows_each, n * 4 * PAIR)] * wide
        got = core_swap(weight_grads(True, False, down_cols, scal, *kept)[0])
        keep = weight_grads(True, True, down_cols, scal, *kept)[0]
        deps = pack_parts(scal, keep, got, count)
        ffn_near = reduce_near(deps, count)
        dqkv, before = [], []
        pieces = None
        for i in range(pairs - 1):
            last = i == pairs - 2
            one, *parts = backward(
                i, parts_of(pairs - 1) if last else [(width, 4 * PAIR)], before if last else [], deps
            )
            dqkv.append(one)
            before += parts
        pieces = sum_parts(at, ffn_near, [one])
        done = reduce_far(pieces, count, wide)
        early_near = reduce_near(parts, count)
        one, *parts = backward(pairs - 1, parts_of(1), (), pieces)
        dqkv.append(one)
        late_near = reduce_near(parts, count)
        pieces = sum_parts(at, early_near, [one])
        early = far_pieces(pieces, count, wide)
        far_da = project_far_half(scal, dqkv, qkv_w, pieces)
        pieces = sum_parts(at, late_near, pieces)
        shards = [early, far_pieces(pieces, count, wide)]
        far_da = core_swap(far_da)
        grad_tokens, mark = final_rows(scal, dqkv, qkv_w, row, far_da, grad_hidden, gains, pieces)
        rows_here = w_in.shape[1]
        low, high = done[:rows_here], done[rows_here:]
        mine = pick(low, high)
        other = core_swap(pick(high, low))
        grad_w_in = jnp.stack(
            [pick(mine[:, :ff], other[:, :ff]), pick(other[:, :ff], mine[:, :ff])]
        )
        grad_down = jnp.concatenate(
            [pick(mine[:, ff:], other[:, ff:]), pick(other[:, ff:], mine[:, ff:])[:, down_cols - offset :]],
            axis=1,
        ).T
    else:
        keep, send = weight_grads(False, True, down_cols, scal, *kept)
        grad_w_in = lax.psum_scatter(keep.astype(f32), everyone, scatter_dimension=1, tiled=True)
        grad_down = lax.psum_scatter(send.astype(f32), everyone, scatter_dimension=0, tiled=True).T
        dqkv, shards = [], []
        for i in range(pairs):
            one, parts = backward(i, [(width, 4 * PAIR)])
            dqkv.append(one)
            shards.append([lax.psum_scatter(parts.astype(f32), "dp", scatter_dimension=0, tiled=True)])
        far_da = core_swap(project_far_half(scal, dqkv, qkv_w))
        grad_tokens, mark = final_rows(scal, dqkv, qkv_w, row, far_da, grad_hidden, gains)

    grad_two = jnp.sum(grad_w_in * w_in.astype(f32), axis=(0, 2)) / ln2_gain.astype(f32)

    grad_qkv, grad_out, partial = finish(shards, w_qkv, [mark])
    rows_here = ln1_gain.shape[0]
    partial = partial[:, 0]
    low, high = partial[:rows_here], partial[rows_here:]
    grad_one = (pick(low, high) + core_swap(pick(high, low))) / ln1_gain.astype(f32)
    return (
        result[None],
        grad_tokens[None],
        grad_qkv,
        grad_out.T,
        grad_w_in,
        grad_down,
        grad_one,
        grad_two,
    )


def solution(mesh):
    placed = (
        P("dp", None, None),
        P("dp", None),
        P("dp"),
        P(None, "dp", "head"),
        P("head", "dp"),
        P(None, ("dp", "head"), None),
        P(None, ("dp", "head")),
        P(("dp", "head")),
        P(("dp", "head")),
        P("dp", "head", None),
    )
    return jax.shard_map(
        local,
        mesh=mesh,
        in_specs=placed,
        out_specs=(
            P("dp", "head", None),
            P("dp", "head", None),
            P(None, "dp", "head"),
            P("head", "dp"),
            P(None, ("dp", "head"), None),
            P(None, ("dp", "head")),
            P(("dp", "head")),
            P(("dp", "head")),
        ),
        check_vma=False,
    )
```
